32 devices in a mesh: outer: 4 (over x, core), inner: 2 (over y), tensor: 4 (over z).
Axes of the slice: x: 2, y: 2, z: 4, core: 2. Of those that a mesh axis runs over, the one named last changes fastest.
Arguments:
- hidden_in: bfloat16 [1536, 4096], P(('outer', 'inner', 'tensor')), may hold values from -15 to 15
- norm_gain: float32 [4096], replicated, may hold values from 0.5 to 5
- w_query: bfloat16 [4096, 4096], P('inner', 'tensor'), may hold values from -0.110485435 to 0.110485435
- w_key: bfloat16 [4096, 1024], P('inner', 'tensor'), may hold values from -0.110485435 to 0.110485435
- value_weight: bfloat16 [4096, 1024], P('inner', 'tensor'), may hold values from -0.09375 to 0.09375
- w_out: bfloat16 [4096, 4096], P('tensor'), may hold values from -0.09375 to 0.09375
- doc_ids: int32 [1536], P(('outer', 'inner')), may hold values from 0 to 5, as said below
- positions: int32 [1536], P(('outer', 'inner')), may hold values from 0 to 65535, as said below
Outputs:
- layer_out: bfloat16 [1536, 4096], P(('outer', 'inner', 'tensor'))
The draws below stay inside these ranges and needn't reach their ends.
Inputs may be any that keep to these rules, and one draw needn't show every extreme that they name: `doc_ids`: document numbers never fall along the sequence; each of the 6 documents has at least one token, and exactly one of them has 960 tokens. Document numbers may be sent packed or coded. `positions`: inside a document the position rises by one from each token to the next; one document other than the one of 960 tokens ends at position 65535.
All inputs are finite; a program needn't handle non-finite values.
Results may differ from the reference program's by a relative error of at most 0.012.
The reference program's roundings to bfloat16 on the way count: a program that leaves them out, or rounds other values in their place, can miss the bound.
Values may be sent and summed in bfloat16 or wider, within the bound.
No kernel may reach another device: no remote copies, remote signals or barrier semaphores. Data moves between devices by JAX's collectives and lax.ppermute only.
A program may use at most 128 MiB of HBM per device.

```python
import math
import jax
import jax.numpy as jnp
from jax import lax

MODEL_WIDTH = 4096
QUERY_HEADS = 32
KEY_VALUE_HEADS = 8
HEAD_SIZE = 128
NDOC = 6
YARN_CTX = 65536
SEQUENCE_TOKENS = 1536
LONGEST = 960


def draw_hidden_in(key, part):
    values = jnp.clip(jax.random.normal(jax.random.fold_in(key, 3), (SEQUENCE_TOKENS, MODEL_WIDTH), jnp.float32), -5.0, 5.0)
    return values.astype(jnp.bfloat16)


def draw_norm_gain(key, part):
    return jax.random.uniform(jax.random.fold_in(key, 5), (MODEL_WIDTH,), jnp.float32, 0.6, 1.4)


def normed_queries(key):
    return jnp.clip(jax.random.normal(jax.random.fold_in(key, 21), (MODEL_WIDTH, QUERY_HEADS * HEAD_SIZE), jnp.float32), -5.0, 5.0)


def draw_w_query(key, part):
    sigma = (MODEL_WIDTH // 2) ** (-0.5)
    return (sigma * normed_queries(key)).astype(jnp.bfloat16)


def draw_w_key(key, part):
    sigma = (MODEL_WIDTH // 2) ** (-0.5)
    random_noise = jnp.clip(jax.random.normal(jax.random.fold_in(key, 22), (MODEL_WIDTH, KEY_VALUE_HEADS * HEAD_SIZE), jnp.float32), -5.0, 5.0)
    return (sigma * random_noise).astype(jnp.bfloat16)


def document_layout(key):
    doc_key = jax.random.fold_in(key, 11)
    cut_key, slot_key, offset_key, end_key = jax.random.split(doc_key, 4)
    remaining = SEQUENCE_TOKENS - LONGEST
    cut_picks = jax.random.permutation(cut_key, remaining - 1)[:NDOC - 2] + 1
    cut_points = jnp.sort(cut_picks).astype(jnp.int32)
    edge_points = jnp.concatenate([jnp.zeros((1,), jnp.int32), cut_points, jnp.full((1,), remaining, jnp.int32)])
    other_lengths = edge_points[1:] - edge_points[:-1]
    long_slot = jax.random.randint(slot_key, (), 0, NDOC)
    end_pick = jax.random.randint(end_key, (), 0, NDOC - 1)
    end_slot = end_pick + (end_pick >= long_slot).astype(jnp.int32)
    indices = jnp.arange(NDOC, dtype=jnp.int32)
    before = jnp.take(other_lengths, jnp.clip(indices, 0, NDOC - 2))
    later_lengths = jnp.take(other_lengths, jnp.clip(indices - 1, 0, NDOC - 2))
    doc_lengths = jnp.where(indices < long_slot, before, jnp.where(indices == long_slot, LONGEST, later_lengths)).astype(jnp.int32)
    doc_ends = jnp.cumsum(doc_lengths)
    doc_begins = doc_ends - doc_lengths
    token_index = jnp.arange(SEQUENCE_TOKENS, dtype=jnp.int32)
    documents = jnp.sum((token_index[:, None] >= doc_ends[None, :NDOC - 1]).astype(jnp.int32), axis=1)
    raw_offsets = jax.random.randint(offset_key, (NDOC,), 0, 2 ** 30)
    offsets = raw_offsets % (YARN_CTX - doc_lengths + 1)
    offsets = jnp.where(indices == long_slot, raw_offsets % (YARN_CTX - LONGEST), offsets)
    offsets = jnp.where(indices == end_slot, YARN_CTX - doc_lengths, offsets)
    placed = jnp.take(offsets, documents) + token_index - jnp.take(doc_begins, documents)
    return (documents.astype(jnp.int32), placed.astype(jnp.int32))


def draw_doc_ids(key, part):
    return document_layout(key)[0]


def draw_positions(key, part):
    return document_layout(key)[1]


def levels(stream_key, shape, pieces, low, top_value):
    level, own = 1.0, jax.random.fold_in(stream_key, 6)
    for position, parts in pieces:
        heights = jnp.exp(jax.random.uniform(jax.random.fold_in(own, position), (parts,), jnp.float32, low / len(pieces), top_value / len(pieces)))
        level = level * jnp.repeat(heights, shape[position] // parts).reshape([-1 if axis == position else 1 for axis in range(len(shape))])
    return level


def gaussian(key, shape, scale, reach, cuts=(), kind=jnp.bfloat16):
    array = jax.random.normal(key, shape, jnp.float32) * scale
    if len(cuts) > 0:
        array = levels(key, shape, cuts, -0.22, 0.18) * array
    return jnp.clip(array, min=-reach, max=reach).astype(kind)


def setup_inputs(seed: int = 0) -> dict:
    seeds = jax.random.split(jax.random.key(seed), 9)
    hidden_in = draw_hidden_in(jax.random.fold_in(seeds[8], 71), 0)
    norm_gain = draw_norm_gain(jax.random.fold_in(seeds[8], 71), 0)
    w_query = draw_w_query(jax.random.fold_in(seeds[8], 71), 0)
    w_key = draw_w_key(jax.random.fold_in(seeds[8], 71), 0)
    value_weight = gaussian(seeds[4], (MODEL_WIDTH, KEY_VALUE_HEADS * HEAD_SIZE), MODEL_WIDTH ** -0.5, 0.09375, ((0, 2), (1, 4)))
    w_out = gaussian(seeds[5], (QUERY_HEADS * HEAD_SIZE, MODEL_WIDTH), (QUERY_HEADS * HEAD_SIZE) ** -0.5, 0.09375, ((0, 4),))
    doc_ids = draw_doc_ids(jax.random.fold_in(seeds[8], 71), 0)
    positions = draw_positions(jax.random.fold_in(seeds[8], 71), 0)
    return dict(hidden_in=hidden_in, norm_gain=norm_gain, w_query=w_query, w_key=w_key, value_weight=value_weight, w_out=w_out, doc_ids=doc_ids, positions=positions)


rope_base = 500000.0
yarn_factor = 8.0
trained_context = 8192.0
beta_fast = 32.0
beta_slow = 1.0
norm_epsilon = 1e-05
masked_score = -1e+30

def yarn_inverse(head_dim):
    half_dim = head_dim // 2

    def correction(rotations):
        return head_dim * math.log(trained_context / (rotations * 2.0 * math.pi)) / (2.0 * math.log(rope_base))
    lowest = max(math.floor(correction(beta_fast)), 0)
    highest = min(math.ceil(correction(beta_slow)), head_dim - 1)
    spread = max(highest - lowest, 0.001)
    values = []
    for column in range(half_dim):
        extrapolated = rope_base ** (-2.0 * column / head_dim)
        ramp = min(max((column - lowest) / spread, 0.0), 1.0)
        values.append(extrapolated / yarn_factor * ramp + extrapolated * (1.0 - ramp))
    return values

def yarn_tables(positions, head_dim):
    inverse = jnp.asarray(yarn_inverse(head_dim), dtype=jnp.float32)
    attention_gain = 0.1 * math.log(yarn_factor) + 1.0
    angles = positions.astype(jnp.float32)[:, None] * inverse[None, :]
    return (jnp.cos(angles) * attention_gain, jnp.sin(angles) * attention_gain)

def apply_rotation(heads, cosine_table, sine_table):
    half_dim = heads.shape[-1] // 2
    first_half = heads[..., :half_dim]
    second_half = heads[..., half_dim:]
    cos_rows = cosine_table[:, None, :]
    sin_rows = sine_table[:, None, :]
    return jnp.concatenate([first_half * cos_rows - second_half * sin_rows, second_half * cos_rows + first_half * sin_rows], axis=-1)

def rms_normed(hidden_in, norm_gain):
    widened = hidden_in.astype(jnp.float32)
    power = lax.optimization_barrier(jnp.mean(widened * widened, axis=-1, keepdims=True))
    return (widened * lax.rsqrt(power + norm_epsilon) * norm_gain).astype(jnp.bfloat16)

def reference(hidden_in, norm_gain, w_query, w_key, value_weight, w_out, doc_ids, positions):
    normed = rms_normed(hidden_in, norm_gain)
    queries = jnp.dot(normed, w_query, preferred_element_type=jnp.float32)
    key_matrix = jnp.dot(normed, w_key, preferred_element_type=jnp.float32)
    value_matrix = jnp.dot(normed, value_weight, preferred_element_type=jnp.float32).astype(jnp.bfloat16)
    cosine_table, sine_table = yarn_tables(positions, HEAD_SIZE)
    query_rot = apply_rotation(queries.reshape(SEQUENCE_TOKENS, QUERY_HEADS, HEAD_SIZE), cosine_table, sine_table).astype(jnp.bfloat16)
    rotated_keys = apply_rotation(key_matrix.reshape(SEQUENCE_TOKENS, KEY_VALUE_HEADS, HEAD_SIZE), cosine_table, sine_table).astype(jnp.bfloat16)
    value_per_head = value_matrix.reshape(SEQUENCE_TOKENS, KEY_VALUE_HEADS, HEAD_SIZE)
    sequence_index = jnp.arange(SEQUENCE_TOKENS, dtype=jnp.int32)
    allowed = (sequence_index[:, None] >= sequence_index[None, :]) & (doc_ids[:, None] == doc_ids[None, :])
    score_scale = HEAD_SIZE ** (-0.5)
    queries_per_group = QUERY_HEADS // KEY_VALUE_HEADS

    def one_head(head_index):
        shared = head_index // queries_per_group
        head_query = lax.dynamic_index_in_dim(query_rot, head_index, 1, keepdims=False)
        head_key = lax.dynamic_index_in_dim(rotated_keys, shared, 1, keepdims=False)
        head_value = lax.dynamic_index_in_dim(value_per_head, shared, 1, keepdims=False)
        scores = jnp.dot(head_query, head_key.T, preferred_element_type=jnp.float32) * score_scale
        scores = jnp.where(allowed, scores, masked_score)
        row_peaks = lax.optimization_barrier(jnp.max(scores, axis=-1, keepdims=True))
        weights = jnp.where(allowed, jnp.exp(scores - row_peaks), 0.0)
        totals = lax.optimization_barrier(jnp.sum(weights, axis=-1, keepdims=True))
        summed = jnp.dot(weights.astype(jnp.bfloat16), head_value, preferred_element_type=jnp.float32)
        return (summed / totals).astype(jnp.bfloat16)
    attended = lax.map(one_head, jnp.arange(QUERY_HEADS, dtype=jnp.int32))
    attended = jnp.transpose(attended, (1, 0, 2)).reshape(SEQUENCE_TOKENS, QUERY_HEADS * HEAD_SIZE)
    projected = jnp.dot(attended, w_out, preferred_element_type=jnp.float32)
    return (hidden_in.astype(jnp.float32) + projected).astype(jnp.bfloat16)
```

```python
import math

import jax
import jax.numpy as jnp
from jax import lax
from jax.experimental import pallas as pl
from jax.experimental.pallas import tpu as pltpu
from jax.sharding import PartitionSpec as P

HEAD_SIZE = 128


rope_base = 500000.0
yarn_factor = 8.0
trained_context = 8192.0
beta_fast = 32.0
beta_slow = 1.0
norm_epsilon = 1e-05
masked_score = -1e30


def yarn_inverse(head_dim):
    half_dim = head_dim // 2

    def correction(rotations):
        return (
            head_dim
            * math.log(trained_context / (rotations * 2.0 * math.pi))
            / (2.0 * math.log(rope_base))
        )

    lowest = max(math.floor(correction(beta_fast)), 0)
    highest = min(math.ceil(correction(beta_slow)), head_dim - 1)
    spread = max(highest - lowest, 0.001)
    values = []
    for column in range(half_dim):
        extrapolated = rope_base ** (-2.0 * column / head_dim)
        ramp = min(max((column - lowest) / spread, 0.0), 1.0)
        values.append(extrapolated / yarn_factor * ramp + extrapolated * (1.0 - ramp))
    return values


def yarn_tables(positions, head_dim):
    inverse = jnp.asarray(yarn_inverse(head_dim), dtype=jnp.float32)
    attention_gain = 0.1 * math.log(yarn_factor) + 1.0
    angles = positions.astype(jnp.float32)[:, None] * inverse[None, :]
    return (jnp.cos(angles) * attention_gain, jnp.sin(angles) * attention_gain)


def apply_rotation(heads, cosine_table, sine_table):
    half_dim = heads.shape[-1] // 2
    first_half = heads[..., :half_dim]
    second_half = heads[..., half_dim:]
    cos_rows = cosine_table[:, None, :]
    sin_rows = sine_table[:, None, :]
    return jnp.concatenate(
        [
            first_half * cos_rows - second_half * sin_rows,
            second_half * cos_rows + first_half * sin_rows,
        ],
        axis=-1,
    )


def rms_normed(hidden_in, norm_gain):
    widened = hidden_in.astype(jnp.float32)
    power = jnp.mean(widened * widened, axis=-1, keepdims=True)
    return (widened * lax.rsqrt(power + norm_epsilon) * norm_gain).astype(jnp.bfloat16)


def body(hidden_in, norm_gain, w_query, w_key, value_weight, w_out, doc_ids, positions):
    normed = rms_normed(hidden_in, norm_gain)
    block_rows = lax.all_gather(normed, "tensor", axis=0, tiled=True)
    tokens_here = block_rows.shape[0]
    query_width = w_query.shape[1]
    key_width = w_key.shape[1]
    inner_count = lax.axis_size("inner")
    slice_width = w_query.shape[0]
    arranged = block_rows.reshape(tokens_here, inner_count, slice_width)
    received = lax.all_to_all(arranged, "inner", split_axis=1, concat_axis=0, tiled=True)
    received = received.reshape(inner_count * tokens_here, slice_width)
    stacked = jnp.concatenate([w_query, w_key, value_weight], axis=1)
    combined = lax.psum_scatter(
        jnp.dot(received, stacked, preferred_element_type=jnp.float32),
        "inner",
        scatter_dimension=0,
        tiled=True,
    )
    queries = combined[:, :query_width]
    key_matrix = combined[:, query_width : query_width + key_width]
    value_matrix = combined[:, query_width + key_width :]
    value_matrix = value_matrix.astype(jnp.bfloat16)
    heads_query = query_width // HEAD_SIZE
    heads_key = key_width // HEAD_SIZE
    queries_per_group = heads_query // heads_key
    cosine_table, sine_table = yarn_tables(positions, HEAD_SIZE)
    query_rot = (
        apply_rotation(
            queries.reshape(tokens_here, heads_query, HEAD_SIZE), cosine_table, sine_table
        )
        .astype(jnp.bfloat16)
        .reshape(tokens_here, query_width)
    )
    rotated_keys = (
        apply_rotation(
            key_matrix.reshape(tokens_here, heads_key, HEAD_SIZE), cosine_table, sine_table
        )
        .astype(jnp.bfloat16)
        .reshape(tokens_here, key_width)
    )
    documents = lax.all_gather(doc_ids, ("outer", "inner"), axis=0, tiled=True)
    length_all = documents.shape[0]
    block_index = lax.axis_index(("outer", "inner"))
    sequence_index = jnp.arange(length_all, dtype=jnp.int32)
    query_documents = lax.dynamic_slice_in_dim(documents, block_index * tokens_here, tokens_here, 0)
    query_index = lax.dynamic_slice_in_dim(
        sequence_index, block_index * tokens_here, tokens_here, 0
    )
    row_documents = jnp.tile(query_documents, queries_per_group)
    row_index = jnp.tile(query_index, queries_per_group)
    top_index = jnp.max(query_index)
    top_document = jnp.max(query_documents)
    low_document = jnp.min(query_documents)
    grouped_heads = jnp.transpose(
        query_rot.reshape(tokens_here, heads_key, queries_per_group, HEAD_SIZE), (1, 2, 0, 3)
    ).reshape(heads_key, queries_per_group * tokens_here, HEAD_SIZE)
    score_scale = HEAD_SIZE ** (-0.5)

    def key_block(running, block_keys, block_values, first_row):
        row_count = block_keys.shape[0]
        piece_index = lax.dynamic_slice_in_dim(sequence_index, first_row, row_count, 0)
        piece_documents = lax.dynamic_slice_in_dim(documents, first_row, row_count, 0)
        live = (
            (jnp.min(piece_index) <= top_index)
            & (jnp.min(piece_documents) <= top_document)
            & (jnp.max(piece_documents) >= low_document)
        )

        def attend(current):
            row_peaks, totals, summed = current
            heads_keys = block_keys.reshape(row_count, heads_key, HEAD_SIZE)
            heads_values = block_values.reshape(row_count, heads_key, HEAD_SIZE)
            scores = (
                jnp.einsum(
                    "hqd,khd->hqk", grouped_heads, heads_keys, preferred_element_type=jnp.float32
                )
                * score_scale
            )
            allowed = (row_index[:, None] >= piece_index[None, :]) & (
                row_documents[:, None] == piece_documents[None, :]
            )
            scores = jnp.where(allowed[None], scores, masked_score)
            fresh = jnp.maximum(row_peaks, jnp.max(scores, axis=-1))
            weights = jnp.where(allowed[None], jnp.exp(scores - fresh[..., None]), 0.0)
            shrink = jnp.exp(row_peaks - fresh)
            totals = totals * shrink + jnp.sum(weights, axis=-1)
            summed = summed * shrink[..., None] + jnp.einsum(
                "hqk,khd->hqd",
                weights.astype(jnp.bfloat16),
                heads_values,
                preferred_element_type=jnp.float32,
            )
            return (fresh, totals, summed)

        return lax.cond(live, attend, lambda current: current, running)

    initial = (
        jnp.full((heads_key, queries_per_group * tokens_here), masked_score, jnp.float32),
        jnp.zeros((heads_key, queries_per_group * tokens_here), jnp.float32),
        jnp.zeros((heads_key, queries_per_group * tokens_here, HEAD_SIZE), jnp.float32),
    )
    piece_keys = lax.all_gather(rotated_keys, ("outer", "inner"), axis=0, tiled=True)
    piece_values = lax.all_gather(value_matrix, ("outer", "inner"), axis=0, tiled=True)
    row_count = piece_keys.shape[0]
    step_rows = 512
    steps_count = row_count // step_rows
    split_keys = piece_keys.reshape(steps_count, step_rows, key_width)
    split_values = piece_values.reshape(steps_count, step_rows, key_width)
    offsets = jnp.arange(steps_count, dtype=jnp.int32) * step_rows

    def scan_step(current, inputs):
        block_keys, block_values, offset = inputs
        return (key_block(current, block_keys, block_values, offset), None)

    result, unused = lax.scan(scan_step, initial, (split_keys, split_values, offsets))
    row_peaks, totals, summed = result
    heads_out = (summed / totals[..., None]).astype(jnp.bfloat16)
    attended = jnp.transpose(
        heads_out.reshape(heads_key, queries_per_group, tokens_here, HEAD_SIZE), (2, 0, 1, 3)
    ).reshape(tokens_here, query_width)
    full_term = jnp.dot(attended, w_out, preferred_element_type=jnp.float32)
    projected = lax.psum_scatter(
        full_term.astype(jnp.bfloat16), "tensor", scatter_dimension=0, tiled=True
    ).astype(jnp.float32)
    return (hidden_in.astype(jnp.float32) + projected).astype(jnp.bfloat16)


def swap_pairs(axis_size, flip):
    return [(place, place ^ flip) for place in range(axis_size)]


def by_xor(parts, index):
    count = len(parts)
    bit = 1
    while bit < count:
        parts = [jnp.where((index & bit) != 0, parts[k ^ bit], parts[k]) for k in range(count)]
        bit *= 2
    return parts


def attention_kernel(
    live, query_kept, query_came, cosines, sines, query_index, query_start, key_index, pairs,
    out, peaks, totals, summed,
):
    tokens = query_kept.shape[0]
    heads = query_kept.shape[1] // HEAD_SIZE
    score_scale = HEAD_SIZE ** (-0.5)
    step = pl.program_id(0)
    whole = query_kept[...] + query_came[...]
    cosine_rows = cosines[...]
    sine_rows = sines[...]
    rotated = []
    for head in range(heads):
        part = whole[:, head * HEAD_SIZE : (head + 1) * HEAD_SIZE]
        turned = pltpu.roll(part, HEAD_SIZE // 2, 1)
        rotated.append((part * cosine_rows + turned * sine_rows).astype(jnp.bfloat16))
    stacked = jnp.concatenate(rotated, axis=0)
    row_index = query_index[...]
    row_start = query_start[...]

    def block_scores(block):
        keys = pairs[block, :, :HEAD_SIZE]
        scores = lax.dot_general(
            stacked, keys, (((1,), (1,)), ((), ())), preferred_element_type=jnp.float32
        )
        places = key_index[block]
        allowed = (places <= row_index) & (places >= row_start)
        scores = scores.reshape(heads, tokens, -1) * score_scale
        return jnp.where(allowed[None], scores, masked_score).reshape(heads * tokens, -1)

    def weighted(block, weights):
        return jnp.dot(
            weights.astype(jnp.bfloat16), pairs[block, :, HEAD_SIZE:],
            preferred_element_type=jnp.float32,
        )

    scores = block_scores(0)
    peak = jnp.max(scores, axis=-1, keepdims=True)
    weights = jnp.exp(scores - peak)
    peaks[...] = peak
    totals[...] = jnp.sum(weights, axis=-1, keepdims=True)
    summed[...] = weighted(0, weights)
    for block in range(1, pairs.shape[0]):

        @pl.when(live[step, block] != 0)
        def _():
            scores = block_scores(block)
            before = peaks[...]
            peak = jnp.maximum(before, jnp.max(scores, axis=-1, keepdims=True))
            weights = jnp.exp(scores - peak)
            shrink = jnp.exp(before - peak)
            peaks[...] = peak
            totals[...] = totals[...] * shrink + jnp.sum(weights, axis=-1, keepdims=True)
            summed[...] = summed[...] * shrink + weighted(block, weights)

    result = (summed[...] / totals[...]).astype(jnp.bfloat16)
    for head in range(heads):
        out[:, head * HEAD_SIZE : (head + 1) * HEAD_SIZE] = result[head * tokens : (head + 1) * tokens]


def attend_rows(
    tokens, live, query_kept, query_came, cosines, sines, query_index, query_start, key_index, pairs
):
    rows, width = query_kept.shape
    heads = width // HEAD_SIZE
    row_block = lambda wide: pl.BlockSpec((tokens, wide), lambda step, live: (step, 0))
    whole_block = lambda array: pl.BlockSpec(array.shape, lambda step, live: (0, 0, 0))
    keys_count = pairs.shape[0] * pairs.shape[1]
    return pl.pallas_call(
        attention_kernel,
        grid_spec=pltpu.PrefetchScalarGridSpec(
            num_scalar_prefetch=1,
            grid=(rows // tokens,),
            in_specs=[
                row_block(width), row_block(width), row_block(HEAD_SIZE), row_block(HEAD_SIZE),
                row_block(1), row_block(1), whole_block(key_index), whole_block(pairs),
            ],
            out_specs=row_block(width),
            scratch_shapes=[
                pltpu.VMEM((heads * tokens, 1), jnp.float32),
                pltpu.VMEM((heads * tokens, 1), jnp.float32),
                pltpu.VMEM((heads * tokens, HEAD_SIZE), jnp.float32),
            ],
        ),
        out_shape=jax.ShapeDtypeStruct((rows, width), jnp.bfloat16),
        compiler_params=pltpu.CompilerParams(vmem_limit_bytes=24 * 1024 * 1024),
        cost_estimate=pl.CostEstimate(
            flops=4 * rows * heads * keys_count * HEAD_SIZE,
            bytes_accessed=2 * keys_count * 2 * HEAD_SIZE + 10 * rows * width,
            transcendentals=rows * heads * keys_count,
        ),
    )(live, query_kept, query_came, cosines, sines, query_index, query_start, key_index, pairs)


def short_body(hidden_in, norm_gain, w_query, w_key, value_weight, w_out, doc_ids, positions):
    place_outer = lax.axis_index("outer")
    place_inner = lax.axis_index("inner")
    place_tensor = lax.axis_index("tensor")
    outer_count = lax.axis_size("outer")
    rows = hidden_in.shape[0]
    half_width = w_query.shape[0]
    query_half = w_query.shape[1] // 2
    key_half = w_key.shape[1] // 2
    block_rows = doc_ids.shape[0]
    across_inner = swap_pairs(2, 1)

    def send(value, axis, pairs):
        return lax.ppermute(value, axis, pairs)

    normed = rms_normed(hidden_in, norm_gain)
    first, second = normed[:, :half_width], normed[:, half_width:]
    lower = place_inner == 0
    mine = jnp.where(lower, first, second)
    others = jnp.where(lower, second, first)
    theirs = send(others, "inner", across_inner)

    def gather_rows(chunk):
        two = send(chunk, "tensor", swap_pairs(4, 2))
        one = send(chunk, "tensor", swap_pairs(4, 1))
        middle = send(chunk, "tensor", [(1, 2), (2, 1)])
        ends = send(two, "tensor", [(1, 0), (2, 3)])
        return [chunk, one, two, middle + ends]

    slots = list(zip(gather_rows(mine), gather_rows(theirs)))

    facts = jnp.stack([doc_ids, positions])
    facts = jnp.stack([facts, send(facts, "inner", across_inner)])
    documents = facts[:, 0]
    bit = 1
    all_documents = documents.reshape(-1)
    while bit < outer_count:
        came = send(all_documents, "outer", swap_pairs(outer_count, bit))
        all_documents = jnp.concatenate([all_documents, came])
        bit *= 2

    def relative(parts):
        pieces = [parts[:, k * rows : (k + 1) * rows] for k in range(4)]
        return jnp.stack(by_xor(pieces, place_tensor)).reshape(-1)

    row_documents = relative(documents)
    row_positions = relative(facts[:, 1])
    starts = jnp.sum((all_documents[None, :] < row_documents[:, None]).astype(jnp.int32), axis=1)
    slot_number = jnp.arange(4, dtype=jnp.int32)[:, None, None]
    part_number = jnp.arange(2, dtype=jnp.int32)[None, :, None]
    row_number = jnp.arange(rows, dtype=jnp.int32)[None, None, :]
    inside = (
        (place_inner ^ part_number) * block_rows + (place_tensor ^ slot_number) * rows + row_number
    ).reshape(-1)
    outer_rows = 2 * block_rows
    blocks = place_outer ^ jnp.arange(outer_count, dtype=jnp.int32)
    row_index = place_outer * outer_rows + inside
    key_index = (blocks[:, None] * outer_rows + inside[None, :])[:, None, :]
    slot_rows = 2 * rows
    earliest = jnp.min(starts.reshape(4, slot_rows), axis=1)
    live = (
        (blocks[None, :] <= place_outer) & ((blocks[None, :] + 1) * outer_rows > earliest[:, None])
    ).astype(jnp.int32)
    inverse = jnp.asarray(yarn_inverse(HEAD_SIZE) * 2, dtype=jnp.float32)
    signs = jnp.asarray([-1.0] * (HEAD_SIZE // 2) + [1.0] * (HEAD_SIZE // 2), dtype=jnp.float32)
    attention_gain = 0.1 * math.log(yarn_factor) + 1.0
    angles = row_positions.astype(jnp.float32)[:, None] * inverse[None, :]
    cosines = jnp.cos(angles) * attention_gain
    sines = jnp.sin(angles) * attention_gain * signs

    def columns(weight, width, which):
        return lax.dynamic_slice_in_dim(weight, which * width, width, 1)

    def split_weights(which):
        pair = [columns(w_key, key_half, which), columns(value_weight, key_half, which)]
        return jnp.concatenate(pair, axis=1), columns(w_query, query_half, which)

    pair_kept, query_kept_weight = split_weights(place_inner)
    pair_sent, query_sent_weight = split_weights(1 - place_inner)

    def product(left, right):
        return jnp.dot(left, right, preferred_element_type=jnp.float32)

    def project(group):
        straight = jnp.concatenate([chunk for slot in group for chunk in slot])
        flipped = jnp.concatenate([chunk for slot in group for chunk in slot[::-1]])
        pair_came = send(product(flipped, pair_sent), "inner", across_inner)
        query_came = send(product(flipped, query_sent_weight), "inner", across_inner)
        pair = product(straight, pair_kept) + pair_came
        return pair, product(straight, query_kept_weight), query_came

    def rotate_keys(pair, first_row):
        count = pair.shape[0]
        keys, values = pair[:, :HEAD_SIZE], pair[:, HEAD_SIZE:]
        half = HEAD_SIZE // 2
        turned = jnp.concatenate([keys[:, half:], keys[:, :half]], axis=1)
        cosine_rows = cosines[first_row : first_row + count]
        sine_rows = sines[first_row : first_row + count]
        keys = keys * cosine_rows + turned * sine_rows
        return jnp.concatenate([keys, values], axis=1).astype(jnp.bfloat16)

    def gather_pairs(pair):
        found = [pair]
        for flip in range(1, outer_count):
            found.append(send(pair, "outer", swap_pairs(outer_count, flip)))
        return jnp.stack(found)

    pair_01, query_kept_01, query_came_01 = project(slots[:2])
    pair_2, query_kept_2, query_came_2 = project(slots[2:3])
    pair_3, query_kept_3, query_came_3 = project(slots[3:])
    early = gather_pairs(rotate_keys(jnp.concatenate([pair_01, pair_2]), 0))
    late = gather_pairs(rotate_keys(pair_3, 3 * slot_rows))
    pairs = jnp.concatenate([early, late], axis=1)

    def attend(slot, count, query_kept, query_came):
        rows_of = lambda array: array[slot * slot_rows : (slot + count) * slot_rows]
        return attend_rows(
            slot_rows, live[slot : slot + count], query_kept, query_came,
            rows_of(cosines), rows_of(sines),
            rows_of(row_index)[:, None], rows_of(starts)[:, None], key_index, pairs,
        )

    def projected(attended):
        count = attended.shape[0] // slot_rows
        parts = attended.reshape(count, 2, rows, attended.shape[1])
        here = parts[:, 0].reshape(count * rows, -1)
        came = send(parts[:, 1].reshape(count * rows, -1), "inner", across_inner)
        joined = jnp.concatenate(
            [jnp.where(lower, here, came), jnp.where(lower, came, here)], axis=1
        )
        return product(joined, w_out)

    term_3 = projected(attend(3, 1, query_kept_3, query_came_3)).astype(jnp.bfloat16)
    inward = send(term_3, "tensor", [(0, 1), (3, 2)])
    middle = send(term_3, "tensor", [(1, 2), (2, 1)])
    term_2 = projected(attend(2, 1, query_kept_2, query_came_2)) + inward.astype(jnp.float32)
    came_2 = send(term_2.astype(jnp.bfloat16), "tensor", swap_pairs(4, 2))
    terms = projected(attend(0, 2, query_kept_01, query_came_01))
    came_1 = send(terms[rows:].astype(jnp.bfloat16), "tensor", swap_pairs(4, 1))
    total = terms[:rows] + came_1.astype(jnp.float32)
    total = total + middle.astype(jnp.float32) + came_2.astype(jnp.float32)
    return (hidden_in.astype(jnp.float32) + total).astype(jnp.bfloat16)


def solution(mesh):
    in_specs = (
        P(("outer", "inner", "tensor"), None),
        P(),
        P("inner", "tensor"),
        P("inner", "tensor"),
        P("inner", "tensor"),
        P("tensor", None),
        P(("outer", "inner")),
        P(("outer", "inner")),
    )
    out_specs = P(("outer", "inner", "tensor"), None)

    def chosen(*arrays):
        outer_count = mesh.shape["outer"]
        key_heads = arrays[3].shape[1] // HEAD_SIZE // mesh.shape["tensor"]
        short = (
            mesh.shape["tensor"] == 4
            and mesh.shape["inner"] == 2
            and key_heads == 2
            and outer_count & (outer_count - 1) == 0
            and arrays[0].shape[0] % (mesh.size * 16) == 0
            and arrays[0].shape[0] // outer_count <= 512
        )
        mapped = jax.shard_map(
            short_body if short else body,
            mesh=mesh, in_specs=in_specs, out_specs=out_specs, check_vma=False,
        )
        return mapped(*arrays)

    return chosen
```

```python
import functools
import math

import jax
import jax.numpy as jnp
from jax import lax
from jax.experimental import pallas as pl
from jax.experimental.pallas import tpu as pltpu
from jax.sharding import PartitionSpec as P

HEAD_SIZE = 128


rope_base = 500000.0
yarn_factor = 8.0
trained_context = 8192.0
beta_fast = 32.0
beta_slow = 1.0
norm_epsilon = 1e-05
masked_score = -1e30
sum_type = jnp.bfloat16


def yarn_inverse(head_dim):
    half_dim = head_dim // 2

    def correction(rotations):
        return (
            head_dim
            * math.log(trained_context / (rotations * 2.0 * math.pi))
            / (2.0 * math.log(rope_base))
        )

    lowest = max(math.floor(correction(beta_fast)), 0)
    highest = min(math.ceil(correction(beta_slow)), head_dim - 1)
    spread = max(highest - lowest, 0.001)
    values = []
    for column in range(half_dim):
        extrapolated = rope_base ** (-2.0 * column / head_dim)
        ramp = min(max((column - lowest) / spread, 0.0), 1.0)
        values.append(extrapolated / yarn_factor * ramp + extrapolated * (1.0 - ramp))
    return values


def yarn_tables(positions, head_dim):
    inverse = jnp.asarray(yarn_inverse(head_dim), dtype=jnp.float32)
    attention_gain = 0.1 * math.log(yarn_factor) + 1.0
    angles = positions.astype(jnp.float32)[:, None] * inverse[None, :]
    return (jnp.cos(angles) * attention_gain, jnp.sin(angles) * attention_gain)


def apply_rotation(heads, cosine_table, sine_table):
    half_dim = heads.shape[-1] // 2
    first_half = heads[..., :half_dim]
    second_half = heads[..., half_dim:]
    cos_rows = cosine_table[:, None, :]
    sin_rows = sine_table[:, None, :]
    return jnp.concatenate(
        [
            first_half * cos_rows - second_half * sin_rows,
            second_half * cos_rows + first_half * sin_rows,
        ],
        axis=-1,
    )


def rms_normed(hidden_in, norm_gain):
    widened = hidden_in.astype(jnp.float32)
    power = jnp.mean(widened * widened, axis=-1, keepdims=True)
    return (widened * lax.rsqrt(power + norm_epsilon) * norm_gain).astype(jnp.bfloat16)


def body(hidden_in, norm_gain, w_query, w_key, value_weight, w_out, doc_ids, positions):
    normed = rms_normed(hidden_in, norm_gain)
    block_rows = lax.all_gather(normed, "tensor", axis=0, tiled=True)
    tokens_here = block_rows.shape[0]
    query_width = w_query.shape[1]
    key_width = w_key.shape[1]
    inner_count = lax.axis_size("inner")
    slice_width = w_query.shape[0]
    arranged = block_rows.reshape(tokens_here, inner_count, slice_width)
    received = lax.all_to_all(arranged, "inner", split_axis=1, concat_axis=0, tiled=True)
    received = received.reshape(inner_count * tokens_here, slice_width)
    stacked = jnp.concatenate([w_query, w_key, value_weight], axis=1)
    combined = lax.psum_scatter(
        jnp.dot(received, stacked, preferred_element_type=jnp.float32),
        "inner",
        scatter_dimension=0,
        tiled=True,
    )
    queries = combined[:, :query_width]
    key_matrix = combined[:, query_width : query_width + key_width]
    value_matrix = combined[:, query_width + key_width :]
    value_matrix = value_matrix.astype(jnp.bfloat16)
    heads_query = query_width // HEAD_SIZE
    heads_key = key_width // HEAD_SIZE
    queries_per_group = heads_query // heads_key
    cosine_table, sine_table = yarn_tables(positions, HEAD_SIZE)
    query_rot = (
        apply_rotation(
            queries.reshape(tokens_here, heads_query, HEAD_SIZE), cosine_table, sine_table
        )
        .astype(jnp.bfloat16)
        .reshape(tokens_here, query_width)
    )
    rotated_keys = (
        apply_rotation(
            key_matrix.reshape(tokens_here, heads_key, HEAD_SIZE), cosine_table, sine_table
        )
        .astype(jnp.bfloat16)
        .reshape(tokens_here, key_width)
    )
    documents = lax.all_gather(doc_ids, ("outer", "inner"), axis=0, tiled=True)
    length_all = documents.shape[0]
    block_index = lax.axis_index(("outer", "inner"))
    sequence_index = jnp.arange(length_all, dtype=jnp.int32)
    query_documents = lax.dynamic_slice_in_dim(documents, block_index * tokens_here, tokens_here, 0)
    query_index = lax.dynamic_slice_in_dim(
        sequence_index, block_index * tokens_here, tokens_here, 0
    )
    row_documents = jnp.tile(query_documents, queries_per_group)
    row_index = jnp.tile(query_index, queries_per_group)
    top_index = jnp.max(query_index)
    top_document = jnp.max(query_documents)
    low_document = jnp.min(query_documents)
    grouped_heads = jnp.transpose(
        query_rot.reshape(tokens_here, heads_key, queries_per_group, HEAD_SIZE), (1, 2, 0, 3)
    ).reshape(heads_key, queries_per_group * tokens_here, HEAD_SIZE)
    score_scale = HEAD_SIZE ** (-0.5)

    def key_block(running, block_keys, block_values, first_row):
        row_count = block_keys.shape[0]
        piece_index = lax.dynamic_slice_in_dim(sequence_index, first_row, row_count, 0)
        piece_documents = lax.dynamic_slice_in_dim(documents, first_row, row_count, 0)
        live = (
            (jnp.min(piece_index) <= top_index)
            & (jnp.min(piece_documents) <= top_document)
            & (jnp.max(piece_documents) >= low_document)
        )

        def attend(current):
            row_peaks, totals, summed = current
            heads_keys = block_keys.reshape(row_count, heads_key, HEAD_SIZE)
            heads_values = block_values.reshape(row_count, heads_key, HEAD_SIZE)
            scores = (
                jnp.einsum(
                    "hqd,khd->hqk", grouped_heads, heads_keys, preferred_element_type=jnp.float32
                )
                * score_scale
            )
            allowed = (row_index[:, None] >= piece_index[None, :]) & (
                row_documents[:, None] == piece_documents[None, :]
            )
            scores = jnp.where(allowed[None], scores, masked_score)
            fresh = jnp.maximum(row_peaks, jnp.max(scores, axis=-1))
            weights = jnp.where(allowed[None], jnp.exp(scores - fresh[..., None]), 0.0)
            shrink = jnp.exp(row_peaks - fresh)
            totals = totals * shrink + jnp.sum(weights, axis=-1)
            summed = summed * shrink[..., None] + jnp.einsum(
                "hqk,khd->hqd",
                weights.astype(jnp.bfloat16),
                heads_values,
                preferred_element_type=jnp.float32,
            )
            return (fresh, totals, summed)

        return lax.cond(live, attend, lambda current: current, running)

    initial = (
        jnp.full((heads_key, queries_per_group * tokens_here), masked_score, jnp.float32),
        jnp.zeros((heads_key, queries_per_group * tokens_here), jnp.float32),
        jnp.zeros((heads_key, queries_per_group * tokens_here, HEAD_SIZE), jnp.float32),
    )
    piece_keys = lax.all_gather(rotated_keys, ("outer", "inner"), axis=0, tiled=True)
    piece_values = lax.all_gather(value_matrix, ("outer", "inner"), axis=0, tiled=True)
    row_count = piece_keys.shape[0]
    step_rows = 512
    steps_count = row_count // step_rows
    split_keys = piece_keys.reshape(steps_count, step_rows, key_width)
    split_values = piece_values.reshape(steps_count, step_rows, key_width)
    offsets = jnp.arange(steps_count, dtype=jnp.int32) * step_rows

    def scan_step(current, inputs):
        block_keys, block_values, offset = inputs
        return (key_block(current, block_keys, block_values, offset), None)

    result, unused = lax.scan(scan_step, initial, (split_keys, split_values, offsets))
    row_peaks, totals, summed = result
    heads_out = (summed / totals[..., None]).astype(jnp.bfloat16)
    attended = jnp.transpose(
        heads_out.reshape(heads_key, queries_per_group, tokens_here, HEAD_SIZE), (2, 0, 1, 3)
    ).reshape(tokens_here, query_width)
    full_term = jnp.dot(attended, w_out, preferred_element_type=jnp.float32)
    projected = lax.psum_scatter(
        full_term.astype(jnp.bfloat16), "tensor", scatter_dimension=0, tiled=True
    ).astype(jnp.float32)
    return (hidden_in.astype(jnp.float32) + projected).astype(jnp.bfloat16)


def swap_pairs(axis_size, flip):
    return [(place, place ^ flip) for place in range(axis_size)]


def by_xor(parts, index):
    count = len(parts)
    bit = 1
    while bit < count:
        parts = [jnp.where((index & bit) != 0, parts[k ^ bit], parts[k]) for k in range(count)]
        bit *= 2
    return parts


def after(value, *others):
    return lax.optimization_barrier((value,) + others)[0]


def whole_spec(array):
    zeros = (0,) * array.ndim
    return pl.BlockSpec(array.shape, lambda step, which: zeros)


def call_kernel(kernel, name, which, arrays, specs, outs, steps=1, scratch=(), mebibytes=16):
    shapes = [jax.ShapeDtypeStruct(shape, dtype) for shape, dtype, unused in outs]
    out_specs = [
        whole_spec(shape) if spec is None else spec for shape, (a, b, spec) in zip(shapes, outs)
    ]
    found = pl.pallas_call(
        kernel,
        name=name,
        grid_spec=pltpu.PrefetchScalarGridSpec(
            num_scalar_prefetch=1,
            grid=(steps,),
            in_specs=[
                whole_spec(array) if spec is None else spec for array, spec in zip(arrays, specs)
            ],
            out_specs=out_specs,
            scratch_shapes=list(scratch),
        ),
        out_shape=shapes,
        compiler_params=pltpu.CompilerParams(vmem_limit_bytes=mebibytes * 1024 * 1024),
    )(which, *arrays)
    return found


def norm_kernel(which, hidden, gain, mine, others):
    half_width = mine.shape[1]
    widened = hidden[...].astype(jnp.float32)
    power = jnp.mean(widened * widened, axis=-1, keepdims=True)
    normed = (widened * lax.rsqrt(power + norm_epsilon) * gain[...]).astype(jnp.bfloat16)

    @pl.when(which[0] == 0)
    def _():
        mine[...] = normed[:, :half_width]
        others[...] = normed[:, half_width:]

    @pl.when(which[0] != 0)
    def _():
        mine[...] = normed[:, half_width:]
        others[...] = normed[:, :half_width]


def stacked_rows(chunks):
    return jnp.concatenate(
        [
            chunk[...] if len(pair) == 1 else pair[0][...] + pair[1][...]
            for pair in chunks
            for chunk in pair[:1]
        ],
        axis=0,
    )


def split_chunks(refs, widths):
    chunks = []
    place = 0
    for width in widths:
        chunks.append(refs[place : place + width])
        place += width
    return chunks, refs[place:]


def product(left, right):
    return jnp.dot(left, right, preferred_element_type=jnp.float32)


def stack_kernel(widths, which, *refs):
    chunks, (out,) = split_chunks(refs, widths)
    out[...] = stacked_rows(chunks)


def other_part(value, rows):
    pieces = [value[place : place + rows] for place in range(0, value.shape[0], rows)]
    return jnp.concatenate([pieces[k ^ 1] for k in range(len(pieces))], axis=0)


def rotated(part, cosine_rows, sine_rows):
    return part * cosine_rows + pltpu.roll(part, HEAD_SIZE // 2, 1) * sine_rows


def pair_kernel(rows, which, keys, values, came, cosines, sines, *refs):
    out = refs[-1]
    count = keys.shape[0]
    added = other_part(came[...], rows).astype(jnp.float32)
    whole = rotated(keys[...] + added[:, :HEAD_SIZE], cosines[...], sines[...])
    out[:count, :HEAD_SIZE] = whole.astype(jnp.bfloat16)
    out[:count, HEAD_SIZE:] = (values[...] + added[:, HEAD_SIZE:]).astype(jnp.bfloat16)
    if len(refs) == 2:
        out[count:, :] = refs[0][...]


def attention_kernel(
    slot, blocks, rows, which, kept, came, cosines, sines, query_document, key_document, *refs
):
    early, late, (out, peaks, totals, summed) = refs[:blocks], refs[blocks : 2 * blocks], refs[2 * blocks :]
    tokens, width = came.shape
    heads = width // HEAD_SIZE
    score_scale = HEAD_SIZE ** (-0.5)
    early_rows = key_document.shape[2] - late[0].shape[0]
    block_rows = 4 * rows
    whole = kept[...] + other_part(came[...], rows).astype(jnp.float32)
    stacked = jnp.concatenate(
        [
            rotated(whole[:, place : place + HEAD_SIZE], cosines[...], sines[...]).astype(
                jnp.bfloat16
            )
            for place in range(0, width, HEAD_SIZE)
        ],
        axis=0,
    )
    place_outer, place_inner, place_tensor = which[0], which[1], which[2]
    document = query_document[...]

    def inside(slot_number, part_number, row_number):
        return (place_inner ^ part_number) * block_rows + (place_tensor ^ slot_number) * rows + row_number

    line = lax.broadcasted_iota(jnp.int32, (tokens, 1), 0)
    second = (line >= rows).astype(jnp.int32)
    row_index = place_outer * 2 * block_rows + inside(slot, second, line - rows * second)
    line = lax.broadcasted_iota(jnp.int32, (1, 2 * block_rows), 1)
    slots = sum((line >= 2 * rows * number).astype(jnp.int32) for number in range(1, 4))
    left = line - 2 * rows * slots
    second = (left >= rows).astype(jnp.int32)
    key_place = inside(slots, second, left - rows * second)

    def joined(block, start):
        stop = start + HEAD_SIZE
        return jnp.concatenate([early[block][:early_rows, start:stop], late[block][:, start:stop]], axis=0)

    def block_scores(block):
        scores = lax.dot_general(
            stacked, joined(block, 0), (((1,), (1,)), ((), ())), preferred_element_type=jnp.float32
        )
        places = (place_outer ^ block) * 2 * block_rows + key_place
        allowed = (places <= row_index) & (key_document[block] == document)
        scores = scores.reshape(heads, tokens, -1) * score_scale
        return jnp.where(allowed[None], scores, masked_score).reshape(heads * tokens, -1)

    def weighted(block, weights):
        return product(weights.astype(jnp.bfloat16), joined(block, HEAD_SIZE))

    scores = block_scores(0)
    peak = jnp.max(scores, axis=-1, keepdims=True)
    weights = jnp.exp(scores - peak)
    peaks[...] = peak
    totals[...] = jnp.sum(weights, axis=-1, keepdims=True)
    summed[...] = weighted(0, weights)
    for block in range(1, blocks):

        @pl.when((place_outer ^ block) < place_outer)
        def _():
            scores = block_scores(block)
            before = peaks[...]
            peak = jnp.maximum(before, jnp.max(scores, axis=-1, keepdims=True))
            weights = jnp.exp(scores - peak)
            shrink = jnp.exp(before - peak)
            peaks[...] = peak
            totals[...] = totals[...] * shrink + jnp.sum(weights, axis=-1, keepdims=True)
            summed[...] = summed[...] * shrink + weighted(block, weights)

    result = (summed[...] / totals[...]).astype(jnp.bfloat16)
    for head in range(heads):
        out[:, head * HEAD_SIZE : (head + 1) * HEAD_SIZE] = result[head * tokens : (head + 1) * tokens]


def short_body(hidden_in, norm_gain, w_query, w_key, value_weight, w_out, doc_ids, positions):
    place_outer = lax.axis_index("outer")
    place_inner = lax.axis_index("inner")
    place_tensor = lax.axis_index("tensor")
    outer_count = lax.axis_size("outer")
    rows, width = hidden_in.shape
    half_width = w_query.shape[0]
    query_half = w_query.shape[1] // 2
    slot_rows = 2 * rows
    early_rows = 3 * slot_rows
    bf16 = jnp.bfloat16
    across_inner = swap_pairs(2, 1)
    which = place_inner.reshape(1)

    def send(value, axis, pairs):
        return lax.ppermute(value, axis, pairs)

    def send_across(value, pairs):
        both = [(a * 4 + b, (1 - a) * 4 + c) for a in range(2) for b, c in pairs]
        return lax.ppermute(value, ("inner", "tensor"), both)

    half = ((rows, half_width), bf16, None)
    mine, others = call_kernel(
        norm_kernel, "norm", which, [hidden_in, norm_gain.reshape(1, width)], [None] * 2, [half] * 2
    )
    two, one, middle = swap_pairs(4, 2), swap_pairs(4, 1), [(1, 2), (2, 1)]
    two_mine = send(mine, "tensor", two)
    two_theirs = send_across(others, two)
    one_mine = send(mine, "tensor", one)
    one_theirs = send_across(others, one)
    theirs = send(others, "inner", across_inner)
    early = [[mine], [theirs], [one_mine], [one_theirs], [two_mine], [two_theirs]]

    facts = jnp.stack([doc_ids, positions])
    facts = jnp.stack([facts, send(facts, "inner", across_inner)])

    def relative(parts):
        pieces = [parts[:, k * rows : (k + 1) * rows] for k in range(4)]
        return jnp.stack(by_xor(pieces, place_tensor)).reshape(-1)

    documents = relative(facts[:, 0])
    row_positions = relative(facts[:, 1])
    padding = 16 * 2 * HEAD_SIZE - documents.shape[0]
    document_rows = jnp.pad(documents, (0, padding)).astype(bf16).reshape(16, 2 * HEAD_SIZE)
    inverse = jnp.asarray(yarn_inverse(HEAD_SIZE) * 2, dtype=jnp.float32)
    signs = jnp.asarray([-1.0] * (HEAD_SIZE // 2) + [1.0] * (HEAD_SIZE // 2), dtype=jnp.float32)
    attention_gain = 0.1 * math.log(yarn_factor) + 1.0
    angles = row_positions.astype(jnp.float32)[:, None] * inverse[None, :]
    cosines = jnp.cos(angles) * attention_gain
    sines = jnp.sin(angles) * attention_gain * signs

    tables = (cosines, sines)
    ends_mine = send(after(two_mine, *tables), "tensor", [(1, 0), (2, 3)])
    middle_mine = send(after(mine, two_mine, *tables), "tensor", middle)
    ends_theirs = send(after(two_theirs, *tables), "tensor", [(1, 0), (2, 3)])
    middle_theirs = send_across(after(others, two_mine, *tables), middle)
    late = [[middle_mine, ends_mine], [middle_theirs, ends_theirs]]

    def stack(name, chunks):
        flat = [array for chunk in chunks for array in chunk]
        return call_kernel(
            functools.partial(stack_kernel, [len(chunk) for chunk in chunks]), name, which, flat,
            [None] * len(flat), [((len(chunks) * rows, half_width), bf16, None)],
        )[0]

    def sent_half(whole):
        wide = whole.shape[1] // 2
        return lax.dynamic_slice_in_dim(whole, (1 - place_inner) * wide, wide, 1).astype(sum_type)

    def project_pair(stacked):
        keys, values = product(stacked, w_key), product(stacked, value_weight)
        gone = jnp.concatenate([sent_half(keys), sent_half(values)], axis=1)
        return keys, values, send(gone, "inner", across_inner)

    def project_query(stacked):
        queries = product(stacked, w_query)
        return queries, send(sent_half(queries), "inner", across_inner)

    def gather_pairs(pair):
        found = [pair]
        for flip in range(1, outer_count):
            found.append(send(pair, "outer", swap_pairs(outer_count, flip)))
        return found

    def rotate_pair(projected, first, extra):
        keys, values, came = projected
        count = came.shape[0]
        half_spec = pl.BlockSpec((count, HEAD_SIZE), lambda step, which: (0, which[0]))
        table_spec = pl.BlockSpec((count, HEAD_SIZE), lambda step, which: (first // count, 0))
        out_rows = count + sum(array.shape[0] for array in extra)
        return call_kernel(
            functools.partial(pair_kernel, rows), "pair", which,
            [keys, values, came, cosines, sines] + extra,
            [half_spec, half_spec, None, table_spec, table_spec] + [None] * len(extra),
            [((out_rows, 2 * HEAD_SIZE), bf16, None)],
        )[0]

    early_stacked = stack("early_rows", early)
    early_projected = project_pair(early_stacked)
    late_stacked = stack("late_rows", late)
    late_projected = project_pair(late_stacked)
    early_queries, early_came = project_query(after(early_stacked, late_projected[0]))
    late_queries, late_came = project_query(late_stacked)
    early_pairs = gather_pairs(rotate_pair(early_projected, 0, [document_rows]))
    late_pairs = gather_pairs(rotate_pair(late_projected, early_rows, []))
    key_documents = jnp.stack(
        [array[early_rows:].reshape(1, -1)[:, : 4 * slot_rows] for array in early_pairs]
    ).astype(jnp.int32)

    places = jnp.stack([place_outer, place_inner, place_tensor])

    def attend(slot, *wait):
        queries, came = (late_queries, late_came) if slot == 3 else (early_queries, early_came)
        block = slot % 3
        if wait:
            came = after(came, *wait)
        rows_spec = lambda wide, block: pl.BlockSpec((slot_rows, wide), lambda step, which: (block, 0))
        half_spec = pl.BlockSpec((slot_rows, query_half), lambda step, which: (block, which[1]))
        stacked = query_half // HEAD_SIZE * slot_rows
        return call_kernel(
            functools.partial(attention_kernel, slot, outer_count, rows), "attention", places,
            [queries, came, cosines, sines, documents[:, None], key_documents] + early_pairs + late_pairs,
            [
                half_spec, rows_spec(query_half, block),
                rows_spec(HEAD_SIZE, slot), rows_spec(HEAD_SIZE, slot), rows_spec(1, slot),
            ] + [None] * (1 + 2 * outer_count),
            [((slot_rows, query_half), bf16, None)],
            scratch=[
                pltpu.VMEM((stacked, 1), jnp.float32),
                pltpu.VMEM((stacked, 1), jnp.float32),
                pltpu.VMEM((stacked, HEAD_SIZE), jnp.float32),
            ],
        )[0]

    lower = place_inner == 0

    def joined(slot, *wait):
        attended = attend(slot, *wait)
        here = attended[:rows]
        came = send(attended[rows:], "inner", across_inner)
        return jnp.concatenate(
            [jnp.where(lower, here, came), jnp.where(lower, came, here)], axis=1
        )

    out_half = w_out.shape[1] // 2
    left, right = w_out[:, :out_half], w_out[:, out_half:]
    inward, outward = [(0, 1), (3, 2)], [(1, 0), (2, 3)]
    rows_3 = joined(3)
    rows_2 = joined(2)
    term_left = product(rows_3, left).astype(bf16)
    inward_left = send(term_left, "tensor", inward)
    term_right = product(rows_3, right).astype(bf16)
    came_middle = send(jnp.concatenate([term_left, term_right], axis=1), "tensor", middle)
    inward_right = send(term_right, "tensor", inward)
    rows_1 = joined(1, term_left, term_right)
    rows_0 = joined(0, term_left, term_right)
    term_1 = product(rows_1, w_out).astype(bf16)
    came_outward = send(term_1, "tensor", outward)
    sum_left = product(rows_2, left) + after(inward_left, term_1).astype(jnp.float32)
    two_left = send(sum_left.astype(bf16), "tensor", two)
    sum_right = product(rows_2, right) + inward_right.astype(jnp.float32)
    two_right = send(sum_right.astype(bf16), "tensor", two)
    came_inward = send(after(term_1, inward_right), "tensor", inward)
    total = lax.optimization_barrier(product(rows_0, w_out))
    total = total + hidden_in.astype(jnp.float32) + came_outward.astype(jnp.float32)
    total = total + came_inward.astype(jnp.float32) + came_middle.astype(jnp.float32)
    came_2 = jnp.concatenate([two_left, two_right], axis=1)
    return (total + came_2.astype(jnp.float32)).astype(bf16)


def solution(mesh):
    in_specs = (
        P(("outer", "inner", "tensor"), None),
        P(),
        P("inner", "tensor"),
        P("inner", "tensor"),
        P("inner", "tensor"),
        P("tensor", None),
        P(("outer", "inner")),
        P(("outer", "inner")),
    )
    out_specs = P(("outer", "inner", "tensor"), None)

    def chosen(*arrays):
        outer_count = mesh.shape["outer"]
        key_heads = arrays[3].shape[1] // HEAD_SIZE // mesh.shape["tensor"]
        short = (
            mesh.shape["tensor"] == 4
            and mesh.shape["inner"] == 2
            and key_heads == 2
            and outer_count & (outer_count - 1) == 0
            and arrays[0].shape[0] % (mesh.size * 16) == 0
            and arrays[0].shape[0] // outer_count <= 512
        )
        mapped = jax.shard_map(
            short_body if short else body,
            mesh=mesh, in_specs=in_specs, out_specs=out_specs, check_vma=False,
        )
        return mapped(*arrays)

    return chosen
```

```python
import functools
import math

import jax
import jax.numpy as jnp
from jax import lax
from jax.experimental import pallas as pl
from jax.experimental.pallas import tpu as pltpu
from jax.sharding import PartitionSpec as P

HEAD_SIZE = 128


rope_base = 500000.0
yarn_factor = 8.0
trained_context = 8192.0
beta_fast = 32.0
beta_slow = 1.0
norm_epsilon = 1e-05
masked_score = -1e30


def yarn_inverse(head_dim):
    half_dim = head_dim // 2

    def correction(rotations):
        return (
            head_dim
            * math.log(trained_context / (rotations * 2.0 * math.pi))
            / (2.0 * math.log(rope_base))
        )

    lowest = max(math.floor(correction(beta_fast)), 0)
    highest = min(math.ceil(correction(beta_slow)), head_dim - 1)
    spread = max(highest - lowest, 0.001)
    values = []
    for column in range(half_dim):
        extrapolated = rope_base ** (-2.0 * column / head_dim)
        ramp = min(max((column - lowest) / spread, 0.0), 1.0)
        values.append(extrapolated / yarn_factor * ramp + extrapolated * (1.0 - ramp))
    return values


def yarn_tables(positions, head_dim):
    inverse = jnp.asarray(yarn_inverse(head_dim), dtype=jnp.float32)
    attention_gain = 0.1 * math.log(yarn_factor) + 1.0
    angles = positions.astype(jnp.float32)[:, None] * inverse[None, :]
    return (jnp.cos(angles) * attention_gain, jnp.sin(angles) * attention_gain)


def apply_rotation(heads, cosine_table, sine_table):
    half_dim = heads.shape[-1] // 2
    first_half = heads[..., :half_dim]
    second_half = heads[..., half_dim:]
    cos_rows = cosine_table[:, None, :]
    sin_rows = sine_table[:, None, :]
    return jnp.concatenate(
        [
            first_half * cos_rows - second_half * sin_rows,
            second_half * cos_rows + first_half * sin_rows,
        ],
        axis=-1,
    )


def rms_normed(hidden_in, norm_gain):
    widened = hidden_in.astype(jnp.float32)
    power = jnp.mean(widened * widened, axis=-1, keepdims=True)
    return (widened * lax.rsqrt(power + norm_epsilon) * norm_gain).astype(jnp.bfloat16)


def body(hidden_in, norm_gain, w_query, w_key, value_weight, w_out, doc_ids, positions):
    normed = rms_normed(hidden_in, norm_gain)
    block_rows = lax.all_gather(normed, "tensor", axis=0, tiled=True)
    tokens_here = block_rows.shape[0]
    query_width = w_query.shape[1]
    key_width = w_key.shape[1]
    inner_count = lax.axis_size("inner")
    slice_width = w_query.shape[0]
    arranged = block_rows.reshape(tokens_here, inner_count, slice_width)
    received = lax.all_to_all(arranged, "inner", split_axis=1, concat_axis=0, tiled=True)
    received = received.reshape(inner_count * tokens_here, slice_width)
    stacked = jnp.concatenate([w_query, w_key, value_weight], axis=1)
    combined = lax.psum_scatter(
        jnp.dot(received, stacked, preferred_element_type=jnp.float32),
        "inner",
        scatter_dimension=0,
        tiled=True,
    )
    queries = combined[:, :query_width]
    key_matrix = combined[:, query_width : query_width + key_width]
    value_matrix = combined[:, query_width + key_width :]
    value_matrix = value_matrix.astype(jnp.bfloat16)
    heads_query = query_width // HEAD_SIZE
    heads_key = key_width // HEAD_SIZE
    queries_per_group = heads_query // heads_key
    cosine_table, sine_table = yarn_tables(positions, HEAD_SIZE)
    query_rot = (
        apply_rotation(
            queries.reshape(tokens_here, heads_query, HEAD_SIZE), cosine_table, sine_table
        )
        .astype(jnp.bfloat16)
        .reshape(tokens_here, query_width)
    )
    rotated_keys = (
        apply_rotation(
            key_matrix.reshape(tokens_here, heads_key, HEAD_SIZE), cosine_table, sine_table
        )
        .astype(jnp.bfloat16)
        .reshape(tokens_here, key_width)
    )
    documents = lax.all_gather(doc_ids, ("outer", "inner"), axis=0, tiled=True)
    length_all = documents.shape[0]
    block_index = lax.axis_index(("outer", "inner"))
    sequence_index = jnp.arange(length_all, dtype=jnp.int32)
    query_documents = lax.dynamic_slice_in_dim(documents, block_index * tokens_here, tokens_here, 0)
    query_index = lax.dynamic_slice_in_dim(
        sequence_index, block_index * tokens_here, tokens_here, 0
    )
    row_documents = jnp.tile(query_documents, queries_per_group)
    row_index = jnp.tile(query_index, queries_per_group)
    top_index = jnp.max(query_index)
    top_document = jnp.max(query_documents)
    low_document = jnp.min(query_documents)
    grouped_heads = jnp.transpose(
        query_rot.reshape(tokens_here, heads_key, queries_per_group, HEAD_SIZE), (1, 2, 0, 3)
    ).reshape(heads_key, queries_per_group * tokens_here, HEAD_SIZE)
    score_scale = HEAD_SIZE ** (-0.5)

    def key_block(running, block_keys, block_values, first_row):
        row_count = block_keys.shape[0]
        piece_index = lax.dynamic_slice_in_dim(sequence_index, first_row, row_count, 0)
        piece_documents = lax.dynamic_slice_in_dim(documents, first_row, row_count, 0)
        live = (
            (jnp.min(piece_index) <= top_index)
            & (jnp.min(piece_documents) <= top_document)
            & (jnp.max(piece_documents) >= low_document)
        )

        def attend(current):
            row_peaks, totals, summed = current
            heads_keys = block_keys.reshape(row_count, heads_key, HEAD_SIZE)
            heads_values = block_values.reshape(row_count, heads_key, HEAD_SIZE)
            scores = (
                jnp.einsum(
                    "hqd,khd->hqk", grouped_heads, heads_keys, preferred_element_type=jnp.float32
                )
                * score_scale
            )
            allowed = (row_index[:, None] >= piece_index[None, :]) & (
                row_documents[:, None] == piece_documents[None, :]
            )
            scores = jnp.where(allowed[None], scores, masked_score)
            fresh = jnp.maximum(row_peaks, jnp.max(scores, axis=-1))
            weights = jnp.where(allowed[None], jnp.exp(scores - fresh[..., None]), 0.0)
            shrink = jnp.exp(row_peaks - fresh)
            totals = totals * shrink + jnp.sum(weights, axis=-1)
            summed = summed * shrink[..., None] + jnp.einsum(
                "hqk,khd->hqd",
                weights.astype(jnp.bfloat16),
                heads_values,
                preferred_element_type=jnp.float32,
            )
            return (fresh, totals, summed)

        return lax.cond(live, attend, lambda current: current, running)

    initial = (
        jnp.full((heads_key, queries_per_group * tokens_here), masked_score, jnp.float32),
        jnp.zeros((heads_key, queries_per_group * tokens_here), jnp.float32),
        jnp.zeros((heads_key, queries_per_group * tokens_here, HEAD_SIZE), jnp.float32),
    )
    piece_keys = lax.all_gather(rotated_keys, ("outer", "inner"), axis=0, tiled=True)
    piece_values = lax.all_gather(value_matrix, ("outer", "inner"), axis=0, tiled=True)
    row_count = piece_keys.shape[0]
    step_rows = 512
    steps_count = row_count // step_rows
    split_keys = piece_keys.reshape(steps_count, step_rows, key_width)
    split_values = piece_values.reshape(steps_count, step_rows, key_width)
    offsets = jnp.arange(steps_count, dtype=jnp.int32) * step_rows

    def scan_step(current, inputs):
        block_keys, block_values, offset = inputs
        return (key_block(current, block_keys, block_values, offset), None)

    result, unused = lax.scan(scan_step, initial, (split_keys, split_values, offsets))
    row_peaks, totals, summed = result
    heads_out = (summed / totals[..., None]).astype(jnp.bfloat16)
    attended = jnp.transpose(
        heads_out.reshape(heads_key, queries_per_group, tokens_here, HEAD_SIZE), (2, 0, 1, 3)
    ).reshape(tokens_here, query_width)
    full_term = jnp.dot(attended, w_out, preferred_element_type=jnp.float32)
    projected = lax.psum_scatter(
        full_term.astype(jnp.bfloat16), "tensor", scatter_dimension=0, tiled=True
    ).astype(jnp.float32)
    return (hidden_in.astype(jnp.float32) + projected).astype(jnp.bfloat16)


def swap_pairs(axis_size, flip):
    return [(place, place ^ flip) for place in range(axis_size)]


def after(value, *others):
    return lax.optimization_barrier((value,) + others)[0]


def whole_spec(array):
    zeros = (0,) * array.ndim
    return pl.BlockSpec(array.shape, lambda step, which: zeros)


def call_kernel(kernel, name, which, arrays, specs, outs, steps=1, scratch=(), mebibytes=16):
    shapes = [jax.ShapeDtypeStruct(shape, dtype) for shape, dtype, unused in outs]
    out_specs = [
        whole_spec(shape) if spec is None else spec for shape, (a, b, spec) in zip(shapes, outs)
    ]
    found = pl.pallas_call(
        kernel,
        name=name,
        grid_spec=pltpu.PrefetchScalarGridSpec(
            num_scalar_prefetch=1,
            grid=(steps,),
            in_specs=[
                whole_spec(array) if spec is None else spec for array, spec in zip(arrays, specs)
            ],
            out_specs=out_specs,
            scratch_shapes=list(scratch),
        ),
        out_shape=shapes,
        compiler_params=pltpu.CompilerParams(vmem_limit_bytes=mebibytes * 1024 * 1024),
    )(which, *arrays)
    return found


def norm_kernel(which, hidden, gain, mine, others):
    half_width = mine.shape[1]
    widened = hidden[...].astype(jnp.float32)
    power = jnp.mean(widened * widened, axis=-1, keepdims=True)
    normed = (widened * lax.rsqrt(power + norm_epsilon) * gain[...]).astype(jnp.bfloat16)

    @pl.when(which[0] == 0)
    def _():
        mine[...] = normed[:, :half_width]
        others[...] = normed[:, half_width:]

    @pl.when(which[0] != 0)
    def _():
        mine[...] = normed[:, half_width:]
        others[...] = normed[:, :half_width]


def stacked_rows(chunks):
    return jnp.concatenate(
        [
            chunk[...] if len(pair) == 1 else pair[0][...] + pair[1][...]
            for pair in chunks
            for chunk in pair[:1]
        ],
        axis=0,
    )


def split_chunks(refs, widths):
    chunks = []
    place = 0
    for width in widths:
        chunks.append(refs[place : place + width])
        place += width
    return chunks, refs[place:]


def product(left, right):
    return jnp.dot(left, right, preferred_element_type=jnp.float32)


def stack_kernel(widths, which, *refs):
    chunks, outs = split_chunks(refs, widths)
    outs[0][...] = stacked_rows(chunks)
    for place, out in zip((0, outs[0].shape[0] * 2 // 3), outs[1:]):
        out[...] = outs[0][place : place + out.shape[0]]


def other_part(value, rows):
    pieces = [value[place : place + rows] for place in range(0, value.shape[0], rows)]
    return jnp.concatenate([pieces[k ^ 1] for k in range(len(pieces))], axis=0)


def rotated(part, cosine_rows, sine_rows):
    return part * cosine_rows + pltpu.roll(part, HEAD_SIZE // 2, 1) * sine_rows


def pair_kernel(rows, which, keys, values, came, cosines, sines, *refs):
    out = refs[-1]
    count = keys.shape[0]
    added = other_part(came[...], rows).astype(jnp.float32)
    whole = rotated(keys[...] + added[:, :HEAD_SIZE], cosines[...], sines[...])
    out[:count, :HEAD_SIZE] = whole.astype(jnp.bfloat16)
    out[:count, HEAD_SIZE:] = (values[...] + added[:, HEAD_SIZE:]).astype(jnp.bfloat16)
    if len(refs) == 2:
        out[count:, :] = refs[0][...]


def facts_kernel(rows, which, here, there, inverse, angles, documents, document_rows):
    block = here.shape[1]
    line = lax.broadcasted_iota(jnp.int32, (block, 1), 0)
    slots = sum((line >= rows * number).astype(jnp.int32) for number in range(1, 4))
    source = (which[2] ^ slots) * rows + line - rows * slots
    chosen = lax.broadcasted_iota(jnp.int32, (block, block), 1) == source

    def ordered(row):
        parts = [
            jnp.sum(jnp.where(chosen, part[row : row + 1, :].astype(jnp.float32), 0.0), axis=1, keepdims=True)
            for part in (here, there)
        ]
        return jnp.concatenate(
            [part[place : place + rows] for place in range(0, block, rows) for part in parts], axis=0
        )

    angles[...] = ordered(1) * inverse[...]
    column = ordered(0)
    documents[...] = column
    count = column.shape[0]
    same = lax.broadcasted_iota(jnp.int32, (count, count), 0) == lax.broadcasted_iota(
        jnp.int32, (count, count), 1
    )
    wide = document_rows.shape[1]
    across = jnp.sum(jnp.where(same, column, 0.0), axis=0, keepdims=True)
    rest = jnp.concatenate(
        [across[:, wide:], jnp.zeros((1, 2 * wide - count), jnp.float32)], axis=1
    )
    number = lax.broadcasted_iota(jnp.int32, document_rows.shape, 0)
    document_rows[...] = jnp.where(
        number == 0, across[:, :wide], jnp.where(number == 1, rest, 0.0)
    ).astype(jnp.bfloat16)


def copy_kernel(which, *refs):
    *parts, out = refs
    place = 0
    for part in parts:
        out[:, place : place + part.shape[1]] = part[...].astype(out.dtype)
        place += part.shape[1]


def join_kernel(which, here, came, out):
    width = here.shape[1]

    @pl.when(which[1] == 0)
    def _():
        out[:, :width] = here[...]
        out[:, width:] = came[...]

    @pl.when(which[1] != 0)
    def _():
        out[:, :width] = came[...]
        out[:, width:] = here[...]


def attention_kernel(
    slot, blocks, rows, which, kept, came, cosines, sines, query_document, *refs
):
    early, late = refs[:blocks], refs[blocks : 2 * blocks]
    here, gone, peaks, totals, summed = refs[2 * blocks :]
    tokens, width = came.shape
    heads = width // HEAD_SIZE
    score_scale = HEAD_SIZE ** (-0.5)
    block_rows = 4 * rows
    early_rows = 2 * block_rows - late[0].shape[0]
    whole = kept[...] + other_part(came[...], rows).astype(jnp.float32)
    stacked = jnp.concatenate(
        [
            rotated(whole[:, place : place + HEAD_SIZE], cosines[...], sines[...]).astype(
                jnp.bfloat16
            )
            for place in range(0, width, HEAD_SIZE)
        ],
        axis=0,
    )
    place_outer, place_inner, place_tensor = which[0], which[1], which[2]
    document = query_document[...]

    def inside(slot_number, part_number, row_number):
        return (place_inner ^ part_number) * block_rows + (place_tensor ^ slot_number) * rows + row_number

    line = lax.broadcasted_iota(jnp.int32, (tokens, 1), 0)
    second = (line >= rows).astype(jnp.int32)
    row_index = place_outer * 2 * block_rows + inside(slot, second, line - rows * second)
    line = lax.broadcasted_iota(jnp.int32, (1, 2 * block_rows), 1)
    slots = sum((line >= 2 * rows * number).astype(jnp.int32) for number in range(1, 4))
    left = line - 2 * rows * slots
    second = (left >= rows).astype(jnp.int32)
    key_place = inside(slots, second, left - rows * second)

    def joined(block, start):
        stop = start + HEAD_SIZE
        return jnp.concatenate([early[block][:early_rows, start:stop], late[block][:, start:stop]], axis=0)

    def block_scores(block):
        scores = lax.dot_general(
            stacked, joined(block, 0), (((1,), (1,)), ((), ())), preferred_element_type=jnp.float32
        )
        places = (place_outer ^ block) * 2 * block_rows + key_place
        lines = early[block][early_rows:, :].astype(jnp.float32)
        rest = 2 * block_rows - lines.shape[1]
        key_document = jnp.concatenate([lines[0:1, :], lines[1:2, :rest]], axis=1)
        allowed = (places <= row_index) & (key_document == document)
        scores = scores.reshape(heads, tokens, -1) * score_scale
        return jnp.where(allowed[None], scores, masked_score).reshape(heads * tokens, -1)

    def weighted(block, weights):
        return product(weights.astype(jnp.bfloat16), joined(block, HEAD_SIZE))

    scores = block_scores(0)
    peak = jnp.max(scores, axis=-1, keepdims=True)
    weights = jnp.exp(scores - peak)
    peaks[...] = peak
    totals[...] = jnp.sum(weights, axis=-1, keepdims=True)
    summed[...] = weighted(0, weights)
    for block in range(1, blocks):

        @pl.when((place_outer ^ block) < place_outer)
        def _():
            scores = block_scores(block)
            before = peaks[...]
            peak = jnp.maximum(before, jnp.max(scores, axis=-1, keepdims=True))
            weights = jnp.exp(scores - peak)
            shrink = jnp.exp(before - peak)
            peaks[...] = peak
            totals[...] = totals[...] * shrink + jnp.sum(weights, axis=-1, keepdims=True)
            summed[...] = summed[...] * shrink + weighted(block, weights)

    result = (summed[...] / totals[...]).astype(jnp.bfloat16)
    for head in range(heads):
        first = head * tokens
        columns = slice(head * HEAD_SIZE, (head + 1) * HEAD_SIZE)
        here[:, columns] = result[first : first + rows]
        gone[:, columns] = result[first + rows : first + tokens]


def short_body(hidden_in, norm_gain, w_query, w_key, value_weight, w_out, doc_ids, positions):
    place_outer = lax.axis_index("outer")
    place_inner = lax.axis_index("inner")
    place_tensor = lax.axis_index("tensor")
    outer_count = lax.axis_size("outer")
    rows, width = hidden_in.shape
    half_width = w_query.shape[0]
    query_half = w_query.shape[1] // 2
    slot_rows = 2 * rows
    early_rows = 3 * slot_rows
    bf16 = jnp.bfloat16
    across_inner = swap_pairs(2, 1)
    which = place_inner.reshape(1)
    places = jnp.stack([place_outer, place_inner, place_tensor])
    hidden_in, which, places = lax.optimization_barrier((hidden_in, which, places))

    def send(value, axis, pairs):
        return lax.ppermute(value, axis, pairs)

    def send_across(value, pairs):
        both = [(a * 4 + b, (1 - a) * 4 + c) for a in range(2) for b, c in pairs]
        return lax.ppermute(value, ("inner", "tensor"), both)

    half = ((rows, half_width), bf16, None)
    mine, others = call_kernel(
        norm_kernel, "norm", which, [hidden_in, norm_gain.reshape(1, width)], [None] * 2, [half] * 2
    )
    two, one, middle = swap_pairs(4, 2), swap_pairs(4, 1), [(1, 2), (2, 1)]
    two_mine = send(mine, "tensor", two)
    two_theirs = send_across(others, two)
    one_mine = send(mine, "tensor", one)
    one_theirs = send_across(others, one)
    theirs = send(others, "inner", across_inner)
    early = [[mine], [theirs], [one_mine], [one_theirs], [two_mine], [two_theirs]]

    facts = jnp.stack([doc_ids, positions])
    facts_there = send(after(facts, theirs), "inner", across_inner)
    inverse = jnp.asarray([yarn_inverse(HEAD_SIZE) * 2], dtype=jnp.float32)
    signs = jnp.asarray([-1.0] * (HEAD_SIZE // 2) + [1.0] * (HEAD_SIZE // 2), dtype=jnp.float32)
    attention_gain = 0.1 * math.log(yarn_factor) + 1.0
    angles, documents, document_rows = call_kernel(
        functools.partial(facts_kernel, rows), "facts", places, [facts, facts_there, inverse],
        [None] * 3,
        [
            ((4 * slot_rows, HEAD_SIZE), jnp.float32, None),
            ((4 * slot_rows, 1), jnp.float32, None),
            ((16, 2 * HEAD_SIZE), bf16, None),
        ],
    )
    cosines = jnp.cos(angles) * attention_gain
    sines = jnp.sin(angles) * attention_gain * signs

    def stack(name, chunks, parts):
        flat = [array for chunk in chunks for array in chunk]
        out = lambda count: ((count * slot_rows, half_width), bf16, None)
        return call_kernel(
            functools.partial(stack_kernel, [len(chunk) for chunk in chunks]), name, which, flat,
            [None] * len(flat), [out(count) for count in parts],
        )

    def sent_halves(wholes, kind):
        count = wholes[0].shape[0]
        wides = [whole.shape[1] // 2 for whole in wholes]
        specs = [
            pl.BlockSpec((count, wide), lambda step, which: (0, 1 - which[1])) for wide in wides
        ]
        return call_kernel(
            copy_kernel, "sent", places, wholes, specs, [((count, sum(wides)), kind, None)]
        )[0]

    def project_pair(stacked):
        keys, values = product(stacked, w_key), product(stacked, value_weight)
        return keys, values, send(sent_halves([keys, values], jnp.float32), "inner", across_inner)

    def project_query(stacked):
        queries = product(stacked, w_query)
        return queries, send(sent_halves([queries], bf16), "inner", across_inner)

    def gather_pairs(pair):
        found = [pair]
        for flip in range(1, outer_count):
            found.append(send(pair, "outer", swap_pairs(outer_count, flip)))
        return found

    def rotate_pair(projected, first, extra):
        keys, values, came = projected
        count = came.shape[0]
        half_spec = pl.BlockSpec((count, HEAD_SIZE), lambda step, which: (0, which[0]))
        table_spec = pl.BlockSpec((count, HEAD_SIZE), lambda step, which: (first // count, 0))
        out_rows = count + sum(array.shape[0] for array in extra)
        return call_kernel(
            functools.partial(pair_kernel, rows), "pair", which,
            [keys, values, came, cosines, sines] + extra,
            [half_spec, half_spec, None, table_spec, table_spec] + [None] * len(extra),
            [((out_rows, 2 * HEAD_SIZE), bf16, None)],
        )[0]

    early_stacked, own_rows, two_rows = stack("early_rows", early, (3, 1, 1))
    middle_rows = send(own_rows, "tensor", middle)
    ends_rows = send(two_rows, "tensor", [(1, 0), (2, 3)])
    early_projected = project_pair(early_stacked)
    early_queries, early_came = project_query(early_stacked)
    late_stacked = stack("late_rows", [[ends_rows, middle_rows]], (1,))[0]
    late_projected = project_pair(late_stacked)
    late_queries, late_came = project_query(late_stacked)
    early_pairs = gather_pairs(rotate_pair(early_projected, 0, [document_rows]))
    late_pairs = gather_pairs(rotate_pair(late_projected, early_rows, []))

    def attend(slot, *wait):
        queries, came = (late_queries, late_came) if slot == 3 else (early_queries, early_came)
        block = slot % 3
        if wait:
            came = after(came, *wait)
        rows_spec = lambda wide, block: pl.BlockSpec((slot_rows, wide), lambda step, which: (block, 0))
        half_spec = pl.BlockSpec((slot_rows, query_half), lambda step, which: (block, which[1]))
        stacked = query_half // HEAD_SIZE * slot_rows
        return call_kernel(
            functools.partial(attention_kernel, slot, outer_count, rows), "attention", places,
            [queries, came, cosines, sines, documents] + early_pairs + late_pairs,
            [
                half_spec, rows_spec(query_half, block),
                rows_spec(HEAD_SIZE, slot), rows_spec(HEAD_SIZE, slot), rows_spec(1, slot),
            ] + [None] * (2 * outer_count),
            [((rows, query_half), bf16, None)] * 2,
            scratch=[
                pltpu.VMEM((stacked, 1), jnp.float32),
                pltpu.VMEM((stacked, 1), jnp.float32),
                pltpu.VMEM((stacked, HEAD_SIZE), jnp.float32),
            ],
        )

    def joined(slot, *wait):
        here, gone = attend(slot, *wait)
        came = send(gone, "inner", across_inner)
        return call_kernel(
            join_kernel, "join", places, [here, came], [None] * 2,
            [((rows, 2 * query_half), bf16, None)],
        )[0]

    out_half = w_out.shape[1] // 2
    left, right = w_out[:, :out_half], w_out[:, out_half:]
    inward, outward = [(0, 1), (3, 2)], [(1, 0), (2, 3)]
    rows_3 = joined(3)
    rows_2 = joined(2)
    term_left = product(rows_3, left).astype(bf16)
    inward_left = send(term_left, "tensor", inward)
    term_right = product(rows_3, right).astype(bf16)
    came_middle = send(jnp.concatenate([term_left, term_right], axis=1), "tensor", middle)
    inward_right = send(term_right, "tensor", inward)
    rows_1 = joined(1, term_left, term_right)
    rows_0 = joined(0, term_left, term_right)
    term_1 = product(rows_1, w_out).astype(bf16)
    came_outward = send(term_1, "tensor", outward)
    sum_left = product(rows_2, left) + after(inward_left, term_1).astype(jnp.float32)
    two_left = send(sum_left.astype(bf16), "tensor", two)
    sum_right = product(rows_2, right) + inward_right.astype(jnp.float32)
    two_right = send(sum_right.astype(bf16), "tensor", two)
    came_inward = send(after(term_1, inward_left), "tensor", inward)
    total = lax.optimization_barrier(product(rows_0, w_out))
    total = total + hidden_in.astype(jnp.float32) + came_outward.astype(jnp.float32)
    total = total + came_inward.astype(jnp.float32) + came_middle.astype(jnp.float32)
    came_2 = jnp.concatenate([two_left, two_right], axis=1)
    return (total + came_2.astype(jnp.float32)).astype(bf16)


def solution(mesh):
    in_specs = (
        P(("outer", "inner", "tensor"), None),
        P(),
        P("inner", "tensor"),
        P("inner", "tensor"),
        P("inner", "tensor"),
        P("tensor", None),
        P(("outer", "inner")),
        P(("outer", "inner")),
    )
    out_specs = P(("outer", "inner", "tensor"), None)

    def chosen(*arrays):
        outer_count = mesh.shape["outer"]
        key_heads = arrays[3].shape[1] // HEAD_SIZE // mesh.shape["tensor"]
        short = (
            mesh.shape["tensor"] == 4
            and mesh.shape["inner"] == 2
            and key_heads == 2
            and outer_count & (outer_count - 1) == 0
            and arrays[0].shape[0] % (mesh.size * 16) == 0
            and arrays[0].shape[0] // outer_count <= 512
        )
        mapped = jax.shard_map(
            short_body if short else body,
            mesh=mesh, in_specs=in_specs, out_specs=out_specs, check_vma=False,
        )
        return mapped(*arrays)

    return chosen
```

```python
import functools
import math

import jax
import jax.numpy as jnp
from jax import lax
from jax.experimental import pallas as pl
from jax.experimental.pallas import tpu as pltpu
from jax.sharding import PartitionSpec as P

HEAD_SIZE = 128


rope_base = 500000.0
yarn_factor = 8.0
trained_context = 8192.0
beta_fast = 32.0
beta_slow = 1.0
norm_epsilon = 1e-05
masked_score = -1e30


def yarn_inverse(head_dim):
    half_dim = head_dim // 2

    def correction(rotations):
        return (
            head_dim
            * math.log(trained_context / (rotations * 2.0 * math.pi))
            / (2.0 * math.log(rope_base))
        )

    lowest = max(math.floor(correction(beta_fast)), 0)
    highest = min(math.ceil(correction(beta_slow)), head_dim - 1)
    spread = max(highest - lowest, 0.001)
    values = []
    for column in range(half_dim):
        extrapolated = rope_base ** (-2.0 * column / head_dim)
        ramp = min(max((column - lowest) / spread, 0.0), 1.0)
        values.append(extrapolated / yarn_factor * ramp + extrapolated * (1.0 - ramp))
    return values


def yarn_tables(positions, head_dim):
    inverse = jnp.asarray(yarn_inverse(head_dim), dtype=jnp.float32)
    attention_gain = 0.1 * math.log(yarn_factor) + 1.0
    angles = positions.astype(jnp.float32)[:, None] * inverse[None, :]
    return (jnp.cos(angles) * attention_gain, jnp.sin(angles) * attention_gain)


def apply_rotation(heads, cosine_table, sine_table):
    half_dim = heads.shape[-1] // 2
    first_half = heads[..., :half_dim]
    second_half = heads[..., half_dim:]
    cos_rows = cosine_table[:, None, :]
    sin_rows = sine_table[:, None, :]
    return jnp.concatenate(
        [
            first_half * cos_rows - second_half * sin_rows,
            second_half * cos_rows + first_half * sin_rows,
        ],
        axis=-1,
    )


def rms_normed(hidden_in, norm_gain):
    widened = hidden_in.astype(jnp.float32)
    power = jnp.mean(widened * widened, axis=-1, keepdims=True)
    return (widened * lax.rsqrt(power + norm_epsilon) * norm_gain).astype(jnp.bfloat16)


def body(hidden_in, norm_gain, w_query, w_key, value_weight, w_out, doc_ids, positions):
    normed = rms_normed(hidden_in, norm_gain)
    block_rows = lax.all_gather(normed, "tensor", axis=0, tiled=True)
    tokens_here = block_rows.shape[0]
    query_width = w_query.shape[1]
    key_width = w_key.shape[1]
    inner_count = lax.axis_size("inner")
    slice_width = w_query.shape[0]
    arranged = block_rows.reshape(tokens_here, inner_count, slice_width)
    received = lax.all_to_all(arranged, "inner", split_axis=1, concat_axis=0, tiled=True)
    received = received.reshape(inner_count * tokens_here, slice_width)
    stacked = jnp.concatenate([w_query, w_key, value_weight], axis=1)
    combined = lax.psum_scatter(
        jnp.dot(received, stacked, preferred_element_type=jnp.float32),
        "inner",
        scatter_dimension=0,
        tiled=True,
    )
    queries = combined[:, :query_width]
    key_matrix = combined[:, query_width : query_width + key_width]
    value_matrix = combined[:, query_width + key_width :]
    value_matrix = value_matrix.astype(jnp.bfloat16)
    heads_query = query_width // HEAD_SIZE
    heads_key = key_width // HEAD_SIZE
    queries_per_group = heads_query // heads_key
    cosine_table, sine_table = yarn_tables(positions, HEAD_SIZE)
    query_rot = (
        apply_rotation(
            queries.reshape(tokens_here, heads_query, HEAD_SIZE), cosine_table, sine_table
        )
        .astype(jnp.bfloat16)
        .reshape(tokens_here, query_width)
    )
    rotated_keys = (
        apply_rotation(
            key_matrix.reshape(tokens_here, heads_key, HEAD_SIZE), cosine_table, sine_table
        )
        .astype(jnp.bfloat16)
        .reshape(tokens_here, key_width)
    )
    documents = lax.all_gather(doc_ids, ("outer", "inner"), axis=0, tiled=True)
    length_all = documents.shape[0]
    block_index = lax.axis_index(("outer", "inner"))
    sequence_index = jnp.arange(length_all, dtype=jnp.int32)
    query_documents = lax.dynamic_slice_in_dim(documents, block_index * tokens_here, tokens_here, 0)
    query_index = lax.dynamic_slice_in_dim(
        sequence_index, block_index * tokens_here, tokens_here, 0
    )
    row_documents = jnp.tile(query_documents, queries_per_group)
    row_index = jnp.tile(query_index, queries_per_group)
    top_index = jnp.max(query_index)
    top_document = jnp.max(query_documents)
    low_document = jnp.min(query_documents)
    grouped_heads = jnp.transpose(
        query_rot.reshape(tokens_here, heads_key, queries_per_group, HEAD_SIZE), (1, 2, 0, 3)
    ).reshape(heads_key, queries_per_group * tokens_here, HEAD_SIZE)
    score_scale = HEAD_SIZE ** (-0.5)

    def key_block(running, block_keys, block_values, first_row):
        row_count = block_keys.shape[0]
        piece_index = lax.dynamic_slice_in_dim(sequence_index, first_row, row_count, 0)
        piece_documents = lax.dynamic_slice_in_dim(documents, first_row, row_count, 0)
        live = (
            (jnp.min(piece_index) <= top_index)
            & (jnp.min(piece_documents) <= top_document)
            & (jnp.max(piece_documents) >= low_document)
        )

        def attend(current):
            row_peaks, totals, summed = current
            heads_keys = block_keys.reshape(row_count, heads_key, HEAD_SIZE)
            heads_values = block_values.reshape(row_count, heads_key, HEAD_SIZE)
            scores = (
                jnp.einsum(
                    "hqd,khd->hqk", grouped_heads, heads_keys, preferred_element_type=jnp.float32
                )
                * score_scale
            )
            allowed = (row_index[:, None] >= piece_index[None, :]) & (
                row_documents[:, None] == piece_documents[None, :]
            )
            scores = jnp.where(allowed[None], scores, masked_score)
            fresh = jnp.maximum(row_peaks, jnp.max(scores, axis=-1))
            weights = jnp.where(allowed[None], jnp.exp(scores - fresh[..., None]), 0.0)
            shrink = jnp.exp(row_peaks - fresh)
            totals = totals * shrink + jnp.sum(weights, axis=-1)
            summed = summed * shrink[..., None] + jnp.einsum(
                "hqk,khd->hqd",
                weights.astype(jnp.bfloat16),
                heads_values,
                preferred_element_type=jnp.float32,
            )
            return (fresh, totals, summed)

        return lax.cond(live, attend, lambda current: current, running)

    initial = (
        jnp.full((heads_key, queries_per_group * tokens_here), masked_score, jnp.float32),
        jnp.zeros((heads_key, queries_per_group * tokens_here), jnp.float32),
        jnp.zeros((heads_key, queries_per_group * tokens_here, HEAD_SIZE), jnp.float32),
    )
    piece_keys = lax.all_gather(rotated_keys, ("outer", "inner"), axis=0, tiled=True)
    piece_values = lax.all_gather(value_matrix, ("outer", "inner"), axis=0, tiled=True)
    row_count = piece_keys.shape[0]
    step_rows = 512
    steps_count = row_count // step_rows
    split_keys = piece_keys.reshape(steps_count, step_rows, key_width)
    split_values = piece_values.reshape(steps_count, step_rows, key_width)
    offsets = jnp.arange(steps_count, dtype=jnp.int32) * step_rows

    def scan_step(current, inputs):
        block_keys, block_values, offset = inputs
        return (key_block(current, block_keys, block_values, offset), None)

    result, unused = lax.scan(scan_step, initial, (split_keys, split_values, offsets))
    row_peaks, totals, summed = result
    heads_out = (summed / totals[..., None]).astype(jnp.bfloat16)
    attended = jnp.transpose(
        heads_out.reshape(heads_key, queries_per_group, tokens_here, HEAD_SIZE), (2, 0, 1, 3)
    ).reshape(tokens_here, query_width)
    full_term = jnp.dot(attended, w_out, preferred_element_type=jnp.float32)
    projected = lax.psum_scatter(
        full_term.astype(jnp.bfloat16), "tensor", scatter_dimension=0, tiled=True
    ).astype(jnp.float32)
    return (hidden_in.astype(jnp.float32) + projected).astype(jnp.bfloat16)


def swap_pairs(axis_size, flip):
    return [(place, place ^ flip) for place in range(axis_size)]


def after(value, *others):
    return lax.optimization_barrier((value,) + others)[0]


def whole_spec(array):
    zeros = (0,) * array.ndim
    return pl.BlockSpec(array.shape, lambda step, which: zeros)


def call_kernel(kernel, name, which, arrays, specs, outs, steps=1, scratch=(), mebibytes=16):
    shapes = [jax.ShapeDtypeStruct(shape, dtype) for shape, dtype, unused in outs]
    out_specs = [
        whole_spec(shape) if spec is None else spec for shape, (a, b, spec) in zip(shapes, outs)
    ]
    found = pl.pallas_call(
        kernel,
        name=name,
        grid_spec=pltpu.PrefetchScalarGridSpec(
            num_scalar_prefetch=1,
            grid=(steps,),
            in_specs=[
                whole_spec(array) if spec is None else spec for array, spec in zip(arrays, specs)
            ],
            out_specs=out_specs,
            scratch_shapes=list(scratch),
        ),
        out_shape=shapes,
        compiler_params=pltpu.CompilerParams(vmem_limit_bytes=mebibytes * 1024 * 1024),
    )(which, *arrays)
    return found


def norm_kernel(which, hidden, gain, mine, others):
    half_width = mine.shape[1]
    widened = hidden[...].astype(jnp.float32)
    power = jnp.mean(widened * widened, axis=-1, keepdims=True)
    normed = (widened * lax.rsqrt(power + norm_epsilon) * gain[...]).astype(jnp.bfloat16)

    @pl.when(which[0] == 0)
    def _():
        mine[...] = normed[:, :half_width]
        others[...] = normed[:, half_width:]

    @pl.when(which[0] != 0)
    def _():
        mine[...] = normed[:, half_width:]
        others[...] = normed[:, :half_width]


def stacked_rows(chunks):
    return jnp.concatenate(
        [
            chunk[...] if len(pair) == 1 else pair[0][...] + pair[1][...]
            for pair in chunks
            for chunk in pair[:1]
        ],
        axis=0,
    )


def split_chunks(refs, widths):
    chunks = []
    place = 0
    for width in widths:
        chunks.append(refs[place : place + width])
        place += width
    return chunks, refs[place:]


def product(left, right):
    return jnp.dot(left, right, preferred_element_type=jnp.float32)


def stack_kernel(widths, which, *refs):
    chunks, outs = split_chunks(refs, widths)
    outs[0][...] = stacked_rows(chunks)
    for place, out in zip((0, outs[0].shape[0] * 2 // 3), outs[1:]):
        out[...] = outs[0][place : place + out.shape[0]]


def other_part(value, rows):
    pieces = [value[place : place + rows] for place in range(0, value.shape[0], rows)]
    return jnp.concatenate([pieces[k ^ 1] for k in range(len(pieces))], axis=0)


def rotated(part, cosine_rows, sine_rows):
    return part * cosine_rows + pltpu.roll(part, HEAD_SIZE // 2, 1) * sine_rows


def pair_kernel(rows, which, keys, values, came, cosines, sines, *refs):
    out = refs[-1]
    count = keys.shape[0]
    added = other_part(came[...], rows).astype(jnp.float32)
    whole = rotated(keys[...] + added[:, :HEAD_SIZE], cosines[...], sines[...])
    out[:count, :HEAD_SIZE] = whole.astype(jnp.bfloat16)
    out[:count, HEAD_SIZE:] = (values[...] + added[:, HEAD_SIZE:]).astype(jnp.bfloat16)
    if len(refs) == 2:
        out[count:, :] = refs[0][...]


def facts_kernel(rows, which, here, there, inverse, angles, documents, document_rows):
    block = here.shape[1]
    line = lax.broadcasted_iota(jnp.int32, (block, 1), 0)
    slots = sum((line >= rows * number).astype(jnp.int32) for number in range(1, 4))
    source = (which[2] ^ slots) * rows + line - rows * slots
    chosen = lax.broadcasted_iota(jnp.int32, (block, block), 1) == source

    def ordered(row):
        parts = [
            jnp.sum(jnp.where(chosen, part[row : row + 1, :].astype(jnp.float32), 0.0), axis=1, keepdims=True)
            for part in (here, there)
        ]
        return jnp.concatenate(
            [part[place : place + rows] for place in range(0, block, rows) for part in parts], axis=0
        )

    angles[...] = ordered(1) * inverse[...]
    column = ordered(0)
    documents[...] = column
    count = column.shape[0]
    same = lax.broadcasted_iota(jnp.int32, (count, count), 0) == lax.broadcasted_iota(
        jnp.int32, (count, count), 1
    )
    wide = document_rows.shape[1]
    across = jnp.sum(jnp.where(same, column, 0.0), axis=0, keepdims=True)
    rest = jnp.concatenate(
        [across[:, wide:], jnp.zeros((1, 2 * wide - count), jnp.float32)], axis=1
    )
    number = lax.broadcasted_iota(jnp.int32, document_rows.shape, 0)
    document_rows[...] = jnp.where(
        number == 0, across[:, :wide], jnp.where(number == 1, rest, 0.0)
    ).astype(jnp.bfloat16)


def copy_kernel(which, *refs):
    *parts, out = refs
    place = 0
    for part in parts:
        out[:, place : place + part.shape[1]] = part[...].astype(out.dtype)
        place += part.shape[1]


def join_kernel(which, here, came, out):
    width = here.shape[1]

    @pl.when(which[1] == 0)
    def _():
        out[:, :width] = here[...]
        out[:, width:] = came[...]

    @pl.when(which[1] != 0)
    def _():
        out[:, :width] = came[...]
        out[:, width:] = here[...]


def attention_kernel(
    slot, blocks, rows, which, kept, came, cosines, sines, query_document, *refs
):
    early, late = refs[:blocks], refs[blocks : 2 * blocks]
    here, gone, peaks, totals, summed = refs[2 * blocks :]
    tokens, width = came.shape
    heads = width // HEAD_SIZE
    score_scale = HEAD_SIZE ** (-0.5)
    block_rows = 4 * rows
    early_rows = 2 * block_rows - late[0].shape[0]
    whole = kept[...] + other_part(came[...], rows).astype(jnp.float32)
    stacked = jnp.concatenate(
        [
            rotated(whole[:, place : place + HEAD_SIZE], cosines[...], sines[...]).astype(
                jnp.bfloat16
            )
            for place in range(0, width, HEAD_SIZE)
        ],
        axis=0,
    )
    place_outer, place_inner, place_tensor = which[0], which[1], which[2]
    document = query_document[...]

    def inside(slot_number, part_number, row_number):
        return (place_inner ^ part_number) * block_rows + (place_tensor ^ slot_number) * rows + row_number

    line = lax.broadcasted_iota(jnp.int32, (tokens, 1), 0)
    second = (line >= rows).astype(jnp.int32)
    row_index = place_outer * 2 * block_rows + inside(slot, second, line - rows * second)
    line = lax.broadcasted_iota(jnp.int32, (1, 2 * block_rows), 1)
    slots = sum((line >= 2 * rows * number).astype(jnp.int32) for number in range(1, 4))
    left = line - 2 * rows * slots
    second = (left >= rows).astype(jnp.int32)
    key_place = inside(slots, second, left - rows * second)

    def joined(block, start):
        stop = start + HEAD_SIZE
        return jnp.concatenate([early[block][:early_rows, start:stop], late[block][:, start:stop]], axis=0)

    def block_scores(block):
        scores = lax.dot_general(
            stacked, joined(block, 0), (((1,), (1,)), ((), ())), preferred_element_type=jnp.float32
        )
        places = (place_outer ^ block) * 2 * block_rows + key_place
        lines = early[block][early_rows:, :].astype(jnp.float32)
        rest = 2 * block_rows - lines.shape[1]
        key_document = jnp.concatenate([lines[0:1, :], lines[1:2, :rest]], axis=1)
        allowed = (places <= row_index) & (key_document == document)
        scores = scores.reshape(heads, tokens, -1) * score_scale
        return jnp.where(allowed[None], scores, masked_score).reshape(heads * tokens, -1)

    def weighted(block, weights):
        return product(weights.astype(jnp.bfloat16), joined(block, HEAD_SIZE))

    scores = block_scores(0)
    peak = jnp.max(scores, axis=-1, keepdims=True)
    weights = jnp.exp(scores - peak)
    peaks[...] = peak
    totals[...] = jnp.sum(weights, axis=-1, keepdims=True)
    summed[...] = weighted(0, weights)
    for block in range(1, blocks):

        @pl.when((place_outer ^ block) < place_outer)
        def _():
            scores = block_scores(block)
            before = peaks[...]
            peak = jnp.maximum(before, jnp.max(scores, axis=-1, keepdims=True))
            weights = jnp.exp(scores - peak)
            shrink = jnp.exp(before - peak)
            peaks[...] = peak
            totals[...] = totals[...] * shrink + jnp.sum(weights, axis=-1, keepdims=True)
            summed[...] = summed[...] * shrink + weighted(block, weights)

    result = (summed[...] / totals[...]).astype(jnp.bfloat16)
    for head in range(heads):
        first = head * tokens
        columns = slice(head * HEAD_SIZE, (head + 1) * HEAD_SIZE)
        here[:, columns] = result[first : first + rows]
        gone[:, columns] = result[first + rows : first + tokens]


def short_body(hidden_in, norm_gain, w_query, w_key, value_weight, w_out, doc_ids, positions):
    place_outer = lax.axis_index("outer")
    place_inner = lax.axis_index("inner")
    place_tensor = lax.axis_index("tensor")
    outer_count = lax.axis_size("outer")
    rows, width = hidden_in.shape
    half_width = w_query.shape[0]
    query_half = w_query.shape[1] // 2
    slot_rows = 2 * rows
    early_rows = 3 * slot_rows
    bf16 = jnp.bfloat16
    across_inner = swap_pairs(2, 1)
    which = place_inner.reshape(1)
    places = jnp.stack([place_outer, place_inner, place_tensor])
    hidden_in, which, places = lax.optimization_barrier((hidden_in, which, places))

    def send(value, axis, pairs):
        return lax.ppermute(value, axis, pairs)

    def send_across(value, pairs):
        both = [(a * 4 + b, (1 - a) * 4 + c) for a in range(2) for b, c in pairs]
        return lax.ppermute(value, ("inner", "tensor"), both)

    half = ((rows, half_width), bf16, None)
    mine, others = call_kernel(
        norm_kernel, "norm", which, [hidden_in, norm_gain.reshape(1, width)], [None] * 2, [half] * 2
    )
    two, one, middle = swap_pairs(4, 2), swap_pairs(4, 1), [(1, 2), (2, 1)]
    two_mine = send(mine, "tensor", two)
    two_theirs = send_across(others, two)
    one_mine = send(mine, "tensor", one)
    one_theirs = send_across(others, one)
    theirs = send(others, "inner", across_inner)
    early = [[mine], [theirs], [one_mine], [one_theirs], [two_mine], [two_theirs]]

    facts = jnp.stack([doc_ids, positions])
    facts_there = send(after(facts, two_theirs), "inner", across_inner)
    inverse = jnp.asarray([yarn_inverse(HEAD_SIZE) * 2], dtype=jnp.float32)
    signs = jnp.asarray([-1.0] * (HEAD_SIZE // 2) + [1.0] * (HEAD_SIZE // 2), dtype=jnp.float32)
    attention_gain = 0.1 * math.log(yarn_factor) + 1.0
    angles, documents, document_rows = call_kernel(
        functools.partial(facts_kernel, rows), "facts", places, [facts, facts_there, inverse],
        [None] * 3,
        [
            ((4 * slot_rows, HEAD_SIZE), jnp.float32, None),
            ((4 * slot_rows, 1), jnp.float32, None),
            ((16, 2 * HEAD_SIZE), bf16, None),
        ],
    )
    cosines = jnp.cos(angles) * attention_gain
    sines = jnp.sin(angles) * attention_gain * signs

    def stack(name, chunks, parts):
        flat = [array for chunk in chunks for array in chunk]
        out = lambda count: ((count * slot_rows, half_width), bf16, None)
        return call_kernel(
            functools.partial(stack_kernel, [len(chunk) for chunk in chunks]), name, which, flat,
            [None] * len(flat), [out(count) for count in parts],
        )

    def sent_halves(wholes, kind):
        count = wholes[0].shape[0]
        wides = [whole.shape[1] // 2 for whole in wholes]
        specs = [
            pl.BlockSpec((count, wide), lambda step, which: (0, 1 - which[1])) for wide in wides
        ]
        return call_kernel(
            copy_kernel, "sent", places, wholes, specs, [((count, sum(wides)), kind, None)]
        )[0]

    def project_pair(stacked):
        keys, values = product(stacked, w_key), product(stacked, value_weight)
        return keys, values, send(sent_halves([keys, values], jnp.float32), "inner", across_inner)

    def project_query(stacked):
        queries = product(stacked, w_query)
        return queries, send(sent_halves([queries], bf16), "inner", across_inner)

    def gather_pairs(pair):
        found = [pair]
        for flip in range(1, outer_count):
            found.append(send(pair, "outer", swap_pairs(outer_count, flip)))
        return found

    def rotate_pair(projected, first, extra):
        keys, values, came = projected
        count = came.shape[0]
        half_spec = pl.BlockSpec((count, HEAD_SIZE), lambda step, which: (0, which[0]))
        table_spec = pl.BlockSpec((count, HEAD_SIZE), lambda step, which: (first // count, 0))
        out_rows = count + sum(array.shape[0] for array in extra)
        return call_kernel(
            functools.partial(pair_kernel, rows), "pair", which,
            [keys, values, came, cosines, sines] + extra,
            [half_spec, half_spec, None, table_spec, table_spec] + [None] * len(extra),
            [((out_rows, 2 * HEAD_SIZE), bf16, None)],
        )[0]

    early_stacked, own_rows, two_rows = stack("early_rows", early, (3, 1, 1))
    middle_rows = send(own_rows, "tensor", middle)
    ends_rows = send(two_rows, "tensor", [(1, 0), (2, 3)])
    early_projected = project_pair(early_stacked)
    early_queries, early_came = project_query(early_stacked)
    late_stacked = stack("late_rows", [[ends_rows, middle_rows]], (1,))[0]
    late_projected = project_pair(late_stacked)
    late_queries, late_came = project_query(late_stacked)
    early_pairs = gather_pairs(rotate_pair(early_projected, 0, [document_rows]))
    late_pairs = gather_pairs(rotate_pair(late_projected, early_rows, []))

    def attend(slot, *wait):
        queries, came = (late_queries, late_came) if slot == 3 else (early_queries, early_came)
        block = slot % 3
        if wait:
            came = after(came, *wait)
        rows_spec = lambda wide, block: pl.BlockSpec((slot_rows, wide), lambda step, which: (block, 0))
        half_spec = pl.BlockSpec((slot_rows, query_half), lambda step, which: (block, which[1]))
        stacked = query_half // HEAD_SIZE * slot_rows
        return call_kernel(
            functools.partial(attention_kernel, slot, outer_count, rows), "attention", places,
            [queries, came, cosines, sines, documents] + early_pairs + late_pairs,
            [
                half_spec, rows_spec(query_half, block),
                rows_spec(HEAD_SIZE, slot), rows_spec(HEAD_SIZE, slot), rows_spec(1, slot),
            ] + [None] * (2 * outer_count),
            [((rows, query_half), bf16, None)] * 2,
            scratch=[
                pltpu.VMEM((stacked, 1), jnp.float32),
                pltpu.VMEM((stacked, 1), jnp.float32),
                pltpu.VMEM((stacked, HEAD_SIZE), jnp.float32),
            ],
        )

    def joined(slot, *wait):
        here, gone = attend(slot, *wait)
        came = send(gone, "inner", across_inner)
        return call_kernel(
            join_kernel, "join", places, [here, came], [None] * 2,
            [((rows, 2 * query_half), bf16, None)],
        )[0]

    rows_3 = joined(3)
    rows_2 = joined(2)
    term_3 = product(rows_3, w_out).astype(bf16)
    came_3 = send(term_3, "tensor", swap_pairs(4, 3))
    came_2 = send(product(rows_2, w_out).astype(bf16), "tensor", two)
    rows_1 = joined(1, term_3)
    came_1 = send(product(rows_1, w_out).astype(bf16), "tensor", one)
    rows_0 = joined(0, term_3)
    total = lax.optimization_barrier(product(rows_0, w_out))
    total = total + hidden_in.astype(jnp.float32) + came_1.astype(jnp.float32)
    total = total + came_2.astype(jnp.float32) + came_3.astype(jnp.float32)
    return total.astype(bf16)


def solution(mesh):
    in_specs = (
        P(("outer", "inner", "tensor"), None),
        P(),
        P("inner", "tensor"),
        P("inner", "tensor"),
        P("inner", "tensor"),
        P("tensor", None),
        P(("outer", "inner")),
        P(("outer", "inner")),
    )
    out_specs = P(("outer", "inner", "tensor"), None)

    def chosen(*arrays):
        outer_count = mesh.shape["outer"]
        key_heads = arrays[3].shape[1] // HEAD_SIZE // mesh.shape["tensor"]
        short = (
            mesh.shape["tensor"] == 4
            and mesh.shape["inner"] == 2
            and key_heads == 2
            and outer_count & (outer_count - 1) == 0
            and arrays[0].shape[0] % (mesh.size * 16) == 0
            and arrays[0].shape[0] // outer_count <= 512
        )
        mapped = jax.shard_map(
            short_body if short else body,
            mesh=mesh, in_specs=in_specs, out_specs=out_specs, check_vma=False,
        )
        return mapped(*arrays)

    return chosen
```

```python
import functools
import math

import jax
import jax.numpy as jnp
from jax import lax
from jax.experimental import pallas as pl
from jax.experimental.pallas import tpu as pltpu
from jax.sharding import PartitionSpec as P

HEAD_SIZE = 128


rope_base = 500000.0
yarn_factor = 8.0
trained_context = 8192.0
beta_fast = 32.0
beta_slow = 1.0
norm_epsilon = 1e-05
masked_score = -1e30


def yarn_inverse(head_dim):
    half_dim = head_dim // 2

    def correction(rotations):
        return (
            head_dim
            * math.log(trained_context / (rotations * 2.0 * math.pi))
            / (2.0 * math.log(rope_base))
        )

    lowest = max(math.floor(correction(beta_fast)), 0)
    highest = min(math.ceil(correction(beta_slow)), head_dim - 1)
    spread = max(highest - lowest, 0.001)
    values = []
    for column in range(half_dim):
        extrapolated = rope_base ** (-2.0 * column / head_dim)
        ramp = min(max((column - lowest) / spread, 0.0), 1.0)
        values.append(extrapolated / yarn_factor * ramp + extrapolated * (1.0 - ramp))
    return values


def yarn_tables(positions, head_dim):
    inverse = jnp.asarray(yarn_inverse(head_dim), dtype=jnp.float32)
    attention_gain = 0.1 * math.log(yarn_factor) + 1.0
    angles = positions.astype(jnp.float32)[:, None] * inverse[None, :]
    return (jnp.cos(angles) * attention_gain, jnp.sin(angles) * attention_gain)


def apply_rotation(heads, cosine_table, sine_table):
    half_dim = heads.shape[-1] // 2
    first_half = heads[..., :half_dim]
    second_half = heads[..., half_dim:]
    cos_rows = cosine_table[:, None, :]
    sin_rows = sine_table[:, None, :]
    return jnp.concatenate(
        [
            first_half * cos_rows - second_half * sin_rows,
            second_half * cos_rows + first_half * sin_rows,
        ],
        axis=-1,
    )


def rms_normed(hidden_in, norm_gain):
    widened = hidden_in.astype(jnp.float32)
    power = jnp.mean(widened * widened, axis=-1, keepdims=True)
    return (widened * lax.rsqrt(power + norm_epsilon) * norm_gain).astype(jnp.bfloat16)


def body(hidden_in, norm_gain, w_query, w_key, value_weight, w_out, doc_ids, positions):
    normed = rms_normed(hidden_in, norm_gain)
    block_rows = lax.all_gather(normed, "tensor", axis=0, tiled=True)
    tokens_here = block_rows.shape[0]
    query_width = w_query.shape[1]
    key_width = w_key.shape[1]
    inner_count = lax.axis_size("inner")
    slice_width = w_query.shape[0]
    arranged = block_rows.reshape(tokens_here, inner_count, slice_width)
    received = lax.all_to_all(arranged, "inner", split_axis=1, concat_axis=0, tiled=True)
    received = received.reshape(inner_count * tokens_here, slice_width)
    stacked = jnp.concatenate([w_query, w_key, value_weight], axis=1)
    combined = lax.psum_scatter(
        jnp.dot(received, stacked, preferred_element_type=jnp.float32),
        "inner",
        scatter_dimension=0,
        tiled=True,
    )
    queries = combined[:, :query_width]
    key_matrix = combined[:, query_width : query_width + key_width]
    value_matrix = combined[:, query_width + key_width :]
    value_matrix = value_matrix.astype(jnp.bfloat16)
    heads_query = query_width // HEAD_SIZE
    heads_key = key_width // HEAD_SIZE
    queries_per_group = heads_query // heads_key
    cosine_table, sine_table = yarn_tables(positions, HEAD_SIZE)
    query_rot = (
        apply_rotation(
            queries.reshape(tokens_here, heads_query, HEAD_SIZE), cosine_table, sine_table
        )
        .astype(jnp.bfloat16)
        .reshape(tokens_here, query_width)
    )
    rotated_keys = (
        apply_rotation(
            key_matrix.reshape(tokens_here, heads_key, HEAD_SIZE), cosine_table, sine_table
        )
        .astype(jnp.bfloat16)
        .reshape(tokens_here, key_width)
    )
    documents = lax.all_gather(doc_ids, ("outer", "inner"), axis=0, tiled=True)
    length_all = documents.shape[0]
    block_index = lax.axis_index(("outer", "inner"))
    sequence_index = jnp.arange(length_all, dtype=jnp.int32)
    query_documents = lax.dynamic_slice_in_dim(documents, block_index * tokens_here, tokens_here, 0)
    query_index = lax.dynamic_slice_in_dim(
        sequence_index, block_index * tokens_here, tokens_here, 0
    )
    row_documents = jnp.tile(query_documents, queries_per_group)
    row_index = jnp.tile(query_index, queries_per_group)
    top_index = jnp.max(query_index)
    top_document = jnp.max(query_documents)
    low_document = jnp.min(query_documents)
    grouped_heads = jnp.transpose(
        query_rot.reshape(tokens_here, heads_key, queries_per_group, HEAD_SIZE), (1, 2, 0, 3)
    ).reshape(heads_key, queries_per_group * tokens_here, HEAD_SIZE)
    score_scale = HEAD_SIZE ** (-0.5)

    def key_block(running, block_keys, block_values, first_row):
        row_count = block_keys.shape[0]
        piece_index = lax.dynamic_slice_in_dim(sequence_index, first_row, row_count, 0)
        piece_documents = lax.dynamic_slice_in_dim(documents, first_row, row_count, 0)
        live = (
            (jnp.min(piece_index) <= top_index)
            & (jnp.min(piece_documents) <= top_document)
            & (jnp.max(piece_documents) >= low_document)
        )

        def attend(current):
            row_peaks, totals, summed = current
            heads_keys = block_keys.reshape(row_count, heads_key, HEAD_SIZE)
            heads_values = block_values.reshape(row_count, heads_key, HEAD_SIZE)
            scores = (
                jnp.einsum(
                    "hqd,khd->hqk", grouped_heads, heads_keys, preferred_element_type=jnp.float32
                )
                * score_scale
            )
            allowed = (row_index[:, None] >= piece_index[None, :]) & (
                row_documents[:, None] == piece_documents[None, :]
            )
            scores = jnp.where(allowed[None], scores, masked_score)
            fresh = jnp.maximum(row_peaks, jnp.max(scores, axis=-1))
            weights = jnp.where(allowed[None], jnp.exp(scores - fresh[..., None]), 0.0)
            shrink = jnp.exp(row_peaks - fresh)
            totals = totals * shrink + jnp.sum(weights, axis=-1)
            summed = summed * shrink[..., None] + jnp.einsum(
                "hqk,khd->hqd",
                weights.astype(jnp.bfloat16),
                heads_values,
                preferred_element_type=jnp.float32,
            )
            return (fresh, totals, summed)

        return lax.cond(live, attend, lambda current: current, running)

    initial = (
        jnp.full((heads_key, queries_per_group * tokens_here), masked_score, jnp.float32),
        jnp.zeros((heads_key, queries_per_group * tokens_here), jnp.float32),
        jnp.zeros((heads_key, queries_per_group * tokens_here, HEAD_SIZE), jnp.float32),
    )
    piece_keys = lax.all_gather(rotated_keys, ("outer", "inner"), axis=0, tiled=True)
    piece_values = lax.all_gather(value_matrix, ("outer", "inner"), axis=0, tiled=True)
    row_count = piece_keys.shape[0]
    step_rows = 512
    steps_count = row_count // step_rows
    split_keys = piece_keys.reshape(steps_count, step_rows, key_width)
    split_values = piece_values.reshape(steps_count, step_rows, key_width)
    offsets = jnp.arange(steps_count, dtype=jnp.int32) * step_rows

    def scan_step(current, inputs):
        block_keys, block_values, offset = inputs
        return (key_block(current, block_keys, block_values, offset), None)

    result, unused = lax.scan(scan_step, initial, (split_keys, split_values, offsets))
    row_peaks, totals, summed = result
    heads_out = (summed / totals[..., None]).astype(jnp.bfloat16)
    attended = jnp.transpose(
        heads_out.reshape(heads_key, queries_per_group, tokens_here, HEAD_SIZE), (2, 0, 1, 3)
    ).reshape(tokens_here, query_width)
    full_term = jnp.dot(attended, w_out, preferred_element_type=jnp.float32)
    projected = lax.psum_scatter(
        full_term.astype(jnp.bfloat16), "tensor", scatter_dimension=0, tiled=True
    ).astype(jnp.float32)
    return (hidden_in.astype(jnp.float32) + projected).astype(jnp.bfloat16)


def swap_pairs(axis_size, flip):
    return [(place, place ^ flip) for place in range(axis_size)]


def after(value, *others):
    return lax.optimization_barrier((value,) + others)[0]


def whole_spec(array):
    zeros = (0,) * array.ndim
    return pl.BlockSpec(array.shape, lambda step, which: zeros)


def call_kernel(kernel, name, which, arrays, specs, outs, steps=1, scratch=(), mebibytes=16):
    shapes = [jax.ShapeDtypeStruct(shape, dtype) for shape, dtype, unused in outs]
    out_specs = [
        whole_spec(shape) if spec is None else spec for shape, (a, b, spec) in zip(shapes, outs)
    ]
    found = pl.pallas_call(
        kernel,
        name=name,
        grid_spec=pltpu.PrefetchScalarGridSpec(
            num_scalar_prefetch=1,
            grid=(steps,),
            in_specs=[
                whole_spec(array) if spec is None else spec for array, spec in zip(arrays, specs)
            ],
            out_specs=out_specs,
            scratch_shapes=list(scratch),
        ),
        out_shape=shapes,
        compiler_params=pltpu.CompilerParams(vmem_limit_bytes=mebibytes * 1024 * 1024),
    )(which, *arrays)
    return found


def norm_kernel(which, hidden, gain, mine, others):
    half_width = mine.shape[1]
    widened = hidden[...].astype(jnp.float32)
    power = jnp.mean(widened * widened, axis=-1, keepdims=True)
    normed = (widened * lax.rsqrt(power + norm_epsilon) * gain[...]).astype(jnp.bfloat16)

    @pl.when(which[0] == 0)
    def _():
        mine[...] = normed[:, :half_width]
        others[...] = normed[:, half_width:]

    @pl.when(which[0] != 0)
    def _():
        mine[...] = normed[:, half_width:]
        others[...] = normed[:, :half_width]


def stacked_rows(chunks):
    return jnp.concatenate(
        [
            chunk[...] if len(pair) == 1 else pair[0][...] + pair[1][...]
            for pair in chunks
            for chunk in pair[:1]
        ],
        axis=0,
    )


def split_chunks(refs, widths):
    chunks = []
    place = 0
    for width in widths:
        chunks.append(refs[place : place + width])
        place += width
    return chunks, refs[place:]


def product(left, right):
    return jnp.dot(left, right, preferred_element_type=jnp.float32)


def stack_kernel(widths, which, *refs):
    chunks, outs = split_chunks(refs, widths)
    outs[0][...] = stacked_rows(chunks)
    for place, out in zip((0, outs[0].shape[0] * 2 // 3), outs[1:]):
        out[...] = outs[0][place : place + out.shape[0]]


def other_part(value, rows):
    pieces = [value[place : place + rows] for place in range(0, value.shape[0], rows)]
    return jnp.concatenate([pieces[k ^ 1] for k in range(len(pieces))], axis=0)


def rotated(part, cosine_rows, sine_rows):
    return part * cosine_rows + pltpu.roll(part, HEAD_SIZE // 2, 1) * sine_rows


def pair_kernel(rows, which, keys, values, came, cosines, sines, *refs):
    out = refs[-1]
    count = keys.shape[0]
    added = other_part(came[...], rows).astype(jnp.float32)
    whole = rotated(keys[...] + added[:, :HEAD_SIZE], cosines[...], sines[...])
    out[:count, :HEAD_SIZE] = whole.astype(jnp.bfloat16)
    out[:count, HEAD_SIZE:] = (values[...] + added[:, HEAD_SIZE:]).astype(jnp.bfloat16)
    if len(refs) == 2:
        out[count:, :] = refs[0][...]


def facts_kernel(rows, which, here, there, inverse, angles, documents, document_rows):
    block = here.shape[1]
    line = lax.broadcasted_iota(jnp.int32, (block, 1), 0)
    slots = sum((line >= rows * number).astype(jnp.int32) for number in range(1, 4))
    source = (which[2] ^ slots) * rows + line - rows * slots
    chosen = lax.broadcasted_iota(jnp.int32, (block, block), 1) == source

    def ordered(row):
        parts = [
            jnp.sum(jnp.where(chosen, part[row : row + 1, :].astype(jnp.float32), 0.0), axis=1, keepdims=True)
            for part in (here, there)
        ]
        return jnp.concatenate(
            [part[place : place + rows] for place in range(0, block, rows) for part in parts], axis=0
        )

    angles[...] = ordered(1) * inverse[...]
    column = ordered(0)
    documents[...] = column
    count = column.shape[0]
    same = lax.broadcasted_iota(jnp.int32, (count, count), 0) == lax.broadcasted_iota(
        jnp.int32, (count, count), 1
    )
    wide = document_rows.shape[1]
    across = jnp.sum(jnp.where(same, column, 0.0), axis=0, keepdims=True)
    rest = jnp.concatenate(
        [across[:, wide:], jnp.zeros((1, 2 * wide - count), jnp.float32)], axis=1
    )
    number = lax.broadcasted_iota(jnp.int32, document_rows.shape, 0)
    document_rows[...] = jnp.where(
        number == 0, across[:, :wide], jnp.where(number == 1, rest, 0.0)
    ).astype(jnp.bfloat16)


def copy_kernel(which, *refs):
    *parts, out = refs
    place = 0
    for part in parts:
        out[:, place : place + part.shape[1]] = part[...].astype(out.dtype)
        place += part.shape[1]


def join_kernel(which, here, came, out):
    width = here.shape[1]

    @pl.when(which[1] == 0)
    def _():
        out[:, :width] = here[...]
        out[:, width:] = came[...]

    @pl.when(which[1] != 0)
    def _():
        out[:, :width] = came[...]
        out[:, width:] = here[...]


def attention_kernel(
    slot, blocks, rows, which, kept, came, cosines, sines, query_document, *refs
):
    early, late = refs[:blocks], refs[blocks : 2 * blocks]
    here, gone, peaks, totals, summed = refs[2 * blocks :]
    tokens, width = came.shape
    heads = width // HEAD_SIZE
    score_scale = HEAD_SIZE ** (-0.5)
    block_rows = 4 * rows
    early_rows = 2 * block_rows - late[0].shape[0]
    whole = kept[...] + other_part(came[...], rows).astype(jnp.float32)
    stacked = jnp.concatenate(
        [
            rotated(whole[:, place : place + HEAD_SIZE], cosines[...], sines[...]).astype(
                jnp.bfloat16
            )
            for place in range(0, width, HEAD_SIZE)
        ],
        axis=0,
    )
    place_outer, place_inner, place_tensor = which[0], which[1], which[2]
    document = query_document[...]

    def inside(slot_number, part_number, row_number):
        return (place_inner ^ part_number) * block_rows + (place_tensor ^ slot_number) * rows + row_number

    line = lax.broadcasted_iota(jnp.int32, (tokens, 1), 0)
    second = (line >= rows).astype(jnp.int32)
    row_index = place_outer * 2 * block_rows + inside(slot, second, line - rows * second)
    line = lax.broadcasted_iota(jnp.int32, (1, 2 * block_rows), 1)
    slots = sum((line >= 2 * rows * number).astype(jnp.int32) for number in range(1, 4))
    left = line - 2 * rows * slots
    second = (left >= rows).astype(jnp.int32)
    key_place = inside(slots, second, left - rows * second)

    def joined(block, start):
        stop = start + HEAD_SIZE
        return jnp.concatenate([early[block][:early_rows, start:stop], late[block][:, start:stop]], axis=0)

    def block_scores(block):
        scores = lax.dot_general(
            stacked, joined(block, 0), (((1,), (1,)), ((), ())), preferred_element_type=jnp.float32
        )
        places = (place_outer ^ block) * 2 * block_rows + key_place
        lines = early[block][early_rows:, :].astype(jnp.float32)
        rest = 2 * block_rows - lines.shape[1]
        key_document = jnp.concatenate([lines[0:1, :], lines[1:2, :rest]], axis=1)
        allowed = (places <= row_index) & (key_document == document)
        scores = scores.reshape(heads, tokens, -1) * score_scale
        return jnp.where(allowed[None], scores, masked_score).reshape(heads * tokens, -1)

    def weighted(block, weights):
        return product(weights.astype(jnp.bfloat16), joined(block, HEAD_SIZE))

    scores = block_scores(0)
    peak = jnp.max(scores, axis=-1, keepdims=True)
    weights = jnp.exp(scores - peak)
    peaks[...] = peak
    totals[...] = jnp.sum(weights, axis=-1, keepdims=True)
    summed[...] = weighted(0, weights)
    for block in range(1, blocks):

        @pl.when((place_outer ^ block) < place_outer)
        def _():
            scores = block_scores(block)
            before = peaks[...]
            peak = jnp.maximum(before, jnp.max(scores, axis=-1, keepdims=True))
            weights = jnp.exp(scores - peak)
            shrink = jnp.exp(before - peak)
            peaks[...] = peak
            totals[...] = totals[...] * shrink + jnp.sum(weights, axis=-1, keepdims=True)
            summed[...] = summed[...] * shrink + weighted(block, weights)

    result = (summed[...] / totals[...]).astype(jnp.bfloat16)
    for head in range(heads):
        first = head * tokens
        columns = slice(head * HEAD_SIZE, (head + 1) * HEAD_SIZE)
        here[:, columns] = result[first : first + rows]
        gone[:, columns] = result[first + rows : first + tokens]


def short_body(hidden_in, norm_gain, w_query, w_key, value_weight, w_out, doc_ids, positions):
    place_outer = lax.axis_index("outer")
    place_inner = lax.axis_index("inner")
    place_tensor = lax.axis_index("tensor")
    outer_count = lax.axis_size("outer")
    rows, width = hidden_in.shape
    half_width = w_query.shape[0]
    query_half = w_query.shape[1] // 2
    slot_rows = 2 * rows
    early_rows = 3 * slot_rows
    bf16 = jnp.bfloat16
    across_inner = swap_pairs(2, 1)
    which = place_inner.reshape(1)
    places = jnp.stack([place_outer, place_inner, place_tensor])
    hidden_in, which, places = lax.optimization_barrier((hidden_in, which, places))

    def send(value, axis, pairs):
        return lax.ppermute(value, axis, pairs)

    def send_across(value, pairs):
        both = [(a * 4 + b, (1 - a) * 4 + c) for a in range(2) for b, c in pairs]
        return lax.ppermute(value, ("inner", "tensor"), both)

    half = ((rows, half_width), bf16, None)
    mine, others = call_kernel(
        norm_kernel, "norm", which, [hidden_in, norm_gain.reshape(1, width)], [None] * 2, [half] * 2
    )
    two, one, middle = swap_pairs(4, 2), swap_pairs(4, 1), [(1, 2), (2, 1)]
    two_mine = send(mine, "tensor", two)
    two_theirs = send_across(others, two)
    one_mine = send(mine, "tensor", one)
    one_theirs = send_across(others, one)
    theirs = send(others, "inner", across_inner)
    early = [[mine], [theirs], [one_mine], [one_theirs], [two_mine], [two_theirs]]

    facts = jnp.stack([doc_ids, positions])
    facts_there = send(after(facts, two_theirs), "inner", across_inner)
    inverse = jnp.asarray([yarn_inverse(HEAD_SIZE) * 2], dtype=jnp.float32)
    signs = jnp.asarray([-1.0] * (HEAD_SIZE // 2) + [1.0] * (HEAD_SIZE // 2), dtype=jnp.float32)
    attention_gain = 0.1 * math.log(yarn_factor) + 1.0
    angles, documents, document_rows = call_kernel(
        functools.partial(facts_kernel, rows), "facts", places, [facts, facts_there, inverse],
        [None] * 3,
        [
            ((4 * slot_rows, HEAD_SIZE), jnp.float32, None),
            ((4 * slot_rows, 1), jnp.float32, None),
            ((16, 2 * HEAD_SIZE), bf16, None),
        ],
    )
    cosines = jnp.cos(angles) * attention_gain
    sines = jnp.sin(angles) * attention_gain * signs

    def stack(name, chunks, parts):
        flat = [array for chunk in chunks for array in chunk]
        out = lambda count: ((count * slot_rows, half_width), bf16, None)
        return call_kernel(
            functools.partial(stack_kernel, [len(chunk) for chunk in chunks]), name, which, flat,
            [None] * len(flat), [out(count) for count in parts],
        )

    def sent_halves(wholes, kind):
        count = wholes[0].shape[0]
        wides = [whole.shape[1] // 2 for whole in wholes]
        specs = [
            pl.BlockSpec((count, wide), lambda step, which: (0, 1 - which[1])) for wide in wides
        ]
        return call_kernel(
            copy_kernel, "sent", places, wholes, specs, [((count, sum(wides)), kind, None)]
        )[0]

    def project_pair(stacked):
        keys, values = product(stacked, w_key), product(stacked, value_weight)
        return keys, values, send(sent_halves([keys, values], jnp.float32), "inner", across_inner)

    def project_query(stacked):
        queries = product(stacked, w_query)
        return queries, send(sent_halves([queries], bf16), "inner", across_inner)

    def gather_pairs(pair):
        found = [pair]
        for flip in range(1, outer_count):
            found.append(send(pair, "outer", swap_pairs(outer_count, flip)))
        return found

    def gather_by_steps(pair):
        found = {0: pair}
        bit = outer_count // 2
        while bit:
            for flip in list(found):
                found[flip | bit] = send(found[flip], "outer", swap_pairs(outer_count, bit))
            bit //= 2
        return [found[flip] for flip in range(outer_count)]

    def rotate_pair(projected, first, extra):
        keys, values, came = projected
        count = came.shape[0]
        half_spec = pl.BlockSpec((count, HEAD_SIZE), lambda step, which: (0, which[0]))
        table_spec = pl.BlockSpec((count, HEAD_SIZE), lambda step, which: (first // count, 0))
        out_rows = count + sum(array.shape[0] for array in extra)
        return call_kernel(
            functools.partial(pair_kernel, rows), "pair", which,
            [keys, values, came, cosines, sines] + extra,
            [half_spec, half_spec, None, table_spec, table_spec] + [None] * len(extra),
            [((out_rows, 2 * HEAD_SIZE), bf16, None)],
        )[0]

    early_stacked, own_rows, two_rows = stack("early_rows", early, (3, 1, 1))
    middle_rows = send(own_rows, "tensor", middle)
    ends_rows = send(two_rows, "tensor", [(1, 0), (2, 3)])
    early_projected = project_pair(early_stacked)
    early_queries, early_came = project_query(early_stacked)
    late_stacked = stack("late_rows", [[ends_rows, middle_rows]], (1,))[0]
    late_projected = project_pair(late_stacked)
    late_queries, late_came = project_query(late_stacked)
    early_pairs = gather_by_steps(rotate_pair(early_projected, 0, [document_rows]))
    late_pairs = gather_pairs(rotate_pair(late_projected, early_rows, []))

    def attend(slot, *wait):
        queries, came = (late_queries, late_came) if slot == 3 else (early_queries, early_came)
        block = slot % 3
        if wait:
            came = after(came, *wait)
        rows_spec = lambda wide, block: pl.BlockSpec((slot_rows, wide), lambda step, which: (block, 0))
        half_spec = pl.BlockSpec((slot_rows, query_half), lambda step, which: (block, which[1]))
        stacked = query_half // HEAD_SIZE * slot_rows
        return call_kernel(
            functools.partial(attention_kernel, slot, outer_count, rows), "attention", places,
            [queries, came, cosines, sines, documents] + early_pairs + late_pairs,
            [
                half_spec, rows_spec(query_half, block),
                rows_spec(HEAD_SIZE, slot), rows_spec(HEAD_SIZE, slot), rows_spec(1, slot),
            ] + [None] * (2 * outer_count),
            [((rows, query_half), bf16, None)] * 2,
            scratch=[
                pltpu.VMEM((stacked, 1), jnp.float32),
                pltpu.VMEM((stacked, 1), jnp.float32),
                pltpu.VMEM((stacked, HEAD_SIZE), jnp.float32),
            ],
        )

    def joined(slot, *wait):
        here, gone = attend(slot, *wait)
        came = send(gone, "inner", across_inner)
        return call_kernel(
            join_kernel, "join", places, [here, came], [None] * 2,
            [((rows, 2 * query_half), bf16, None)],
        )[0]

    rows_3 = joined(3)
    rows_2 = joined(2)
    term_3 = product(rows_3, w_out).astype(bf16)
    came_3 = send(term_3, "tensor", swap_pairs(4, 3))
    came_2 = send(product(rows_2, w_out).astype(bf16), "tensor", two)
    rows_1 = joined(1, term_3)
    came_1 = send(product(rows_1, w_out).astype(bf16), "tensor", one)
    rows_0 = joined(0, term_3)
    total = lax.optimization_barrier(product(rows_0, w_out))
    total = total + hidden_in.astype(jnp.float32) + came_1.astype(jnp.float32)
    total = total + came_2.astype(jnp.float32) + came_3.astype(jnp.float32)
    return total.astype(bf16)


def solution(mesh):
    in_specs = (
        P(("outer", "inner", "tensor"), None),
        P(),
        P("inner", "tensor"),
        P("inner", "tensor"),
        P("inner", "tensor"),
        P("tensor", None),
        P(("outer", "inner")),
        P(("outer", "inner")),
    )
    out_specs = P(("outer", "inner", "tensor"), None)

    def chosen(*arrays):
        outer_count = mesh.shape["outer"]
        key_heads = arrays[3].shape[1] // HEAD_SIZE // mesh.shape["tensor"]
        short = (
            mesh.shape["tensor"] == 4
            and mesh.shape["inner"] == 2
            and key_heads == 2
            and outer_count & (outer_count - 1) == 0
            and arrays[0].shape[0] % (mesh.size * 16) == 0
            and arrays[0].shape[0] // outer_count <= 512
        )
        mapped = jax.shard_map(
            short_body if short else body,
            mesh=mesh, in_specs=in_specs, out_specs=out_specs, check_vma=False,
        )
        return mapped(*arrays)

    return chosen
```

```python
import functools
import math

import jax
import jax.numpy as jnp
from jax import lax
from jax.experimental import pallas as pl
from jax.experimental.pallas import tpu as pltpu
from jax.sharding import PartitionSpec as P

HEAD_SIZE = 128


rope_base = 500000.0
yarn_factor = 8.0
trained_context = 8192.0
beta_fast = 32.0
beta_slow = 1.0
norm_epsilon = 1e-05
masked_score = -1e30


def yarn_inverse(head_dim):
    half_dim = head_dim // 2

    def correction(rotations):
        return (
            head_dim
            * math.log(trained_context / (rotations * 2.0 * math.pi))
            / (2.0 * math.log(rope_base))
        )

    lowest = max(math.floor(correction(beta_fast)), 0)
    highest = min(math.ceil(correction(beta_slow)), head_dim - 1)
    spread = max(highest - lowest, 0.001)
    values = []
    for column in range(half_dim):
        extrapolated = rope_base ** (-2.0 * column / head_dim)
        ramp = min(max((column - lowest) / spread, 0.0), 1.0)
        values.append(extrapolated / yarn_factor * ramp + extrapolated * (1.0 - ramp))
    return values


def yarn_tables(positions, head_dim):
    inverse = jnp.asarray(yarn_inverse(head_dim), dtype=jnp.float32)
    attention_gain = 0.1 * math.log(yarn_factor) + 1.0
    angles = positions.astype(jnp.float32)[:, None] * inverse[None, :]
    return (jnp.cos(angles) * attention_gain, jnp.sin(angles) * attention_gain)


def apply_rotation(heads, cosine_table, sine_table):
    half_dim = heads.shape[-1] // 2
    first_half = heads[..., :half_dim]
    second_half = heads[..., half_dim:]
    cos_rows = cosine_table[:, None, :]
    sin_rows = sine_table[:, None, :]
    return jnp.concatenate(
        [
            first_half * cos_rows - second_half * sin_rows,
            second_half * cos_rows + first_half * sin_rows,
        ],
        axis=-1,
    )


def rms_normed(hidden_in, norm_gain):
    widened = hidden_in.astype(jnp.float32)
    power = jnp.mean(widened * widened, axis=-1, keepdims=True)
    return (widened * lax.rsqrt(power + norm_epsilon) * norm_gain).astype(jnp.bfloat16)


def body(hidden_in, norm_gain, w_query, w_key, value_weight, w_out, doc_ids, positions):
    normed = rms_normed(hidden_in, norm_gain)
    block_rows = lax.all_gather(normed, "tensor", axis=0, tiled=True)
    tokens_here = block_rows.shape[0]
    query_width = w_query.shape[1]
    key_width = w_key.shape[1]
    inner_count = lax.axis_size("inner")
    slice_width = w_query.shape[0]
    arranged = block_rows.reshape(tokens_here, inner_count, slice_width)
    received = lax.all_to_all(arranged, "inner", split_axis=1, concat_axis=0, tiled=True)
    received = received.reshape(inner_count * tokens_here, slice_width)
    stacked = jnp.concatenate([w_query, w_key, value_weight], axis=1)
    combined = lax.psum_scatter(
        jnp.dot(received, stacked, preferred_element_type=jnp.float32),
        "inner",
        scatter_dimension=0,
        tiled=True,
    )
    queries = combined[:, :query_width]
    key_matrix = combined[:, query_width : query_width + key_width]
    value_matrix = combined[:, query_width + key_width :]
    value_matrix = value_matrix.astype(jnp.bfloat16)
    heads_query = query_width // HEAD_SIZE
    heads_key = key_width // HEAD_SIZE
    queries_per_group = heads_query // heads_key
    cosine_table, sine_table = yarn_tables(positions, HEAD_SIZE)
    query_rot = (
        apply_rotation(
            queries.reshape(tokens_here, heads_query, HEAD_SIZE), cosine_table, sine_table
        )
        .astype(jnp.bfloat16)
        .reshape(tokens_here, query_width)
    )
    rotated_keys = (
        apply_rotation(
            key_matrix.reshape(tokens_here, heads_key, HEAD_SIZE), cosine_table, sine_table
        )
        .astype(jnp.bfloat16)
        .reshape(tokens_here, key_width)
    )
    documents = lax.all_gather(doc_ids, ("outer", "inner"), axis=0, tiled=True)
    length_all = documents.shape[0]
    block_index = lax.axis_index(("outer", "inner"))
    sequence_index = jnp.arange(length_all, dtype=jnp.int32)
    query_documents = lax.dynamic_slice_in_dim(documents, block_index * tokens_here, tokens_here, 0)
    query_index = lax.dynamic_slice_in_dim(
        sequence_index, block_index * tokens_here, tokens_here, 0
    )
    row_documents = jnp.tile(query_documents, queries_per_group)
    row_index = jnp.tile(query_index, queries_per_group)
    top_index = jnp.max(query_index)
    top_document = jnp.max(query_documents)
    low_document = jnp.min(query_documents)
    grouped_heads = jnp.transpose(
        query_rot.reshape(tokens_here, heads_key, queries_per_group, HEAD_SIZE), (1, 2, 0, 3)
    ).reshape(heads_key, queries_per_group * tokens_here, HEAD_SIZE)
    score_scale = HEAD_SIZE ** (-0.5)

    def key_block(running, block_keys, block_values, first_row):
        row_count = block_keys.shape[0]
        piece_index = lax.dynamic_slice_in_dim(sequence_index, first_row, row_count, 0)
        piece_documents = lax.dynamic_slice_in_dim(documents, first_row, row_count, 0)
        live = (
            (jnp.min(piece_index) <= top_index)
            & (jnp.min(piece_documents) <= top_document)
            & (jnp.max(piece_documents) >= low_document)
        )

        def attend(current):
            row_peaks, totals, summed = current
            heads_keys = block_keys.reshape(row_count, heads_key, HEAD_SIZE)
            heads_values = block_values.reshape(row_count, heads_key, HEAD_SIZE)
            scores = (
                jnp.einsum(
                    "hqd,khd->hqk", grouped_heads, heads_keys, preferred_element_type=jnp.float32
                )
                * score_scale
            )
            allowed = (row_index[:, None] >= piece_index[None, :]) & (
                row_documents[:, None] == piece_documents[None, :]
            )
            scores = jnp.where(allowed[None], scores, masked_score)
            fresh = jnp.maximum(row_peaks, jnp.max(scores, axis=-1))
            weights = jnp.where(allowed[None], jnp.exp(scores - fresh[..., None]), 0.0)
            shrink = jnp.exp(row_peaks - fresh)
            totals = totals * shrink + jnp.sum(weights, axis=-1)
            summed = summed * shrink[..., None] + jnp.einsum(
                "hqk,khd->hqd",
                weights.astype(jnp.bfloat16),
                heads_values,
                preferred_element_type=jnp.float32,
            )
            return (fresh, totals, summed)

        return lax.cond(live, attend, lambda current: current, running)

    initial = (
        jnp.full((heads_key, queries_per_group * tokens_here), masked_score, jnp.float32),
        jnp.zeros((heads_key, queries_per_group * tokens_here), jnp.float32),
        jnp.zeros((heads_key, queries_per_group * tokens_here, HEAD_SIZE), jnp.float32),
    )
    piece_keys = lax.all_gather(rotated_keys, ("outer", "inner"), axis=0, tiled=True)
    piece_values = lax.all_gather(value_matrix, ("outer", "inner"), axis=0, tiled=True)
    row_count = piece_keys.shape[0]
    step_rows = 512
    steps_count = row_count // step_rows
    split_keys = piece_keys.reshape(steps_count, step_rows, key_width)
    split_values = piece_values.reshape(steps_count, step_rows, key_width)
    offsets = jnp.arange(steps_count, dtype=jnp.int32) * step_rows

    def scan_step(current, inputs):
        block_keys, block_values, offset = inputs
        return (key_block(current, block_keys, block_values, offset), None)

    result, unused = lax.scan(scan_step, initial, (split_keys, split_values, offsets))
    row_peaks, totals, summed = result
    heads_out = (summed / totals[..., None]).astype(jnp.bfloat16)
    attended = jnp.transpose(
        heads_out.reshape(heads_key, queries_per_group, tokens_here, HEAD_SIZE), (2, 0, 1, 3)
    ).reshape(tokens_here, query_width)
    full_term = jnp.dot(attended, w_out, preferred_element_type=jnp.float32)
    projected = lax.psum_scatter(
        full_term.astype(jnp.bfloat16), "tensor", scatter_dimension=0, tiled=True
    ).astype(jnp.float32)
    return (hidden_in.astype(jnp.float32) + projected).astype(jnp.bfloat16)


def swap_pairs(axis_size, flip):
    return [(place, place ^ flip) for place in range(axis_size)]


def after(value, *others):
    return lax.optimization_barrier((value,) + others)[0]


def whole_spec(array):
    zeros = (0,) * array.ndim
    return pl.BlockSpec(array.shape, lambda step, which: zeros)


def call_kernel(kernel, name, which, arrays, specs, outs, steps=1, scratch=(), mebibytes=16):
    shapes = [jax.ShapeDtypeStruct(shape, dtype) for shape, dtype, unused in outs]
    out_specs = [
        whole_spec(shape) if spec is None else spec for shape, (a, b, spec) in zip(shapes, outs)
    ]
    found = pl.pallas_call(
        kernel,
        name=name,
        grid_spec=pltpu.PrefetchScalarGridSpec(
            num_scalar_prefetch=1,
            grid=(steps,),
            in_specs=[
                whole_spec(array) if spec is None else spec for array, spec in zip(arrays, specs)
            ],
            out_specs=out_specs,
            scratch_shapes=list(scratch),
        ),
        out_shape=shapes,
        compiler_params=pltpu.CompilerParams(vmem_limit_bytes=mebibytes * 1024 * 1024),
    )(which, *arrays)
    return found


def norm_kernel(which, hidden, gain, mine, others):
    half_width = mine.shape[1]
    widened = hidden[...].astype(jnp.float32)
    power = jnp.mean(widened * widened, axis=-1, keepdims=True)
    normed = (widened * lax.rsqrt(power + norm_epsilon) * gain[...]).astype(jnp.bfloat16)

    @pl.when(which[0] == 0)
    def _():
        mine[...] = normed[:, :half_width]
        others[...] = normed[:, half_width:]

    @pl.when(which[0] != 0)
    def _():
        mine[...] = normed[:, half_width:]
        others[...] = normed[:, :half_width]


def stacked_rows(chunks):
    return jnp.concatenate(
        [
            chunk[...] if len(pair) == 1 else pair[0][...] + pair[1][...]
            for pair in chunks
            for chunk in pair[:1]
        ],
        axis=0,
    )


def split_chunks(refs, widths):
    chunks = []
    place = 0
    for width in widths:
        chunks.append(refs[place : place + width])
        place += width
    return chunks, refs[place:]


def product(left, right):
    return jnp.dot(left, right, preferred_element_type=jnp.float32)


def stack_kernel(widths, which, *refs):
    chunks, outs = split_chunks(refs, widths)
    outs[0][...] = stacked_rows(chunks)
    for place, out in zip((0, outs[0].shape[0] * 2 // 3), outs[1:]):
        out[...] = outs[0][place : place + out.shape[0]]


def other_part(value, rows):
    pieces = [value[place : place + rows] for place in range(0, value.shape[0], rows)]
    return jnp.concatenate([pieces[k ^ 1] for k in range(len(pieces))], axis=0)


def rotated(part, cosine_rows, sine_rows):
    return part * cosine_rows + pltpu.roll(part, HEAD_SIZE // 2, 1) * sine_rows


def pair_kernel(rows, which, keys, values, came, cosines, sines, *refs):
    out = refs[-1]
    count = keys.shape[0]
    added = other_part(came[...], rows).astype(jnp.float32)
    whole = rotated(keys[...] + added[:, :HEAD_SIZE], cosines[...], sines[...])
    out[:count, :HEAD_SIZE] = whole.astype(jnp.bfloat16)
    out[:count, HEAD_SIZE:] = (values[...] + added[:, HEAD_SIZE:]).astype(jnp.bfloat16)
    if len(refs) == 2:
        out[count:, :] = refs[0][...]


def facts_kernel(rows, which, here, there, inverse, angles, documents, document_rows):
    block = here.shape[1]
    line = lax.broadcasted_iota(jnp.int32, (block, 1), 0)
    slots = sum((line >= rows * number).astype(jnp.int32) for number in range(1, 4))
    source = (which[2] ^ slots) * rows + line - rows * slots
    chosen = lax.broadcasted_iota(jnp.int32, (block, block), 1) == source

    def ordered(row):
        parts = [
            jnp.sum(jnp.where(chosen, part[row : row + 1, :].astype(jnp.float32), 0.0), axis=1, keepdims=True)
            for part in (here, there)
        ]
        return jnp.concatenate(
            [part[place : place + rows] for place in range(0, block, rows) for part in parts], axis=0
        )

    angles[...] = ordered(1) * inverse[...]
    column = ordered(0)
    documents[...] = column
    count = column.shape[0]
    same = lax.broadcasted_iota(jnp.int32, (count, count), 0) == lax.broadcasted_iota(
        jnp.int32, (count, count), 1
    )
    wide = document_rows.shape[1]
    across = jnp.sum(jnp.where(same, column, 0.0), axis=0, keepdims=True)
    rest = jnp.concatenate(
        [across[:, wide:], jnp.zeros((1, 2 * wide - count), jnp.float32)], axis=1
    )
    number = lax.broadcasted_iota(jnp.int32, document_rows.shape, 0)
    document_rows[...] = jnp.where(
        number == 0, across[:, :wide], jnp.where(number == 1, rest, 0.0)
    ).astype(jnp.bfloat16)


def copy_kernel(which, *refs):
    *parts, out = refs
    place = 0
    for part in parts:
        out[:, place : place + part.shape[1]] = part[...].astype(out.dtype)
        place += part.shape[1]


def join_kernel(which, here, came, out):
    width = here.shape[1]

    @pl.when(which[1] == 0)
    def _():
        out[:, :width] = here[...]
        out[:, width:] = came[...]

    @pl.when(which[1] != 0)
    def _():
        out[:, :width] = came[...]
        out[:, width:] = here[...]


def attention_kernel(
    slot, blocks, rows, which, kept, came, cosines, sines, query_document, *refs
):
    early, late = refs[:blocks], refs[blocks : 2 * blocks]
    here, gone, peaks, totals, summed = refs[2 * blocks :]
    tokens, width = came.shape
    heads = width // HEAD_SIZE
    score_scale = HEAD_SIZE ** (-0.5) / math.log(2.0)
    block_rows = 4 * rows
    early_rows = 2 * block_rows - late[0].shape[0]
    whole = kept[...] + other_part(came[...], rows).astype(jnp.float32)
    stacked = jnp.concatenate(
        [
            rotated(whole[:, place : place + HEAD_SIZE], cosines[...], sines[...]).astype(
                jnp.bfloat16
            )
            for place in range(0, width, HEAD_SIZE)
        ],
        axis=0,
    )
    place_outer, place_inner, place_tensor = which[0], which[1], which[2]
    document = query_document[...]

    def inside(slot_number, part_number, row_number):
        return (place_inner ^ part_number) * block_rows + (place_tensor ^ slot_number) * rows + row_number

    line = lax.broadcasted_iota(jnp.int32, (tokens, 1), 0)
    second = (line >= rows).astype(jnp.int32)
    row_place = inside(slot, second, line - rows * second)
    line = lax.broadcasted_iota(jnp.int32, (1, 2 * block_rows), 1)
    slots = sum((line >= 2 * rows * number).astype(jnp.int32) for number in range(1, 4))
    left = line - 2 * rows * slots
    second = (left >= rows).astype(jnp.int32)
    key_place = inside(slots, second, left - rows * second)

    def joined(block, start):
        stop = start + HEAD_SIZE
        return jnp.concatenate([early[block][:early_rows, start:stop], late[block][:, start:stop]], axis=0)

    def key_document(block):
        lines = early[block][early_rows:, :].astype(jnp.float32)
        rest = 2 * block_rows - lines.shape[1]
        return jnp.concatenate([lines[0:1, :], lines[1:2, :rest]], axis=1)

    def block_scores(block):
        scores = lax.dot_general(
            stacked, joined(block, 0), (((1,), (1,)), ((), ())), preferred_element_type=jnp.float32
        )
        allowed = key_document(block) == document
        if block == 0:
            allowed = allowed & (key_place <= row_place)
        scores = scores.reshape(heads, tokens, -1) * score_scale
        return jnp.where(allowed[None], scores, masked_score).reshape(heads * tokens, -1)

    def weighted(block, weights):
        return product(weights.astype(jnp.bfloat16), joined(block, HEAD_SIZE))

    scores = block_scores(0)
    peak = jnp.max(scores, axis=-1, keepdims=True)
    weights = jnp.exp2(scores - peak)
    peaks[...] = peak
    totals[...] = jnp.sum(weights, axis=-1, keepdims=True)
    summed[...] = weighted(0, weights)
    lowest = jnp.min(document)
    for block in range(1, blocks):

        @pl.when(((place_outer ^ block) < place_outer) & (jnp.max(key_document(block)) >= lowest))
        def _():
            scores = block_scores(block)
            before = peaks[...]
            peak = jnp.maximum(before, jnp.max(scores, axis=-1, keepdims=True))
            weights = jnp.exp2(scores - peak)
            shrink = jnp.exp2(before - peak)
            peaks[...] = peak
            totals[...] = totals[...] * shrink + jnp.sum(weights, axis=-1, keepdims=True)
            summed[...] = summed[...] * shrink + weighted(block, weights)

    result = (summed[...] / totals[...]).astype(jnp.bfloat16)
    for head in range(heads):
        first = head * tokens
        columns = slice(head * HEAD_SIZE, (head + 1) * HEAD_SIZE)
        here[:, columns] = result[first : first + rows]
        gone[:, columns] = result[first + rows : first + tokens]


def short_body(hidden_in, norm_gain, w_query, w_key, value_weight, w_out, doc_ids, positions):
    place_outer = lax.axis_index("outer")
    place_inner = lax.axis_index("inner")
    place_tensor = lax.axis_index("tensor")
    outer_count = lax.axis_size("outer")
    rows, width = hidden_in.shape
    half_width = w_query.shape[0]
    query_half = w_query.shape[1] // 2
    slot_rows = 2 * rows
    early_rows = 3 * slot_rows
    bf16 = jnp.bfloat16
    across_inner = swap_pairs(2, 1)
    which = place_inner.reshape(1)
    places = jnp.stack([place_outer, place_inner, place_tensor])
    hidden_in, which, places = lax.optimization_barrier((hidden_in, which, places))

    def send(value, axis, pairs):
        return lax.ppermute(value, axis, pairs)

    def send_across(value, pairs):
        both = [(a * 4 + b, (1 - a) * 4 + c) for a in range(2) for b, c in pairs]
        return lax.ppermute(value, ("inner", "tensor"), both)

    half = ((rows, half_width), bf16, None)
    mine, others = call_kernel(
        norm_kernel, "norm", which, [hidden_in, norm_gain.reshape(1, width)], [None] * 2, [half] * 2
    )
    two, one, middle = swap_pairs(4, 2), swap_pairs(4, 1), [(1, 2), (2, 1)]
    two_mine = send(mine, "tensor", two)
    two_theirs = send_across(others, two)
    one_mine = send(mine, "tensor", one)
    one_theirs = send_across(others, one)
    theirs = send(others, "inner", across_inner)
    early = [[mine], [theirs], [one_mine], [one_theirs], [two_mine], [two_theirs]]

    facts = jnp.stack([doc_ids, positions])
    facts_there = send(after(facts, two_theirs), "inner", across_inner)
    inverse = jnp.asarray([yarn_inverse(HEAD_SIZE) * 2], dtype=jnp.float32)
    signs = jnp.asarray([-1.0] * (HEAD_SIZE // 2) + [1.0] * (HEAD_SIZE // 2), dtype=jnp.float32)
    attention_gain = 0.1 * math.log(yarn_factor) + 1.0
    angles, documents, document_rows = call_kernel(
        functools.partial(facts_kernel, rows), "facts", places, [facts, facts_there, inverse],
        [None] * 3,
        [
            ((4 * slot_rows, HEAD_SIZE), jnp.float32, None),
            ((4 * slot_rows, 1), jnp.float32, None),
            ((16, 2 * HEAD_SIZE), bf16, None),
        ],
    )
    cosines = jnp.cos(angles) * attention_gain
    sines = jnp.sin(angles) * attention_gain * signs

    def stack(name, chunks, parts):
        flat = [array for chunk in chunks for array in chunk]
        out = lambda count: ((count * slot_rows, half_width), bf16, None)
        return call_kernel(
            functools.partial(stack_kernel, [len(chunk) for chunk in chunks]), name, which, flat,
            [None] * len(flat), [out(count) for count in parts],
        )

    def sent_halves(wholes, kind):
        count = wholes[0].shape[0]
        wides = [whole.shape[1] // 2 for whole in wholes]
        specs = [
            pl.BlockSpec((count, wide), lambda step, which: (0, 1 - which[1])) for wide in wides
        ]
        return call_kernel(
            copy_kernel, "sent", places, wholes, specs, [((count, sum(wides)), kind, None)]
        )[0]

    def project_pair(stacked):
        keys, values = product(stacked, w_key), product(stacked, value_weight)
        return keys, values, send(sent_halves([keys, values], jnp.float32), "inner", across_inner)

    def project_query(stacked):
        queries = product(stacked, w_query)
        return queries, send(sent_halves([queries], bf16), "inner", across_inner)

    def gather_pairs(pair):
        found = [pair]
        for flip in range(1, outer_count):
            found.append(send(pair, "outer", swap_pairs(outer_count, flip)))
        return found

    def gather_by_steps(pair):
        found = {0: pair}
        bit = outer_count // 2
        while bit:
            for flip in list(found):
                found[flip | bit] = send(found[flip], "outer", swap_pairs(outer_count, bit))
            bit //= 2
        return [found[flip] for flip in range(outer_count)]

    def rotate_pair(projected, first, extra):
        keys, values, came = projected
        count = came.shape[0]
        half_spec = pl.BlockSpec((count, HEAD_SIZE), lambda step, which: (0, which[0]))
        table_spec = pl.BlockSpec((count, HEAD_SIZE), lambda step, which: (first // count, 0))
        out_rows = count + sum(array.shape[0] for array in extra)
        return call_kernel(
            functools.partial(pair_kernel, rows), "pair", which,
            [keys, values, came, cosines, sines] + extra,
            [half_spec, half_spec, None, table_spec, table_spec] + [None] * len(extra),
            [((out_rows, 2 * HEAD_SIZE), bf16, None)],
        )[0]

    early_stacked, own_rows, two_rows = stack("early_rows", early, (3, 1, 1))
    middle_rows = send(own_rows, "tensor", middle)
    ends_rows = send(two_rows, "tensor", [(1, 0), (2, 3)])
    early_projected = project_pair(early_stacked)
    early_queries, early_came = project_query(early_stacked)
    late_stacked = stack("late_rows", [[ends_rows, middle_rows]], (1,))[0]
    late_projected = project_pair(late_stacked)
    late_queries, late_came = project_query(late_stacked)
    early_pairs = gather_by_steps(rotate_pair(early_projected, 0, [document_rows]))
    late_pairs = gather_pairs(rotate_pair(late_projected, early_rows, []))

    def attend(slot, *wait):
        queries, came = (late_queries, late_came) if slot == 3 else (early_queries, early_came)
        block = slot % 3
        if wait:
            came = after(came, *wait)
        rows_spec = lambda wide, block: pl.BlockSpec((slot_rows, wide), lambda step, which: (block, 0))
        half_spec = pl.BlockSpec((slot_rows, query_half), lambda step, which: (block, which[1]))
        stacked = query_half // HEAD_SIZE * slot_rows
        return call_kernel(
            functools.partial(attention_kernel, slot, outer_count, rows), "attention", places,
            [queries, came, cosines, sines, documents] + early_pairs + late_pairs,
            [
                half_spec, rows_spec(query_half, block),
                rows_spec(HEAD_SIZE, slot), rows_spec(HEAD_SIZE, slot), rows_spec(1, slot),
            ] + [None] * (2 * outer_count),
            [((rows, query_half), bf16, None)] * 2,
            scratch=[
                pltpu.VMEM((stacked, 1), jnp.float32),
                pltpu.VMEM((stacked, 1), jnp.float32),
                pltpu.VMEM((stacked, HEAD_SIZE), jnp.float32),
            ],
        )

    def joined(slot, *wait):
        here, gone = attend(slot, *wait)
        came = send(gone, "inner", across_inner)
        return call_kernel(
            join_kernel, "join", places, [here, came], [None] * 2,
            [((rows, 2 * query_half), bf16, None)],
        )[0]

    rows_3 = joined(3)
    rows_2 = joined(2)
    term_3 = product(rows_3, w_out).astype(bf16)
    came_3 = send(term_3, "tensor", swap_pairs(4, 3))
    came_2 = send(product(rows_2, w_out).astype(bf16), "tensor", two)
    rows_1 = joined(1, term_3)
    came_1 = send(product(rows_1, w_out).astype(bf16), "tensor", one)
    rows_0 = joined(0, term_3)
    total = lax.optimization_barrier(product(rows_0, w_out))
    total = total + hidden_in.astype(jnp.float32) + came_1.astype(jnp.float32)
    total = total + came_2.astype(jnp.float32) + came_3.astype(jnp.float32)
    return total.astype(bf16)


def solution(mesh):
    in_specs = (
        P(("outer", "inner", "tensor"), None),
        P(),
        P("inner", "tensor"),
        P("inner", "tensor"),
        P("inner", "tensor"),
        P("tensor", None),
        P(("outer", "inner")),
        P(("outer", "inner")),
    )
    out_specs = P(("outer", "inner", "tensor"), None)

    def chosen(*arrays):
        outer_count = mesh.shape["outer"]
        key_heads = arrays[3].shape[1] // HEAD_SIZE // mesh.shape["tensor"]
        short = (
            mesh.shape["tensor"] == 4
            and mesh.shape["inner"] == 2
            and key_heads == 2
            and outer_count & (outer_count - 1) == 0
            and arrays[0].shape[0] % (mesh.size * 16) == 0
            and arrays[0].shape[0] // outer_count <= 512
        )
        mapped = jax.shard_map(
            short_body if short else body,
            mesh=mesh, in_specs=in_specs, out_specs=out_specs, check_vma=False,
        )
        return mapped(*arrays)

    return chosen
```

```python
import functools
import math

import jax
import jax.numpy as jnp
from jax import lax
from jax.experimental import pallas as pl
from jax.experimental.pallas import tpu as pltpu
from jax.sharding import PartitionSpec as P

HEAD_SIZE = 128


rope_base = 500000.0
yarn_factor = 8.0
trained_context = 8192.0
beta_fast = 32.0
beta_slow = 1.0
norm_epsilon = 1e-05
masked_score = -1e30


def yarn_inverse(head_dim):
    half_dim = head_dim // 2

    def correction(rotations):
        return (
            head_dim
            * math.log(trained_context / (rotations * 2.0 * math.pi))
            / (2.0 * math.log(rope_base))
        )

    lowest = max(math.floor(correction(beta_fast)), 0)
    highest = min(math.ceil(correction(beta_slow)), head_dim - 1)
    spread = max(highest - lowest, 0.001)
    values = []
    for column in range(half_dim):
        extrapolated = rope_base ** (-2.0 * column / head_dim)
        ramp = min(max((column - lowest) / spread, 0.0), 1.0)
        values.append(extrapolated / yarn_factor * ramp + extrapolated * (1.0 - ramp))
    return values


def yarn_tables(positions, head_dim):
    inverse = jnp.asarray(yarn_inverse(head_dim), dtype=jnp.float32)
    attention_gain = 0.1 * math.log(yarn_factor) + 1.0
    angles = positions.astype(jnp.float32)[:, None] * inverse[None, :]
    return (jnp.cos(angles) * attention_gain, jnp.sin(angles) * attention_gain)


def apply_rotation(heads, cosine_table, sine_table):
    half_dim = heads.shape[-1] // 2
    first_half = heads[..., :half_dim]
    second_half = heads[..., half_dim:]
    cos_rows = cosine_table[:, None, :]
    sin_rows = sine_table[:, None, :]
    return jnp.concatenate(
        [
            first_half * cos_rows - second_half * sin_rows,
            second_half * cos_rows + first_half * sin_rows,
        ],
        axis=-1,
    )


def rms_normed(hidden_in, norm_gain):
    widened = hidden_in.astype(jnp.float32)
    power = jnp.mean(widened * widened, axis=-1, keepdims=True)
    return (widened * lax.rsqrt(power + norm_epsilon) * norm_gain).astype(jnp.bfloat16)


def body(hidden_in, norm_gain, w_query, w_key, value_weight, w_out, doc_ids, positions):
    normed = rms_normed(hidden_in, norm_gain)
    block_rows = lax.all_gather(normed, "tensor", axis=0, tiled=True)
    tokens_here = block_rows.shape[0]
    query_width = w_query.shape[1]
    key_width = w_key.shape[1]
    inner_count = lax.axis_size("inner")
    slice_width = w_query.shape[0]
    arranged = block_rows.reshape(tokens_here, inner_count, slice_width)
    received = lax.all_to_all(arranged, "inner", split_axis=1, concat_axis=0, tiled=True)
    received = received.reshape(inner_count * tokens_here, slice_width)
    stacked = jnp.concatenate([w_query, w_key, value_weight], axis=1)
    combined = lax.psum_scatter(
        jnp.dot(received, stacked, preferred_element_type=jnp.float32),
        "inner",
        scatter_dimension=0,
        tiled=True,
    )
    queries = combined[:, :query_width]
    key_matrix = combined[:, query_width : query_width + key_width]
    value_matrix = combined[:, query_width + key_width :]
    value_matrix = value_matrix.astype(jnp.bfloat16)
    heads_query = query_width // HEAD_SIZE
    heads_key = key_width // HEAD_SIZE
    queries_per_group = heads_query // heads_key
    cosine_table, sine_table = yarn_tables(positions, HEAD_SIZE)
    query_rot = (
        apply_rotation(
            queries.reshape(tokens_here, heads_query, HEAD_SIZE), cosine_table, sine_table
        )
        .astype(jnp.bfloat16)
        .reshape(tokens_here, query_width)
    )
    rotated_keys = (
        apply_rotation(
            key_matrix.reshape(tokens_here, heads_key, HEAD_SIZE), cosine_table, sine_table
        )
        .astype(jnp.bfloat16)
        .reshape(tokens_here, key_width)
    )
    documents = lax.all_gather(doc_ids, ("outer", "inner"), axis=0, tiled=True)
    length_all = documents.shape[0]
    block_index = lax.axis_index(("outer", "inner"))
    sequence_index = jnp.arange(length_all, dtype=jnp.int32)
    query_documents = lax.dynamic_slice_in_dim(documents, block_index * tokens_here, tokens_here, 0)
    query_index = lax.dynamic_slice_in_dim(
        sequence_index, block_index * tokens_here, tokens_here, 0
    )
    row_documents = jnp.tile(query_documents, queries_per_group)
    row_index = jnp.tile(query_index, queries_per_group)
    top_index = jnp.max(query_index)
    top_document = jnp.max(query_documents)
    low_document = jnp.min(query_documents)
    grouped_heads = jnp.transpose(
        query_rot.reshape(tokens_here, heads_key, queries_per_group, HEAD_SIZE), (1, 2, 0, 3)
    ).reshape(heads_key, queries_per_group * tokens_here, HEAD_SIZE)
    score_scale = HEAD_SIZE ** (-0.5)

    def key_block(running, block_keys, block_values, first_row):
        row_count = block_keys.shape[0]
        piece_index = lax.dynamic_slice_in_dim(sequence_index, first_row, row_count, 0)
        piece_documents = lax.dynamic_slice_in_dim(documents, first_row, row_count, 0)
        live = (
            (jnp.min(piece_index) <= top_index)
            & (jnp.min(piece_documents) <= top_document)
            & (jnp.max(piece_documents) >= low_document)
        )

        def attend(current):
            row_peaks, totals, summed = current
            heads_keys = block_keys.reshape(row_count, heads_key, HEAD_SIZE)
            heads_values = block_values.reshape(row_count, heads_key, HEAD_SIZE)
            scores = (
                jnp.einsum(
                    "hqd,khd->hqk", grouped_heads, heads_keys, preferred_element_type=jnp.float32
                )
                * score_scale
            )
            allowed = (row_index[:, None] >= piece_index[None, :]) & (
                row_documents[:, None] == piece_documents[None, :]
            )
            scores = jnp.where(allowed[None], scores, masked_score)
            fresh = jnp.maximum(row_peaks, jnp.max(scores, axis=-1))
            weights = jnp.where(allowed[None], jnp.exp(scores - fresh[..., None]), 0.0)
            shrink = jnp.exp(row_peaks - fresh)
            totals = totals * shrink + jnp.sum(weights, axis=-1)
            summed = summed * shrink[..., None] + jnp.einsum(
                "hqk,khd->hqd",
                weights.astype(jnp.bfloat16),
                heads_values,
                preferred_element_type=jnp.float32,
            )
            return (fresh, totals, summed)

        return lax.cond(live, attend, lambda current: current, running)

    initial = (
        jnp.full((heads_key, queries_per_group * tokens_here), masked_score, jnp.float32),
        jnp.zeros((heads_key, queries_per_group * tokens_here), jnp.float32),
        jnp.zeros((heads_key, queries_per_group * tokens_here, HEAD_SIZE), jnp.float32),
    )
    piece_keys = lax.all_gather(rotated_keys, ("outer", "inner"), axis=0, tiled=True)
    piece_values = lax.all_gather(value_matrix, ("outer", "inner"), axis=0, tiled=True)
    row_count = piece_keys.shape[0]
    step_rows = 512
    steps_count = row_count // step_rows
    split_keys = piece_keys.reshape(steps_count, step_rows, key_width)
    split_values = piece_values.reshape(steps_count, step_rows, key_width)
    offsets = jnp.arange(steps_count, dtype=jnp.int32) * step_rows

    def scan_step(current, inputs):
        block_keys, block_values, offset = inputs
        return (key_block(current, block_keys, block_values, offset), None)

    result, unused = lax.scan(scan_step, initial, (split_keys, split_values, offsets))
    row_peaks, totals, summed = result
    heads_out = (summed / totals[..., None]).astype(jnp.bfloat16)
    attended = jnp.transpose(
        heads_out.reshape(heads_key, queries_per_group, tokens_here, HEAD_SIZE), (2, 0, 1, 3)
    ).reshape(tokens_here, query_width)
    full_term = jnp.dot(attended, w_out, preferred_element_type=jnp.float32)
    projected = lax.psum_scatter(
        full_term.astype(jnp.bfloat16), "tensor", scatter_dimension=0, tiled=True
    ).astype(jnp.float32)
    return (hidden_in.astype(jnp.float32) + projected).astype(jnp.bfloat16)


def swap_pairs(axis_size, flip):
    return [(place, place ^ flip) for place in range(axis_size)]


def after(value, *others):
    return lax.optimization_barrier((value,) + others)[0]


def whole_spec(array):
    zeros = (0,) * array.ndim
    return pl.BlockSpec(array.shape, lambda step, which: zeros)


def call_kernel(kernel, name, which, arrays, specs, outs, steps=1, scratch=(), mebibytes=16):
    shapes = [jax.ShapeDtypeStruct(shape, dtype) for shape, dtype, unused in outs]
    out_specs = [
        whole_spec(shape) if spec is None else spec for shape, (a, b, spec) in zip(shapes, outs)
    ]
    found = pl.pallas_call(
        kernel,
        name=name,
        grid_spec=pltpu.PrefetchScalarGridSpec(
            num_scalar_prefetch=1,
            grid=(steps,),
            in_specs=[
                whole_spec(array) if spec is None else spec for array, spec in zip(arrays, specs)
            ],
            out_specs=out_specs,
            scratch_shapes=list(scratch),
        ),
        out_shape=shapes,
        compiler_params=pltpu.CompilerParams(vmem_limit_bytes=mebibytes * 1024 * 1024),
    )(which, *arrays)
    return found


def norm_kernel(which, hidden, gain, mine, others):
    half_width = mine.shape[1]
    widened = hidden[...].astype(jnp.float32)
    power = jnp.mean(widened * widened, axis=-1, keepdims=True)
    normed = (widened * lax.rsqrt(power + norm_epsilon) * gain[...]).astype(jnp.bfloat16)

    @pl.when(which[0] == 0)
    def _():
        mine[...] = normed[:, :half_width]
        others[...] = normed[:, half_width:]

    @pl.when(which[0] != 0)
    def _():
        mine[...] = normed[:, half_width:]
        others[...] = normed[:, :half_width]


def stacked_rows(chunks):
    return jnp.concatenate(
        [
            chunk[...] if len(pair) == 1 else pair[0][...] + pair[1][...]
            for pair in chunks
            for chunk in pair[:1]
        ],
        axis=0,
    )


def split_chunks(refs, widths):
    chunks = []
    place = 0
    for width in widths:
        chunks.append(refs[place : place + width])
        place += width
    return chunks, refs[place:]


def product(left, right):
    return jnp.dot(left, right, preferred_element_type=jnp.float32)


def stack_kernel(widths, which, *refs):
    chunks, outs = split_chunks(refs, widths)
    outs[0][...] = stacked_rows(chunks)
    for place, out in zip((0, outs[0].shape[0] * 2 // 3), outs[1:]):
        out[...] = outs[0][place : place + out.shape[0]]


def other_part(value, rows):
    pieces = [value[place : place + rows] for place in range(0, value.shape[0], rows)]
    return jnp.concatenate([pieces[k ^ 1] for k in range(len(pieces))], axis=0)


def rotated(part, cosine_rows, sine_rows):
    return part * cosine_rows + pltpu.roll(part, HEAD_SIZE // 2, 1) * sine_rows


def pair_kernel(rows, which, keys, values, came, cosines, sines, *refs):
    out = refs[-1]
    count = keys.shape[0]
    added = other_part(came[...], rows).astype(jnp.float32)
    whole = rotated(keys[...] + added[:, :HEAD_SIZE], cosines[...], sines[...])
    out[:count, :HEAD_SIZE] = whole.astype(jnp.bfloat16)
    out[:count, HEAD_SIZE:] = (values[...] + added[:, HEAD_SIZE:]).astype(jnp.bfloat16)
    if len(refs) == 2:
        out[count:, :] = refs[0][...]


def facts_kernel(rows, which, here, there, inverse, angles, documents, document_rows):
    block = here.shape[1]
    line = lax.broadcasted_iota(jnp.int32, (block, 1), 0)
    slots = sum((line >= rows * number).astype(jnp.int32) for number in range(1, 4))
    source = (which[2] ^ slots) * rows + line - rows * slots
    chosen = lax.broadcasted_iota(jnp.int32, (block, block), 1) == source

    def ordered(row):
        parts = [
            jnp.sum(jnp.where(chosen, part[row : row + 1, :].astype(jnp.float32), 0.0), axis=1, keepdims=True)
            for part in (here, there)
        ]
        return jnp.concatenate(
            [part[place : place + rows] for place in range(0, block, rows) for part in parts], axis=0
        )

    angles[...] = ordered(1) * inverse[...]
    column = ordered(0)
    documents[...] = column
    count = column.shape[0]
    same = lax.broadcasted_iota(jnp.int32, (count, count), 0) == lax.broadcasted_iota(
        jnp.int32, (count, count), 1
    )
    wide = document_rows.shape[1]
    across = jnp.sum(jnp.where(same, column, 0.0), axis=0, keepdims=True)
    rest = jnp.concatenate(
        [across[:, wide:], jnp.zeros((1, 2 * wide - count), jnp.float32)], axis=1
    )
    number = lax.broadcasted_iota(jnp.int32, document_rows.shape, 0)
    document_rows[...] = jnp.where(
        number == 0, across[:, :wide], jnp.where(number == 1, rest, 0.0)
    ).astype(jnp.bfloat16)


def copy_kernel(which, *refs):
    *parts, out = refs
    place = 0
    for part in parts:
        out[:, place : place + part.shape[1]] = part[...].astype(out.dtype)
        place += part.shape[1]


def join_kernel(which, here, came, out):
    width = here.shape[1]

    @pl.when(which[1] == 0)
    def _():
        out[:, :width] = here[...]
        out[:, width:] = came[...]

    @pl.when(which[1] != 0)
    def _():
        out[:, :width] = came[...]
        out[:, width:] = here[...]


def attention_kernel(
    slot, blocks, rows, which, kept, came, cosines, sines, query_document, *refs
):
    early, late = refs[:blocks], refs[blocks : 2 * blocks]
    here, gone, peaks, totals, summed = refs[2 * blocks :]
    tokens, width = came.shape
    heads = width // HEAD_SIZE
    score_scale = HEAD_SIZE ** (-0.5) / math.log(2.0)
    block_rows = 4 * rows
    early_rows = 2 * block_rows - late[0].shape[0]
    whole = kept[...] + other_part(came[...], rows).astype(jnp.float32)
    stacked = jnp.concatenate(
        [
            rotated(whole[:, place : place + HEAD_SIZE], cosines[...], sines[...]).astype(
                jnp.bfloat16
            )
            for place in range(0, width, HEAD_SIZE)
        ],
        axis=0,
    )
    place_outer, place_inner, place_tensor = which[0], which[1], which[2]
    document = query_document[...]

    def inside(slot_number, part_number, row_number):
        return (place_inner ^ part_number) * block_rows + (place_tensor ^ slot_number) * rows + row_number

    line = lax.broadcasted_iota(jnp.int32, (tokens, 1), 0)
    second = (line >= rows).astype(jnp.int32)
    row_place = inside(slot, second, line - rows * second)
    line = lax.broadcasted_iota(jnp.int32, (1, 2 * block_rows), 1)
    slots = sum((line >= 2 * rows * number).astype(jnp.int32) for number in range(1, 4))
    left = line - 2 * rows * slots
    second = (left >= rows).astype(jnp.int32)
    key_place = inside(slots, second, left - rows * second)

    def joined(block, start):
        stop = start + HEAD_SIZE
        return jnp.concatenate([early[block][:early_rows, start:stop], late[block][:, start:stop]], axis=0)

    def key_document(block):
        lines = early[block][early_rows:, :].astype(jnp.float32)
        rest = 2 * block_rows - lines.shape[1]
        return jnp.concatenate([lines[0:1, :], lines[1:2, :rest]], axis=1)

    def block_scores(block):
        scores = lax.dot_general(
            stacked, joined(block, 0), (((1,), (1,)), ((), ())), preferred_element_type=jnp.float32
        )
        allowed = key_document(block) == document
        if block == 0:
            allowed = allowed & (key_place <= row_place)
        scores = scores.reshape(heads, tokens, -1) * score_scale
        return jnp.where(allowed[None], scores, masked_score).reshape(heads * tokens, -1)

    def weighted(block, weights):
        return product(weights.astype(jnp.bfloat16), joined(block, HEAD_SIZE))

    scores = block_scores(0)
    peak = jnp.max(scores, axis=-1, keepdims=True)
    weights = jnp.exp2(scores - peak)
    peaks[...] = peak
    totals[...] = jnp.sum(weights, axis=-1, keepdims=True)
    summed[...] = weighted(0, weights)
    lowest = jnp.min(document)
    for block in range(1, blocks):

        @pl.when(((place_outer ^ block) < place_outer) & (jnp.max(key_document(block)) >= lowest))
        def _():
            scores = block_scores(block)
            before = peaks[...]
            peak = jnp.maximum(before, jnp.max(scores, axis=-1, keepdims=True))
            weights = jnp.exp2(scores - peak)
            shrink = jnp.exp2(before - peak)
            peaks[...] = peak
            totals[...] = totals[...] * shrink + jnp.sum(weights, axis=-1, keepdims=True)
            summed[...] = summed[...] * shrink + weighted(block, weights)

    result = (summed[...] / totals[...]).astype(jnp.bfloat16)
    for head in range(heads):
        first = head * tokens
        columns = slice(head * HEAD_SIZE, (head + 1) * HEAD_SIZE)
        here[:, columns] = result[first : first + rows]
        gone[:, columns] = result[first + rows : first + tokens]


def short_body(hidden_in, norm_gain, w_query, w_key, value_weight, w_out, doc_ids, positions):
    place_outer = lax.axis_index("outer")
    place_inner = lax.axis_index("inner")
    place_tensor = lax.axis_index("tensor")
    outer_count = lax.axis_size("outer")
    rows, width = hidden_in.shape
    half_width = w_query.shape[0]
    query_half = w_query.shape[1] // 2
    slot_rows = 2 * rows
    early_rows = 3 * slot_rows
    bf16 = jnp.bfloat16
    across_inner = swap_pairs(2, 1)
    which = place_inner.reshape(1)
    places = jnp.stack([place_outer, place_inner, place_tensor])
    hidden_in, which, places = lax.optimization_barrier((hidden_in, which, places))

    def send(value, axis, pairs):
        return lax.ppermute(value, axis, pairs)

    def send_across(value, pairs):
        both = [(a * 4 + b, (1 - a) * 4 + c) for a in range(2) for b, c in pairs]
        return lax.ppermute(value, ("inner", "tensor"), both)

    half = ((rows, half_width), bf16, None)
    mine, others = call_kernel(
        norm_kernel, "norm", which, [hidden_in, norm_gain.reshape(1, width)], [None] * 2, [half] * 2
    )
    two, one, middle = swap_pairs(4, 2), swap_pairs(4, 1), [(1, 2), (2, 1)]
    two_mine = send(mine, "tensor", two)
    two_theirs = send_across(others, two)
    one_mine = send(mine, "tensor", one)
    one_theirs = send_across(others, one)
    theirs = send(others, "inner", across_inner)
    early = [[mine], [theirs], [one_mine], [one_theirs], [two_mine], [two_theirs]]

    facts = jnp.stack([doc_ids, positions])
    facts_there = send(after(facts, two_theirs), "inner", across_inner)
    inverse = jnp.asarray([yarn_inverse(HEAD_SIZE) * 2], dtype=jnp.float32)
    signs = jnp.asarray([-1.0] * (HEAD_SIZE // 2) + [1.0] * (HEAD_SIZE // 2), dtype=jnp.float32)
    attention_gain = 0.1 * math.log(yarn_factor) + 1.0
    angles, documents, document_rows = call_kernel(
        functools.partial(facts_kernel, rows), "facts", places, [facts, facts_there, inverse],
        [None] * 3,
        [
            ((4 * slot_rows, HEAD_SIZE), jnp.float32, None),
            ((4 * slot_rows, 1), jnp.float32, None),
            ((16, 2 * HEAD_SIZE), bf16, None),
        ],
    )
    cosines = jnp.cos(angles) * attention_gain
    sines = jnp.sin(angles) * attention_gain * signs

    def stack(name, chunks, parts):
        flat = [array for chunk in chunks for array in chunk]
        out = lambda count: ((count * slot_rows, half_width), bf16, None)
        return call_kernel(
            functools.partial(stack_kernel, [len(chunk) for chunk in chunks]), name, which, flat,
            [None] * len(flat), [out(count) for count in parts],
        )

    def sent_halves(wholes, kind):
        count = wholes[0].shape[0]
        wides = [whole.shape[1] // 2 for whole in wholes]
        specs = [
            pl.BlockSpec((count, wide), lambda step, which: (0, 1 - which[1])) for wide in wides
        ]
        return call_kernel(
            copy_kernel, "sent", places, wholes, specs, [((count, sum(wides)), kind, None)]
        )[0]

    def project_pair(stacked):
        keys, values = product(stacked, w_key), product(stacked, value_weight)
        return keys, values, send(sent_halves([keys, values], jnp.float32), "inner", across_inner)

    def project_query(stacked):
        queries = product(stacked, w_query)
        return queries, send(sent_halves([queries], bf16), "inner", across_inner)

    def gather_pairs(pair):
        found = [pair]
        for flip in range(1, outer_count):
            found.append(send(pair, "outer", swap_pairs(outer_count, flip)))
        return found

    def gather_by_steps(pair):
        found = {0: pair}
        bit = outer_count // 2
        while bit:
            for flip in list(found):
                found[flip | bit] = send(found[flip], "outer", swap_pairs(outer_count, bit))
            bit //= 2
        return [found[flip] for flip in range(outer_count)]

    def rotate_pair(projected, first, extra):
        keys, values, came = projected
        count = came.shape[0]
        half_spec = pl.BlockSpec((count, HEAD_SIZE), lambda step, which: (0, which[0]))
        table_spec = pl.BlockSpec((count, HEAD_SIZE), lambda step, which: (first // count, 0))
        out_rows = count + sum(array.shape[0] for array in extra)
        return call_kernel(
            functools.partial(pair_kernel, rows), "pair", which,
            [keys, values, came, cosines, sines] + extra,
            [half_spec, half_spec, None, table_spec, table_spec] + [None] * len(extra),
            [((out_rows, 2 * HEAD_SIZE), bf16, None)],
        )[0]

    early_stacked, own_rows, two_rows = stack("early_rows", early, (3, 1, 1))
    middle_rows = send(own_rows, "tensor", middle)
    ends_rows = send(two_rows, "tensor", [(1, 0), (2, 3)])
    early_projected = project_pair(early_stacked)
    early_queries, early_came = project_query(early_stacked)
    late_stacked = stack("late_rows", [[middle_rows, ends_rows]], (1,))[0]
    late_projected = project_pair(late_stacked)
    late_queries, late_came = project_query(late_stacked)
    early_pairs = gather_by_steps(rotate_pair(early_projected, 0, [document_rows]))
    late_pairs = gather_pairs(rotate_pair(late_projected, early_rows, []))

    def attend(slot, *wait):
        queries, came = (late_queries, late_came) if slot == 3 else (early_queries, early_came)
        block = slot % 3
        if wait:
            came = after(came, *wait)
        rows_spec = lambda wide, block: pl.BlockSpec((slot_rows, wide), lambda step, which: (block, 0))
        half_spec = pl.BlockSpec((slot_rows, query_half), lambda step, which: (block, which[1]))
        stacked = query_half // HEAD_SIZE * slot_rows
        return call_kernel(
            functools.partial(attention_kernel, slot, outer_count, rows), "attention", places,
            [queries, came, cosines, sines, documents] + early_pairs + late_pairs,
            [
                half_spec, rows_spec(query_half, block),
                rows_spec(HEAD_SIZE, slot), rows_spec(HEAD_SIZE, slot), rows_spec(1, slot),
            ] + [None] * (2 * outer_count),
            [((rows, query_half), bf16, None)] * 2,
            scratch=[
                pltpu.VMEM((stacked, 1), jnp.float32),
                pltpu.VMEM((stacked, 1), jnp.float32),
                pltpu.VMEM((stacked, HEAD_SIZE), jnp.float32),
            ],
        )

    def joined(slot, *wait):
        here, gone = attend(slot, *wait)
        came = send(gone, "inner", across_inner)
        return call_kernel(
            join_kernel, "join", places, [here, came], [None] * 2,
            [((rows, 2 * query_half), bf16, None)],
        )[0]

    rows_3 = joined(3)
    rows_2 = joined(2)
    term_3 = product(rows_3, w_out).astype(bf16)
    came_3 = send(term_3, "tensor", swap_pairs(4, 3))
    term_2 = product(rows_2, w_out).astype(bf16)
    came_2 = send(term_2, "tensor", two)
    rows_1 = joined(1, term_3)
    came_1 = send(product(rows_1, w_out).astype(bf16), "tensor", one)
    rows_0 = joined(0, term_2)
    total = lax.optimization_barrier(product(rows_0, w_out))
    total = total + hidden_in.astype(jnp.float32) + came_1.astype(jnp.float32)
    total = total + came_2.astype(jnp.float32) + came_3.astype(jnp.float32)
    return total.astype(bf16)


def solution(mesh):
    in_specs = (
        P(("outer", "inner", "tensor"), None),
        P(),
        P("inner", "tensor"),
        P("inner", "tensor"),
        P("inner", "tensor"),
        P("tensor", None),
        P(("outer", "inner")),
        P(("outer", "inner")),
    )
    out_specs = P(("outer", "inner", "tensor"), None)

    def chosen(*arrays):
        outer_count = mesh.shape["outer"]
        key_heads = arrays[3].shape[1] // HEAD_SIZE // mesh.shape["tensor"]
        short = (
            mesh.shape["tensor"] == 4
            and mesh.shape["inner"] == 2
            and key_heads == 2
            and outer_count & (outer_count - 1) == 0
            and arrays[0].shape[0] % (mesh.size * 16) == 0
            and arrays[0].shape[0] // outer_count <= 512
        )
        mapped = jax.shard_map(
            short_body if short else body,
            mesh=mesh, in_specs=in_specs, out_specs=out_specs, check_vma=False,
        )
        return mapped(*arrays)

    return chosen
```

```python
import functools
import math

import jax
import jax.numpy as jnp
from jax import lax
from jax.experimental import pallas as pl
from jax.experimental.pallas import tpu as pltpu
from jax.sharding import PartitionSpec as P

HEAD_SIZE = 128


rope_base = 500000.0
yarn_factor = 8.0
trained_context = 8192.0
beta_fast = 32.0
beta_slow = 1.0
norm_epsilon = 1e-05
masked_score = -1e30


def yarn_inverse(head_dim):
    half_dim = head_dim // 2

    def correction(rotations):
        return (
            head_dim
            * math.log(trained_context / (rotations * 2.0 * math.pi))
            / (2.0 * math.log(rope_base))
        )

    lowest = max(math.floor(correction(beta_fast)), 0)
    highest = min(math.ceil(correction(beta_slow)), head_dim - 1)
    spread = max(highest - lowest, 0.001)
    values = []
    for column in range(half_dim):
        extrapolated = rope_base ** (-2.0 * column / head_dim)
        ramp = min(max((column - lowest) / spread, 0.0), 1.0)
        values.append(extrapolated / yarn_factor * ramp + extrapolated * (1.0 - ramp))
    return values


def yarn_tables(positions, head_dim):
    inverse = jnp.asarray(yarn_inverse(head_dim), dtype=jnp.float32)
    attention_gain = 0.1 * math.log(yarn_factor) + 1.0
    angles = positions.astype(jnp.float32)[:, None] * inverse[None, :]
    return (jnp.cos(angles) * attention_gain, jnp.sin(angles) * attention_gain)


def apply_rotation(heads, cosine_table, sine_table):
    half_dim = heads.shape[-1] // 2
    first_half = heads[..., :half_dim]
    second_half = heads[..., half_dim:]
    cos_rows = cosine_table[:, None, :]
    sin_rows = sine_table[:, None, :]
    return jnp.concatenate(
        [
            first_half * cos_rows - second_half * sin_rows,
            second_half * cos_rows + first_half * sin_rows,
        ],
        axis=-1,
    )


def rms_normed(hidden_in, norm_gain):
    widened = hidden_in.astype(jnp.float32)
    power = jnp.mean(widened * widened, axis=-1, keepdims=True)
    return (widened * lax.rsqrt(power + norm_epsilon) * norm_gain).astype(jnp.bfloat16)


def body(hidden_in, norm_gain, w_query, w_key, value_weight, w_out, doc_ids, positions):
    normed = rms_normed(hidden_in, norm_gain)
    block_rows = lax.all_gather(normed, "tensor", axis=0, tiled=True)
    tokens_here = block_rows.shape[0]
    query_width = w_query.shape[1]
    key_width = w_key.shape[1]
    inner_count = lax.axis_size("inner")
    slice_width = w_query.shape[0]
    arranged = block_rows.reshape(tokens_here, inner_count, slice_width)
    received = lax.all_to_all(arranged, "inner", split_axis=1, concat_axis=0, tiled=True)
    received = received.reshape(inner_count * tokens_here, slice_width)
    stacked = jnp.concatenate([w_query, w_key, value_weight], axis=1)
    combined = lax.psum_scatter(
        jnp.dot(received, stacked, preferred_element_type=jnp.float32),
        "inner",
        scatter_dimension=0,
        tiled=True,
    )
    queries = combined[:, :query_width]
    key_matrix = combined[:, query_width : query_width + key_width]
    value_matrix = combined[:, query_width + key_width :]
    value_matrix = value_matrix.astype(jnp.bfloat16)
    heads_query = query_width // HEAD_SIZE
    heads_key = key_width // HEAD_SIZE
    queries_per_group = heads_query // heads_key
    cosine_table, sine_table = yarn_tables(positions, HEAD_SIZE)
    query_rot = (
        apply_rotation(
            queries.reshape(tokens_here, heads_query, HEAD_SIZE), cosine_table, sine_table
        )
        .astype(jnp.bfloat16)
        .reshape(tokens_here, query_width)
    )
    rotated_keys = (
        apply_rotation(
            key_matrix.reshape(tokens_here, heads_key, HEAD_SIZE), cosine_table, sine_table
        )
        .astype(jnp.bfloat16)
        .reshape(tokens_here, key_width)
    )
    documents = lax.all_gather(doc_ids, ("outer", "inner"), axis=0, tiled=True)
    length_all = documents.shape[0]
    block_index = lax.axis_index(("outer", "inner"))
    sequence_index = jnp.arange(length_all, dtype=jnp.int32)
    query_documents = lax.dynamic_slice_in_dim(documents, block_index * tokens_here, tokens_here, 0)
    query_index = lax.dynamic_slice_in_dim(
        sequence_index, block_index * tokens_here, tokens_here, 0
    )
    row_documents = jnp.tile(query_documents, queries_per_group)
    row_index = jnp.tile(query_index, queries_per_group)
    top_index = jnp.max(query_index)
    top_document = jnp.max(query_documents)
    low_document = jnp.min(query_documents)
    grouped_heads = jnp.transpose(
        query_rot.reshape(tokens_here, heads_key, queries_per_group, HEAD_SIZE), (1, 2, 0, 3)
    ).reshape(heads_key, queries_per_group * tokens_here, HEAD_SIZE)
    score_scale = HEAD_SIZE ** (-0.5)

    def key_block(running, block_keys, block_values, first_row):
        row_count = block_keys.shape[0]
        piece_index = lax.dynamic_slice_in_dim(sequence_index, first_row, row_count, 0)
        piece_documents = lax.dynamic_slice_in_dim(documents, first_row, row_count, 0)
        live = (
            (jnp.min(piece_index) <= top_index)
            & (jnp.min(piece_documents) <= top_document)
            & (jnp.max(piece_documents) >= low_document)
        )

        def attend(current):
            row_peaks, totals, summed = current
            heads_keys = block_keys.reshape(row_count, heads_key, HEAD_SIZE)
            heads_values = block_values.reshape(row_count, heads_key, HEAD_SIZE)
            scores = (
                jnp.einsum(
                    "hqd,khd->hqk", grouped_heads, heads_keys, preferred_element_type=jnp.float32
                )
                * score_scale
            )
            allowed = (row_index[:, None] >= piece_index[None, :]) & (
                row_documents[:, None] == piece_documents[None, :]
            )
            scores = jnp.where(allowed[None], scores, masked_score)
            fresh = jnp.maximum(row_peaks, jnp.max(scores, axis=-1))
            weights = jnp.where(allowed[None], jnp.exp(scores - fresh[..., None]), 0.0)
            shrink = jnp.exp(row_peaks - fresh)
            totals = totals * shrink + jnp.sum(weights, axis=-1)
            summed = summed * shrink[..., None] + jnp.einsum(
                "hqk,khd->hqd",
                weights.astype(jnp.bfloat16),
                heads_values,
                preferred_element_type=jnp.float32,
            )
            return (fresh, totals, summed)

        return lax.cond(live, attend, lambda current: current, running)

    initial = (
        jnp.full((heads_key, queries_per_group * tokens_here), masked_score, jnp.float32),
        jnp.zeros((heads_key, queries_per_group * tokens_here), jnp.float32),
        jnp.zeros((heads_key, queries_per_group * tokens_here, HEAD_SIZE), jnp.float32),
    )
    piece_keys = lax.all_gather(rotated_keys, ("outer", "inner"), axis=0, tiled=True)
    piece_values = lax.all_gather(value_matrix, ("outer", "inner"), axis=0, tiled=True)
    row_count = piece_keys.shape[0]
    step_rows = 512
    steps_count = row_count // step_rows
    split_keys = piece_keys.reshape(steps_count, step_rows, key_width)
    split_values = piece_values.reshape(steps_count, step_rows, key_width)
    offsets = jnp.arange(steps_count, dtype=jnp.int32) * step_rows

    def scan_step(current, inputs):
        block_keys, block_values, offset = inputs
        return (key_block(current, block_keys, block_values, offset), None)

    result, unused = lax.scan(scan_step, initial, (split_keys, split_values, offsets))
    row_peaks, totals, summed = result
    heads_out = (summed / totals[..., None]).astype(jnp.bfloat16)
    attended = jnp.transpose(
        heads_out.reshape(heads_key, queries_per_group, tokens_here, HEAD_SIZE), (2, 0, 1, 3)
    ).reshape(tokens_here, query_width)
    full_term = jnp.dot(attended, w_out, preferred_element_type=jnp.float32)
    projected = lax.psum_scatter(
        full_term.astype(jnp.bfloat16), "tensor", scatter_dimension=0, tiled=True
    ).astype(jnp.float32)
    return (hidden_in.astype(jnp.float32) + projected).astype(jnp.bfloat16)


def swap_pairs(axis_size, flip):
    return [(place, place ^ flip) for place in range(axis_size)]


def after(value, *others):
    return lax.optimization_barrier((value,) + others)[0]


def whole_spec(array):
    zeros = (0,) * array.ndim
    return pl.BlockSpec(array.shape, lambda step, which: zeros)


def call_kernel(kernel, name, which, arrays, specs, outs, steps=1, scratch=(), mebibytes=16):
    shapes = [jax.ShapeDtypeStruct(shape, dtype) for shape, dtype, unused in outs]
    out_specs = [
        whole_spec(shape) if spec is None else spec for shape, (a, b, spec) in zip(shapes, outs)
    ]
    found = pl.pallas_call(
        kernel,
        name=name,
        grid_spec=pltpu.PrefetchScalarGridSpec(
            num_scalar_prefetch=1,
            grid=(steps,),
            in_specs=[
                whole_spec(array) if spec is None else spec for array, spec in zip(arrays, specs)
            ],
            out_specs=out_specs,
            scratch_shapes=list(scratch),
        ),
        out_shape=shapes,
        compiler_params=pltpu.CompilerParams(vmem_limit_bytes=mebibytes * 1024 * 1024),
    )(which, *arrays)
    return found


def norm_kernel(which, hidden, gain, mine, others):
    half_width = mine.shape[1]
    widened = hidden[...].astype(jnp.float32)
    power = jnp.mean(widened * widened, axis=-1, keepdims=True)
    normed = (widened * lax.rsqrt(power + norm_epsilon) * gain[...]).astype(jnp.bfloat16)

    @pl.when(which[0] == 0)
    def _():
        mine[...] = normed[:, :half_width]
        others[...] = normed[:, half_width:]

    @pl.when(which[0] != 0)
    def _():
        mine[...] = normed[:, half_width:]
        others[...] = normed[:, :half_width]


def stacked_rows(chunks):
    return jnp.concatenate(
        [
            chunk[...] if len(pair) == 1 else pair[0][...] + pair[1][...]
            for pair in chunks
            for chunk in pair[:1]
        ],
        axis=0,
    )


def split_chunks(refs, widths):
    chunks = []
    place = 0
    for width in widths:
        chunks.append(refs[place : place + width])
        place += width
    return chunks, refs[place:]


def product(left, right):
    return jnp.dot(left, right, preferred_element_type=jnp.float32)


def stack_kernel(widths, which, *refs):
    chunks, outs = split_chunks(refs, widths)
    outs[0][...] = stacked_rows(chunks)
    for place, out in zip((0, outs[0].shape[0] * 2 // 3), outs[1:]):
        out[...] = outs[0][place : place + out.shape[0]]


def other_part(value, rows):
    pieces = [value[place : place + rows] for place in range(0, value.shape[0], rows)]
    return jnp.concatenate([pieces[k ^ 1] for k in range(len(pieces))], axis=0)


def rotated(part, cosine_rows, sine_rows):
    return part * cosine_rows + pltpu.roll(part, HEAD_SIZE // 2, 1) * sine_rows


def pair_kernel(rows, which, keys, values, came, cosines, sines, *refs):
    out = refs[-1]
    count = keys.shape[0]
    added = other_part(came[...], rows).astype(jnp.float32)
    whole = rotated(keys[...] + added[:, :HEAD_SIZE], cosines[...], sines[...])
    out[:count, :HEAD_SIZE] = whole.astype(jnp.bfloat16)
    out[:count, HEAD_SIZE:] = (values[...] + added[:, HEAD_SIZE:]).astype(jnp.bfloat16)
    if len(refs) == 2:
        out[count:, :] = refs[0][...]


def facts_kernel(rows, which, here, there, inverse, angles, documents, document_rows):
    block = here.shape[1]
    line = lax.broadcasted_iota(jnp.int32, (block, 1), 0)
    slots = sum((line >= rows * number).astype(jnp.int32) for number in range(1, 4))
    source = (which[2] ^ slots) * rows + line - rows * slots
    chosen = lax.broadcasted_iota(jnp.int32, (block, block), 1) == source

    def ordered(row):
        parts = [
            jnp.sum(jnp.where(chosen, part[row : row + 1, :].astype(jnp.float32), 0.0), axis=1, keepdims=True)
            for part in (here, there)
        ]
        return jnp.concatenate(
            [part[place : place + rows] for place in range(0, block, rows) for part in parts], axis=0
        )

    angles[...] = ordered(1) * inverse[...]
    column = ordered(0)
    documents[...] = column
    count = column.shape[0]
    same = lax.broadcasted_iota(jnp.int32, (count, count), 0) == lax.broadcasted_iota(
        jnp.int32, (count, count), 1
    )
    wide = document_rows.shape[1]
    across = jnp.sum(jnp.where(same, column, 0.0), axis=0, keepdims=True)
    rest = jnp.concatenate(
        [across[:, wide:], jnp.zeros((1, 2 * wide - count), jnp.float32)], axis=1
    )
    number = lax.broadcasted_iota(jnp.int32, document_rows.shape, 0)
    document_rows[...] = jnp.where(
        number == 0, across[:, :wide], jnp.where(number == 1, rest, 0.0)
    ).astype(jnp.bfloat16)


def copy_kernel(which, *refs):
    *parts, out = refs
    place = 0
    for part in parts:
        out[:, place : place + part.shape[1]] = part[...].astype(out.dtype)
        place += part.shape[1]


def join_kernel(which, here, came, out):
    width = here.shape[1]

    @pl.when(which[1] == 0)
    def _():
        out[:, :width] = here[...]
        out[:, width:] = came[...]

    @pl.when(which[1] != 0)
    def _():
        out[:, :width] = came[...]
        out[:, width:] = here[...]


def attention_kernel(
    slot, blocks, rows, which, kept, came, cosines, sines, query_document, *refs
):
    early, late = refs[:blocks], refs[blocks : 2 * blocks]
    here, gone, peaks, totals, summed = refs[2 * blocks :]
    tokens, width = came.shape
    heads = width // HEAD_SIZE
    score_scale = HEAD_SIZE ** (-0.5) / math.log(2.0)
    block_rows = 4 * rows
    early_rows = 2 * block_rows - late[0].shape[0]
    whole = kept[...] + other_part(came[...], rows).astype(jnp.float32)
    stacked = jnp.concatenate(
        [
            rotated(whole[:, place : place + HEAD_SIZE], cosines[...], sines[...]).astype(
                jnp.bfloat16
            )
            for place in range(0, width, HEAD_SIZE)
        ],
        axis=0,
    )
    place_outer, place_inner, place_tensor = which[0], which[1], which[2]
    document = query_document[...]

    def inside(slot_number, part_number, row_number):
        return (place_inner ^ part_number) * block_rows + (place_tensor ^ slot_number) * rows + row_number

    line = lax.broadcasted_iota(jnp.int32, (tokens, 1), 0)
    second = (line >= rows).astype(jnp.int32)
    row_place = inside(slot, second, line - rows * second)
    line = lax.broadcasted_iota(jnp.int32, (1, 2 * block_rows), 1)
    slots = sum((line >= 2 * rows * number).astype(jnp.int32) for number in range(1, 4))
    left = line - 2 * rows * slots
    second = (left >= rows).astype(jnp.int32)
    key_place = inside(slots, second, left - rows * second)

    def joined(block, start):
        stop = start + HEAD_SIZE
        return jnp.concatenate([early[block][:early_rows, start:stop], late[block][:, start:stop]], axis=0)

    def key_document(block):
        lines = early[block][early_rows:, :].astype(jnp.float32)
        rest = 2 * block_rows - lines.shape[1]
        return jnp.concatenate([lines[0:1, :], lines[1:2, :rest]], axis=1)

    def block_scores(block):
        allowed = key_document(block) == document
        if block == 0:
            allowed = allowed & (key_place <= row_place)
        barred = jnp.where(allowed, 0.0, masked_score)
        scores = lax.dot_general(
            stacked, joined(block, 0), (((1,), (1,)), ((), ())), preferred_element_type=jnp.float32
        )
        scores = scores.reshape(heads, tokens, -1) * score_scale + barred[None]
        return scores.reshape(heads * tokens, -1)

    def weighted(block, weights):
        return product(weights.astype(jnp.bfloat16), joined(block, HEAD_SIZE))

    scores = block_scores(0)
    peak = jnp.max(scores, axis=-1, keepdims=True)
    weights = jnp.exp2(scores - peak)
    peaks[...] = peak
    totals[...] = jnp.sum(weights, axis=-1, keepdims=True)
    summed[...] = weighted(0, weights)
    lowest = jnp.min(document)
    for block in range(1, blocks):

        @pl.when(((place_outer ^ block) < place_outer) & (jnp.max(key_document(block)) >= lowest))
        def _():
            scores = block_scores(block)
            before = peaks[...]
            peak = jnp.maximum(before, jnp.max(scores, axis=-1, keepdims=True))
            weights = jnp.exp2(scores - peak)
            shrink = jnp.exp2(before - peak)
            peaks[...] = peak
            totals[...] = totals[...] * shrink + jnp.sum(weights, axis=-1, keepdims=True)
            summed[...] = summed[...] * shrink + weighted(block, weights)

    result = (summed[...] / totals[...]).astype(jnp.bfloat16)
    for head in range(heads):
        first = head * tokens
        columns = slice(head * HEAD_SIZE, (head + 1) * HEAD_SIZE)
        here[:, columns] = result[first : first + rows]
        gone[:, columns] = result[first + rows : first + tokens]


def short_body(hidden_in, norm_gain, w_query, w_key, value_weight, w_out, doc_ids, positions):
    place_outer = lax.axis_index("outer")
    place_inner = lax.axis_index("inner")
    place_tensor = lax.axis_index("tensor")
    outer_count = lax.axis_size("outer")
    rows, width = hidden_in.shape
    half_width = w_query.shape[0]
    query_half = w_query.shape[1] // 2
    slot_rows = 2 * rows
    early_rows = 3 * slot_rows
    bf16 = jnp.bfloat16
    across_inner = swap_pairs(2, 1)
    which = place_inner.reshape(1)
    places = jnp.stack([place_outer, place_inner, place_tensor])
    hidden_in, which, places = lax.optimization_barrier((hidden_in, which, places))

    def send(value, axis, pairs):
        return lax.ppermute(value, axis, pairs)

    def send_across(value, pairs):
        both = [(a * 4 + b, (1 - a) * 4 + c) for a in range(2) for b, c in pairs]
        return lax.ppermute(value, ("inner", "tensor"), both)

    half = ((rows, half_width), bf16, None)
    mine, others = call_kernel(
        norm_kernel, "norm", which, [hidden_in, norm_gain.reshape(1, width)], [None] * 2, [half] * 2
    )
    two, one, middle = swap_pairs(4, 2), swap_pairs(4, 1), [(1, 2), (2, 1)]
    two_mine = send(mine, "tensor", two)
    two_theirs = send_across(others, two)
    one_mine = send(mine, "tensor", one)
    one_theirs = send_across(others, one)
    theirs = send(others, "inner", across_inner)
    early = [[mine], [theirs], [one_mine], [one_theirs], [two_mine], [two_theirs]]

    facts = jnp.stack([doc_ids, positions])
    facts_there = send(after(facts, two_theirs), "inner", across_inner)
    inverse = jnp.asarray([yarn_inverse(HEAD_SIZE) * 2], dtype=jnp.float32)
    signs = jnp.asarray([-1.0] * (HEAD_SIZE // 2) + [1.0] * (HEAD_SIZE // 2), dtype=jnp.float32)
    attention_gain = 0.1 * math.log(yarn_factor) + 1.0
    angles, documents, document_rows = call_kernel(
        functools.partial(facts_kernel, rows), "facts", places, [facts, facts_there, inverse],
        [None] * 3,
        [
            ((4 * slot_rows, HEAD_SIZE), jnp.float32, None),
            ((4 * slot_rows, 1), jnp.float32, None),
            ((16, 2 * HEAD_SIZE), bf16, None),
        ],
    )
    cosines = jnp.cos(angles) * attention_gain
    sines = jnp.sin(angles) * attention_gain * signs

    def stack(name, chunks, parts):
        flat = [array for chunk in chunks for array in chunk]
        out = lambda count: ((count * slot_rows, half_width), bf16, None)
        return call_kernel(
            functools.partial(stack_kernel, [len(chunk) for chunk in chunks]), name, which, flat,
            [None] * len(flat), [out(count) for count in parts],
        )

    def sent_halves(wholes, kind):
        count = wholes[0].shape[0]
        wides = [whole.shape[1] // 2 for whole in wholes]
        specs = [
            pl.BlockSpec((count, wide), lambda step, which: (0, 1 - which[1])) for wide in wides
        ]
        return call_kernel(
            copy_kernel, "sent", places, wholes, specs, [((count, sum(wides)), kind, None)]
        )[0]

    def project_pair(stacked):
        keys, values = product(stacked, w_key), product(stacked, value_weight)
        return keys, values, send(sent_halves([keys, values], jnp.float32), "inner", across_inner)

    def project_query(stacked):
        queries = product(stacked, w_query)
        return queries, send(sent_halves([queries], bf16), "inner", across_inner)

    def gather_pairs(pair):
        found = [pair]
        for flip in range(1, outer_count):
            found.append(send(pair, "outer", swap_pairs(outer_count, flip)))
        return found

    def gather_by_steps(pair):
        found = {0: pair}
        bit = outer_count // 2
        while bit:
            for flip in list(found):
                found[flip | bit] = send(found[flip], "outer", swap_pairs(outer_count, bit))
            bit //= 2
        return [found[flip] for flip in range(outer_count)]

    def rotate_pair(projected, first, extra):
        keys, values, came = projected
        count = came.shape[0]
        half_spec = pl.BlockSpec((count, HEAD_SIZE), lambda step, which: (0, which[0]))
        table_spec = pl.BlockSpec((count, HEAD_SIZE), lambda step, which: (first // count, 0))
        out_rows = count + sum(array.shape[0] for array in extra)
        return call_kernel(
            functools.partial(pair_kernel, rows), "pair", which,
            [keys, values, came, cosines, sines] + extra,
            [half_spec, half_spec, None, table_spec, table_spec] + [None] * len(extra),
            [((out_rows, 2 * HEAD_SIZE), bf16, None)],
        )[0]

    early_stacked, unused_rows, two_rows = stack("early_rows", early, (3, 1, 1))
    own_rows = stack("own_rows", [[after(mine, one_mine)], [theirs]], (1,))[0]
    middle_rows = send(own_rows, "tensor", middle)
    ends_rows = send(two_rows, "tensor", [(1, 0), (2, 3)])
    early_projected = project_pair(early_stacked)
    early_queries, early_came = project_query(early_stacked)
    late_stacked = stack("late_rows", [[middle_rows, ends_rows]], (1,))[0]
    late_projected = project_pair(late_stacked)
    late_queries, late_came = project_query(late_stacked)
    early_pairs = gather_by_steps(rotate_pair(early_projected, 0, [document_rows]))
    late_pairs = gather_pairs(rotate_pair(late_projected, early_rows, []))

    def attend(slot, *wait):
        queries, came = (late_queries, late_came) if slot == 3 else (early_queries, early_came)
        block = slot % 3
        if wait:
            came = after(came, *wait)
        rows_spec = lambda wide, block: pl.BlockSpec((slot_rows, wide), lambda step, which: (block, 0))
        half_spec = pl.BlockSpec((slot_rows, query_half), lambda step, which: (block, which[1]))
        stacked = query_half // HEAD_SIZE * slot_rows
        return call_kernel(
            functools.partial(attention_kernel, slot, outer_count, rows), "attention", places,
            [queries, came, cosines, sines, documents] + early_pairs + late_pairs,
            [
                half_spec, rows_spec(query_half, block),
                rows_spec(HEAD_SIZE, slot), rows_spec(HEAD_SIZE, slot), rows_spec(1, slot),
            ] + [None] * (2 * outer_count),
            [((rows, query_half), bf16, None)] * 2,
            scratch=[
                pltpu.VMEM((stacked, 1), jnp.float32),
                pltpu.VMEM((stacked, 1), jnp.float32),
                pltpu.VMEM((stacked, HEAD_SIZE), jnp.float32),
            ],
        )

    def joined(slot, *wait):
        here, gone = attend(slot, *wait)
        came = send(gone, "inner", across_inner)
        return call_kernel(
            join_kernel, "join", places, [here, came], [None] * 2,
            [((rows, 2 * query_half), bf16, None)],
        )[0]

    rows_3 = joined(3)
    rows_2 = joined(2)
    term_3 = product(rows_3, w_out).astype(bf16)
    came_3 = send(term_3, "tensor", swap_pairs(4, 3))
    term_2 = product(rows_2, w_out).astype(bf16)
    came_2 = send(term_2, "tensor", two)
    rows_1 = joined(1, term_3)
    came_1 = send(product(rows_1, w_out).astype(bf16), "tensor", one)
    rows_0 = joined(0, term_2)
    total = lax.optimization_barrier(product(rows_0, w_out))
    total = total + hidden_in.astype(jnp.float32) + came_1.astype(jnp.float32)
    total = total + came_2.astype(jnp.float32) + came_3.astype(jnp.float32)
    return total.astype(bf16)


def solution(mesh):
    in_specs = (
        P(("outer", "inner", "tensor"), None),
        P(),
        P("inner", "tensor"),
        P("inner", "tensor"),
        P("inner", "tensor"),
        P("tensor", None),
        P(("outer", "inner")),
        P(("outer", "inner")),
    )
    out_specs = P(("outer", "inner", "tensor"), None)

    def chosen(*arrays):
        outer_count = mesh.shape["outer"]
        key_heads = arrays[3].shape[1] // HEAD_SIZE // mesh.shape["tensor"]
        short = (
            mesh.shape["tensor"] == 4
            and mesh.shape["inner"] == 2
            and key_heads == 2
            and outer_count & (outer_count - 1) == 0
            and arrays[0].shape[0] % (mesh.size * 16) == 0
            and arrays[0].shape[0] // outer_count <= 512
        )
        mapped = jax.shard_map(
            short_body if short else body,
            mesh=mesh, in_specs=in_specs, out_specs=out_specs, check_vma=False,
        )
        return mapped(*arrays)

    return chosen
```

```python
import functools
import math

import jax
import jax.numpy as jnp
from jax import lax
from jax.experimental import pallas as pl
from jax.experimental.pallas import tpu as pltpu
from jax.sharding import PartitionSpec as P

HEAD_SIZE = 128


rope_base = 500000.0
yarn_factor = 8.0
trained_context = 8192.0
beta_fast = 32.0
beta_slow = 1.0
norm_epsilon = 1e-05
masked_score = -1e30


def yarn_inverse(head_dim):
    half_dim = head_dim // 2

    def correction(rotations):
        return (
            head_dim
            * math.log(trained_context / (rotations * 2.0 * math.pi))
            / (2.0 * math.log(rope_base))
        )

    lowest = max(math.floor(correction(beta_fast)), 0)
    highest = min(math.ceil(correction(beta_slow)), head_dim - 1)
    spread = max(highest - lowest, 0.001)
    values = []
    for column in range(half_dim):
        extrapolated = rope_base ** (-2.0 * column / head_dim)
        ramp = min(max((column - lowest) / spread, 0.0), 1.0)
        values.append(extrapolated / yarn_factor * ramp + extrapolated * (1.0 - ramp))
    return values


def yarn_tables(positions, head_dim):
    inverse = jnp.asarray(yarn_inverse(head_dim), dtype=jnp.float32)
    attention_gain = 0.1 * math.log(yarn_factor) + 1.0
    angles = positions.astype(jnp.float32)[:, None] * inverse[None, :]
    return (jnp.cos(angles) * attention_gain, jnp.sin(angles) * attention_gain)


def apply_rotation(heads, cosine_table, sine_table):
    half_dim = heads.shape[-1] // 2
    first_half = heads[..., :half_dim]
    second_half = heads[..., half_dim:]
    cos_rows = cosine_table[:, None, :]
    sin_rows = sine_table[:, None, :]
    return jnp.concatenate(
        [
            first_half * cos_rows - second_half * sin_rows,
            second_half * cos_rows + first_half * sin_rows,
        ],
        axis=-1,
    )


def rms_normed(hidden_in, norm_gain):
    widened = hidden_in.astype(jnp.float32)
    power = jnp.mean(widened * widened, axis=-1, keepdims=True)
    return (widened * lax.rsqrt(power + norm_epsilon) * norm_gain).astype(jnp.bfloat16)


def body(hidden_in, norm_gain, w_query, w_key, value_weight, w_out, doc_ids, positions):
    normed = rms_normed(hidden_in, norm_gain)
    block_rows = lax.all_gather(normed, "tensor", axis=0, tiled=True)
    tokens_here = block_rows.shape[0]
    query_width = w_query.shape[1]
    key_width = w_key.shape[1]
    inner_count = lax.axis_size("inner")
    slice_width = w_query.shape[0]
    arranged = block_rows.reshape(tokens_here, inner_count, slice_width)
    received = lax.all_to_all(arranged, "inner", split_axis=1, concat_axis=0, tiled=True)
    received = received.reshape(inner_count * tokens_here, slice_width)
    stacked = jnp.concatenate([w_query, w_key, value_weight], axis=1)
    combined = lax.psum_scatter(
        jnp.dot(received, stacked, preferred_element_type=jnp.float32),
        "inner",
        scatter_dimension=0,
        tiled=True,
    )
    queries = combined[:, :query_width]
    key_matrix = combined[:, query_width : query_width + key_width]
    value_matrix = combined[:, query_width + key_width :]
    value_matrix = value_matrix.astype(jnp.bfloat16)
    heads_query = query_width // HEAD_SIZE
    heads_key = key_width // HEAD_SIZE
    queries_per_group = heads_query // heads_key
    cosine_table, sine_table = yarn_tables(positions, HEAD_SIZE)
    query_rot = (
        apply_rotation(
            queries.reshape(tokens_here, heads_query, HEAD_SIZE), cosine_table, sine_table
        )
        .astype(jnp.bfloat16)
        .reshape(tokens_here, query_width)
    )
    rotated_keys = (
        apply_rotation(
            key_matrix.reshape(tokens_here, heads_key, HEAD_SIZE), cosine_table, sine_table
        )
        .astype(jnp.bfloat16)
        .reshape(tokens_here, key_width)
    )
    documents = lax.all_gather(doc_ids, ("outer", "inner"), axis=0, tiled=True)
    length_all = documents.shape[0]
    block_index = lax.axis_index(("outer", "inner"))
    sequence_index = jnp.arange(length_all, dtype=jnp.int32)
    query_documents = lax.dynamic_slice_in_dim(documents, block_index * tokens_here, tokens_here, 0)
    query_index = lax.dynamic_slice_in_dim(
        sequence_index, block_index * tokens_here, tokens_here, 0
    )
    row_documents = jnp.tile(query_documents, queries_per_group)
    row_index = jnp.tile(query_index, queries_per_group)
    top_index = jnp.max(query_index)
    top_document = jnp.max(query_documents)
    low_document = jnp.min(query_documents)
    grouped_heads = jnp.transpose(
        query_rot.reshape(tokens_here, heads_key, queries_per_group, HEAD_SIZE), (1, 2, 0, 3)
    ).reshape(heads_key, queries_per_group * tokens_here, HEAD_SIZE)
    score_scale = HEAD_SIZE ** (-0.5)

    def key_block(running, block_keys, block_values, first_row):
        row_count = block_keys.shape[0]
        piece_index = lax.dynamic_slice_in_dim(sequence_index, first_row, row_count, 0)
        piece_documents = lax.dynamic_slice_in_dim(documents, first_row, row_count, 0)
        live = (
            (jnp.min(piece_index) <= top_index)
            & (jnp.min(piece_documents) <= top_document)
            & (jnp.max(piece_documents) >= low_document)
        )

        def attend(current):
            row_peaks, totals, summed = current
            heads_keys = block_keys.reshape(row_count, heads_key, HEAD_SIZE)
            heads_values = block_values.reshape(row_count, heads_key, HEAD_SIZE)
            scores = (
                jnp.einsum(
                    "hqd,khd->hqk", grouped_heads, heads_keys, preferred_element_type=jnp.float32
                )
                * score_scale
            )
            allowed = (row_index[:, None] >= piece_index[None, :]) & (
                row_documents[:, None] == piece_documents[None, :]
            )
            scores = jnp.where(allowed[None], scores, masked_score)
            fresh = jnp.maximum(row_peaks, jnp.max(scores, axis=-1))
            weights = jnp.where(allowed[None], jnp.exp(scores - fresh[..., None]), 0.0)
            shrink = jnp.exp(row_peaks - fresh)
            totals = totals * shrink + jnp.sum(weights, axis=-1)
            summed = summed * shrink[..., None] + jnp.einsum(
                "hqk,khd->hqd",
                weights.astype(jnp.bfloat16),
                heads_values,
                preferred_element_type=jnp.float32,
            )
            return (fresh, totals, summed)

        return lax.cond(live, attend, lambda current: current, running)

    initial = (
        jnp.full((heads_key, queries_per_group * tokens_here), masked_score, jnp.float32),
        jnp.zeros((heads_key, queries_per_group * tokens_here), jnp.float32),
        jnp.zeros((heads_key, queries_per_group * tokens_here, HEAD_SIZE), jnp.float32),
    )
    piece_keys = lax.all_gather(rotated_keys, ("outer", "inner"), axis=0, tiled=True)
    piece_values = lax.all_gather(value_matrix, ("outer", "inner"), axis=0, tiled=True)
    row_count = piece_keys.shape[0]
    step_rows = 512
    steps_count = row_count // step_rows
    split_keys = piece_keys.reshape(steps_count, step_rows, key_width)
    split_values = piece_values.reshape(steps_count, step_rows, key_width)
    offsets = jnp.arange(steps_count, dtype=jnp.int32) * step_rows

    def scan_step(current, inputs):
        block_keys, block_values, offset = inputs
        return (key_block(current, block_keys, block_values, offset), None)

    result, unused = lax.scan(scan_step, initial, (split_keys, split_values, offsets))
    row_peaks, totals, summed = result
    heads_out = (summed / totals[..., None]).astype(jnp.bfloat16)
    attended = jnp.transpose(
        heads_out.reshape(heads_key, queries_per_group, tokens_here, HEAD_SIZE), (2, 0, 1, 3)
    ).reshape(tokens_here, query_width)
    full_term = jnp.dot(attended, w_out, preferred_element_type=jnp.float32)
    projected = lax.psum_scatter(
        full_term.astype(jnp.bfloat16), "tensor", scatter_dimension=0, tiled=True
    ).astype(jnp.float32)
    return (hidden_in.astype(jnp.float32) + projected).astype(jnp.bfloat16)


def swap_pairs(axis_size, flip):
    return [(place, place ^ flip) for place in range(axis_size)]


def after(value, *others):
    return lax.optimization_barrier((value,) + others)[0]


def whole_spec(array):
    zeros = (0,) * array.ndim
    return pl.BlockSpec(array.shape, lambda step, which: zeros)


def call_kernel(kernel, name, which, arrays, specs, outs, steps=1, scratch=(), mebibytes=16):
    shapes = [jax.ShapeDtypeStruct(shape, dtype) for shape, dtype, unused in outs]
    out_specs = [
        whole_spec(shape) if spec is None else spec for shape, (a, b, spec) in zip(shapes, outs)
    ]
    found = pl.pallas_call(
        kernel,
        name=name,
        grid_spec=pltpu.PrefetchScalarGridSpec(
            num_scalar_prefetch=1,
            grid=(steps,),
            in_specs=[
                whole_spec(array) if spec is None else spec for array, spec in zip(arrays, specs)
            ],
            out_specs=out_specs,
            scratch_shapes=list(scratch),
        ),
        out_shape=shapes,
        compiler_params=pltpu.CompilerParams(vmem_limit_bytes=mebibytes * 1024 * 1024),
    )(which, *arrays)
    return found


def norm_kernel(which, hidden, gain, mine, others):
    half_width = mine.shape[1]
    widened = hidden[...].astype(jnp.float32)
    power = jnp.mean(widened * widened, axis=-1, keepdims=True)
    normed = (widened * lax.rsqrt(power + norm_epsilon) * gain[...]).astype(jnp.bfloat16)

    @pl.when(which[0] == 0)
    def _():
        mine[...] = normed[:, :half_width]
        others[...] = normed[:, half_width:]

    @pl.when(which[0] != 0)
    def _():
        mine[...] = normed[:, half_width:]
        others[...] = normed[:, :half_width]


def stacked_rows(chunks):
    return jnp.concatenate(
        [
            chunk[...] if len(pair) == 1 else pair[0][...] + pair[1][...]
            for pair in chunks
            for chunk in pair[:1]
        ],
        axis=0,
    )


def split_chunks(refs, widths):
    chunks = []
    place = 0
    for width in widths:
        chunks.append(refs[place : place + width])
        place += width
    return chunks, refs[place:]


def product(left, right):
    return jnp.dot(left, right, preferred_element_type=jnp.float32)


def stack_kernel(widths, which, *refs):
    chunks, outs = split_chunks(refs, widths)
    outs[0][...] = stacked_rows(chunks)
    for place, out in zip((0, outs[0].shape[0] * 2 // 3), outs[1:]):
        out[...] = outs[0][place : place + out.shape[0]]


def other_part(value, rows):
    pieces = [value[place : place + rows] for place in range(0, value.shape[0], rows)]
    return jnp.concatenate([pieces[k ^ 1] for k in range(len(pieces))], axis=0)


def rotated(part, cosine_rows, sine_rows):
    return part * cosine_rows + pltpu.roll(part, HEAD_SIZE // 2, 1) * sine_rows


def pair_kernel(rows, which, keys, values, came, cosines, sines, *refs):
    out = refs[-1]
    count = keys.shape[0]
    added = other_part(came[...], rows).astype(jnp.float32)
    whole = rotated(keys[...] + added[:, :HEAD_SIZE], cosines[...], sines[...])
    out[:count, :HEAD_SIZE] = whole.astype(jnp.bfloat16)
    out[:count, HEAD_SIZE:] = (values[...] + added[:, HEAD_SIZE:]).astype(jnp.bfloat16)
    if len(refs) == 2:
        out[count:, :] = refs[0][...]


def facts_kernel(rows, which, here, there, inverse, angles, documents, document_rows):
    block = here.shape[1]
    line = lax.broadcasted_iota(jnp.int32, (block, 1), 0)
    slots = sum((line >= rows * number).astype(jnp.int32) for number in range(1, 4))
    source = (which[2] ^ slots) * rows + line - rows * slots
    chosen = lax.broadcasted_iota(jnp.int32, (block, block), 1) == source

    def ordered(row):
        parts = [
            jnp.sum(jnp.where(chosen, part[row : row + 1, :].astype(jnp.float32), 0.0), axis=1, keepdims=True)
            for part in (here, there)
        ]
        return jnp.concatenate(
            [part[place : place + rows] for place in range(0, block, rows) for part in parts], axis=0
        )

    angles[...] = ordered(1) * inverse[...]
    column = ordered(0)
    documents[...] = column
    count = column.shape[0]
    same = lax.broadcasted_iota(jnp.int32, (count, count), 0) == lax.broadcasted_iota(
        jnp.int32, (count, count), 1
    )
    wide = document_rows.shape[1]
    across = jnp.sum(jnp.where(same, column, 0.0), axis=0, keepdims=True)
    rest = jnp.concatenate(
        [across[:, wide:], jnp.zeros((1, 2 * wide - count), jnp.float32)], axis=1
    )
    number = lax.broadcasted_iota(jnp.int32, document_rows.shape, 0)
    document_rows[...] = jnp.where(
        number == 0, across[:, :wide], jnp.where(number == 1, rest, 0.0)
    ).astype(jnp.bfloat16)


def copy_kernel(which, *refs):
    *parts, out = refs
    place = 0
    for part in parts:
        out[:, place : place + part.shape[1]] = part[...].astype(out.dtype)
        place += part.shape[1]


def join_kernel(which, here, came, out):
    width = here.shape[1]

    @pl.when(which[1] == 0)
    def _():
        out[:, :width] = here[...]
        out[:, width:] = came[...]

    @pl.when(which[1] != 0)
    def _():
        out[:, :width] = came[...]
        out[:, width:] = here[...]


def attention_kernel(
    slot, blocks, rows, which, kept, came, cosines, sines, query_document, *refs
):
    early, late = refs[:blocks], refs[blocks : 2 * blocks]
    here, gone, peaks, totals, summed = refs[2 * blocks :]
    tokens, width = came.shape
    heads = width // HEAD_SIZE
    score_scale = HEAD_SIZE ** (-0.5) / math.log(2.0)
    block_rows = 4 * rows
    early_rows = 2 * block_rows - late[0].shape[0]
    whole = kept[...] + other_part(came[...], rows).astype(jnp.float32)
    stacked = jnp.concatenate(
        [
            rotated(whole[:, place : place + HEAD_SIZE], cosines[...], sines[...]).astype(
                jnp.bfloat16
            )
            for place in range(0, width, HEAD_SIZE)
        ],
        axis=0,
    )
    place_outer, place_inner, place_tensor = which[0], which[1], which[2]
    document = query_document[...]

    def inside(slot_number, part_number, row_number):
        return (place_inner ^ part_number) * block_rows + (place_tensor ^ slot_number) * rows + row_number

    line = lax.broadcasted_iota(jnp.int32, (tokens, 1), 0)
    second = (line >= rows).astype(jnp.int32)
    row_place = inside(slot, second, line - rows * second)
    line = lax.broadcasted_iota(jnp.int32, (1, 2 * block_rows), 1)
    slots = sum((line >= 2 * rows * number).astype(jnp.int32) for number in range(1, 4))
    left = line - 2 * rows * slots
    second = (left >= rows).astype(jnp.int32)
    key_place = inside(slots, second, left - rows * second)

    def joined(block, start):
        stop = start + HEAD_SIZE
        return jnp.concatenate([early[block][:early_rows, start:stop], late[block][:, start:stop]], axis=0)

    def key_document(block):
        lines = early[block][early_rows:, :].astype(jnp.float32)
        rest = 2 * block_rows - lines.shape[1]
        return jnp.concatenate([lines[0:1, :], lines[1:2, :rest]], axis=1)

    def block_scores(block):
        allowed = key_document(block) == document
        if block == 0:
            allowed = allowed & (key_place <= row_place)
        barred = jnp.where(allowed, 0.0, masked_score)
        scores = lax.dot_general(
            stacked, joined(block, 0), (((1,), (1,)), ((), ())), preferred_element_type=jnp.float32
        )
        scores = scores.reshape(heads, tokens, -1) * score_scale + barred[None]
        return scores.reshape(heads * tokens, -1)

    def weighted(block, weights):
        return product(weights.astype(jnp.bfloat16), joined(block, HEAD_SIZE))

    scores = block_scores(0)
    peak = jnp.max(scores, axis=-1, keepdims=True)
    weights = jnp.exp2(scores - peak)
    peaks[...] = peak
    totals[...] = jnp.sum(weights, axis=-1, keepdims=True)
    summed[...] = weighted(0, weights)
    lowest = jnp.min(document)
    for block in range(1, blocks):

        @pl.when(((place_outer ^ block) < place_outer) & (jnp.max(key_document(block)) >= lowest))
        def _():
            scores = block_scores(block)
            before = peaks[...]
            peak = jnp.maximum(before, jnp.max(scores, axis=-1, keepdims=True))
            weights = jnp.exp2(scores - peak)
            shrink = jnp.exp2(before - peak)
            peaks[...] = peak
            totals[...] = totals[...] * shrink + jnp.sum(weights, axis=-1, keepdims=True)
            summed[...] = summed[...] * shrink + weighted(block, weights)

    result = (summed[...] / totals[...]).astype(jnp.bfloat16)
    for head in range(heads):
        first = head * tokens
        columns = slice(head * HEAD_SIZE, (head + 1) * HEAD_SIZE)
        here[:, columns] = result[first : first + rows]
        gone[:, columns] = result[first + rows : first + tokens]


def short_body(hidden_in, norm_gain, w_query, w_key, value_weight, w_out, doc_ids, positions):
    place_outer = lax.axis_index("outer")
    place_inner = lax.axis_index("inner")
    place_tensor = lax.axis_index("tensor")
    outer_count = lax.axis_size("outer")
    rows, width = hidden_in.shape
    half_width = w_query.shape[0]
    query_half = w_query.shape[1] // 2
    slot_rows = 2 * rows
    early_rows = 3 * slot_rows
    bf16 = jnp.bfloat16
    across_inner = swap_pairs(2, 1)
    which = place_inner.reshape(1)
    places = jnp.stack([place_outer, place_inner, place_tensor])
    hidden_in, which, places = lax.optimization_barrier((hidden_in, which, places))

    def send(value, axis, pairs):
        return lax.ppermute(value, axis, pairs)

    def send_across(value, pairs):
        both = [(a * 4 + b, (1 - a) * 4 + c) for a in range(2) for b, c in pairs]
        return lax.ppermute(value, ("inner", "tensor"), both)

    half = ((rows, half_width), bf16, None)
    mine, others = call_kernel(
        norm_kernel, "norm", which, [hidden_in, norm_gain.reshape(1, width)], [None] * 2, [half] * 2
    )
    two, one, middle = swap_pairs(4, 2), swap_pairs(4, 1), [(1, 2), (2, 1)]
    two_mine = send(mine, "tensor", two)
    two_theirs = send_across(others, two)
    one_mine = send(mine, "tensor", one)
    one_theirs = send_across(others, one)
    theirs = send(others, "inner", across_inner)
    early = [[mine], [theirs], [one_mine], [one_theirs], [two_mine], [two_theirs]]

    facts = jnp.stack([doc_ids, positions])
    facts_there = send(after(facts, two_theirs), "inner", across_inner)
    inverse = jnp.asarray([yarn_inverse(HEAD_SIZE) * 2], dtype=jnp.float32)
    signs = jnp.asarray([-1.0] * (HEAD_SIZE // 2) + [1.0] * (HEAD_SIZE // 2), dtype=jnp.float32)
    attention_gain = 0.1 * math.log(yarn_factor) + 1.0
    angles, documents, document_rows = call_kernel(
        functools.partial(facts_kernel, rows), "facts", places, [facts, facts_there, inverse],
        [None] * 3,
        [
            ((4 * slot_rows, HEAD_SIZE), jnp.float32, None),
            ((4 * slot_rows, 1), jnp.float32, None),
            ((16, 2 * HEAD_SIZE), bf16, None),
        ],
    )
    cosines = jnp.cos(angles) * attention_gain
    sines = jnp.sin(angles) * attention_gain * signs

    def stack(name, chunks, parts):
        flat = [array for chunk in chunks for array in chunk]
        out = lambda count: ((count * slot_rows, half_width), bf16, None)
        return call_kernel(
            functools.partial(stack_kernel, [len(chunk) for chunk in chunks]), name, which, flat,
            [None] * len(flat), [out(count) for count in parts],
        )

    def sent_halves(wholes, kind):
        count = wholes[0].shape[0]
        wides = [whole.shape[1] // 2 for whole in wholes]
        specs = [
            pl.BlockSpec((count, wide), lambda step, which: (0, 1 - which[1])) for wide in wides
        ]
        return call_kernel(
            copy_kernel, "sent", places, wholes, specs, [((count, sum(wides)), kind, None)]
        )[0]

    def project_pair(stacked):
        keys, values = product(stacked, w_key), product(stacked, value_weight)
        return keys, values, send(sent_halves([keys, values], jnp.float32), "inner", across_inner)

    def project_query(stacked):
        queries = product(stacked, w_query)
        return queries, send(sent_halves([queries], bf16), "inner", across_inner)

    def gather_pairs(pair):
        found = [pair]
        for flip in range(1, outer_count):
            found.append(send(pair, "outer", swap_pairs(outer_count, flip)))
        return found

    def gather_by_steps(pair):
        found = {0: pair}
        bit = outer_count // 2
        while bit:
            for flip in list(found):
                found[flip | bit] = send(found[flip], "outer", swap_pairs(outer_count, bit))
            bit //= 2
        return [found[flip] for flip in range(outer_count)]

    def rotate_pair(projected, first, extra):
        keys, values, came = projected
        count = came.shape[0]
        half_spec = pl.BlockSpec((count, HEAD_SIZE), lambda step, which: (0, which[0]))
        table_spec = pl.BlockSpec((count, HEAD_SIZE), lambda step, which: (first // count, 0))
        out_rows = count + sum(array.shape[0] for array in extra)
        return call_kernel(
            functools.partial(pair_kernel, rows), "pair", which,
            [keys, values, came, cosines, sines] + extra,
            [half_spec, half_spec, None, table_spec, table_spec] + [None] * len(extra),
            [((out_rows, 2 * HEAD_SIZE), bf16, None)],
        )[0]

    early_stacked, unused_rows, two_rows = stack("early_rows", early, (3, 1, 1))
    own_rows = stack("own_rows", [[after(mine, one_mine)], [theirs]], (1,))[0]
    middle_rows = send(own_rows, "tensor", middle)
    ends_rows = send(two_rows, "tensor", [(1, 0), (2, 3)])
    early_projected = project_pair(early_stacked)
    early_queries, early_came = project_query(early_stacked)
    late_stacked = stack("late_rows", [[ends_rows, middle_rows]], (1,))[0]
    late_projected = project_pair(late_stacked)
    late_queries, late_came = project_query(late_stacked)
    early_pairs = gather_by_steps(rotate_pair(early_projected, 0, [document_rows]))
    late_pairs = gather_pairs(rotate_pair(late_projected, early_rows, []))

    def attend(slot, *wait):
        queries, came = (late_queries, late_came) if slot == 3 else (early_queries, early_came)
        block = slot % 3
        if wait:
            came = after(came, *wait)
        rows_spec = lambda wide, block: pl.BlockSpec((slot_rows, wide), lambda step, which: (block, 0))
        half_spec = pl.BlockSpec((slot_rows, query_half), lambda step, which: (block, which[1]))
        stacked = query_half // HEAD_SIZE * slot_rows
        return call_kernel(
            functools.partial(attention_kernel, slot, outer_count, rows), "attention", places,
            [queries, came, cosines, sines, documents] + early_pairs + late_pairs,
            [
                half_spec, rows_spec(query_half, block),
                rows_spec(HEAD_SIZE, slot), rows_spec(HEAD_SIZE, slot), rows_spec(1, slot),
            ] + [None] * (2 * outer_count),
            [((rows, query_half), bf16, None)] * 2,
            scratch=[
                pltpu.VMEM((stacked, 1), jnp.float32),
                pltpu.VMEM((stacked, 1), jnp.float32),
                pltpu.VMEM((stacked, HEAD_SIZE), jnp.float32),
            ],
        )

    def joined(slot, *wait):
        here, gone = attend(slot, *wait)
        came = send(gone, "inner", across_inner)
        return call_kernel(
            join_kernel, "join", places, [here, came], [None] * 2,
            [((rows, 2 * query_half), bf16, None)],
        )[0]

    rows_3 = joined(3)
    rows_2 = joined(2)
    term_3 = product(rows_3, w_out).astype(bf16)
    came_3 = send(term_3, "tensor", swap_pairs(4, 3))
    term_2 = product(rows_2, w_out).astype(bf16)
    came_2 = send(term_2, "tensor", two)
    rows_1 = joined(1, term_3)
    came_1 = send(product(rows_1, w_out).astype(bf16), "tensor", one)
    rows_0 = joined(0, term_3)
    total = lax.optimization_barrier(product(rows_0, w_out))
    total = total + hidden_in.astype(jnp.float32) + came_1.astype(jnp.float32)
    total = total + came_2.astype(jnp.float32) + came_3.astype(jnp.float32)
    return total.astype(bf16)


def solution(mesh):
    in_specs = (
        P(("outer", "inner", "tensor"), None),
        P(),
        P("inner", "tensor"),
        P("inner", "tensor"),
        P("inner", "tensor"),
        P("tensor", None),
        P(("outer", "inner")),
        P(("outer", "inner")),
    )
    out_specs = P(("outer", "inner", "tensor"), None)

    def chosen(*arrays):
        outer_count = mesh.shape["outer"]
        key_heads = arrays[3].shape[1] // HEAD_SIZE // mesh.shape["tensor"]
        short = (
            mesh.shape["tensor"] == 4
            and mesh.shape["inner"] == 2
            and key_heads == 2
            and outer_count & (outer_count - 1) == 0
            and arrays[0].shape[0] % (mesh.size * 16) == 0
            and arrays[0].shape[0] // outer_count <= 512
        )
        mapped = jax.shard_map(
            short_body if short else body,
            mesh=mesh, in_specs=in_specs, out_specs=out_specs, check_vma=False,
        )
        return mapped(*arrays)

    return chosen
```
